512 devices in a mesh: seq: 128 (over y, x, z_hi), ch: 4 (over z_lo, core).
Axes of the slice: x: 4, y: 8, z: 8 (z_hi: 4, z_lo: 2; z = z_hi * 2 + z_lo), core: 2. Of those that a mesh axis runs over, the one named last changes fastest.
Arguments:
- dna_features: bfloat16 [2, 8192, 1280], P(None, 'seq'), may hold values from -6 to 6
- gain_a: float32 [1280], replicated, may hold values from 0.25 to 1.75
- conv_a: bfloat16 [5, 1280, 1408], P(None, 'seq', 'ch'), may hold values from -0.078125 to 0.078125
- bias_a: float32 [1408], P('ch'), may hold values from -3 to 3
- gain_b: float32 [1408], replicated, may hold values from 0.25 to 1.75
- conv_b: bfloat16 [5, 1408, 1536], P(None, 'seq', 'ch'), may hold values from -0.0625 to 0.0625
- bias_b: float32 [1536], P('ch'), may hold values from -3 to 3
- grad_out: bfloat16 [2, 2048, 1536], P(None, 'seq', 'ch'), may hold values from -6 to 6
Outputs:
- pooled_out: bfloat16 [2, 2048, 1536], P(None, 'seq', 'ch')
- input_grad: bfloat16 [2, 8192, 1280], P(None, 'seq', 'ch')
The draws below stay inside these ranges and needn't reach their ends.
All inputs are finite; a program needn't handle non-finite values.
Results may differ from the reference program's by a relative error of at most 0.018.
Values may be sent and summed in bfloat16 or wider, within the bound.
A program may use at most 128 MiB of HBM per device.

```python
import math
import jax
import jax.numpy as jnp
from jax import lax

CH_IN = 1280
CH_MID = 1408
CH_OUT = 1536
TAPS = 5
WINDOWS = 2
LEN_IN = 8192
LEN_MID = 4096
LEN_OUT = 2048


def shard_levels(key, dims, pieces, least, top_value):
    def one(axis_at, blocks):
        draws = jax.random.uniform(jax.random.fold_in(jax.random.fold_in(key, 6), axis_at), (blocks,), jnp.float32, least / len(pieces), top_value / len(pieces))
        return jnp.repeat(jnp.exp(draws), dims[axis_at] // blocks).reshape((-1,) + (1,) * (len(dims) - axis_at - 1))

    factor_of = one(*pieces[0])
    for cut in pieces[1:]:
        factor_of = factor_of * one(*cut)
    return factor_of


def gaussian(key, extent, deviation, most, cuts=(), kind=jnp.bfloat16):
    array = jax.random.normal(key, extent, jnp.float32) * deviation
    if len(cuts) > 0:
        array = shard_levels(key, extent, cuts, -0.22, 0.18) * array
    return jnp.clip(array, min=-most, max=most).astype(kind)


def setup_inputs(seed: int = 0) -> dict:
    key_of = jax.random.split(jax.random.key(seed), 9)
    return {
        "dna_features": gaussian(key_of[0], (WINDOWS, LEN_IN, CH_IN), 1.0, 6.0, ((1, 128),)),
        "gain_a": jnp.clip(1.0 + 0.15 * jax.random.normal(key_of[1], (CH_IN,), jnp.float32), 0.25, 1.75),
        "conv_a": gaussian(key_of[2], (TAPS, CH_IN, CH_MID), (TAPS * CH_IN) ** -0.5, 0.078125, ((1, 128), (2, 4))),
        "bias_a": gaussian(key_of[3], (CH_MID,), 0.5, 3.0, ((0, 4),), jnp.float32),
        "gain_b": jnp.clip(1.0 + 0.15 * jax.random.normal(key_of[4], (CH_MID,), jnp.float32), 0.25, 1.75),
        "conv_b": gaussian(key_of[5], (TAPS, CH_MID, CH_OUT), (TAPS * CH_MID) ** -0.5, 0.0625, ((1, 128), (2, 4))),
        "bias_b": gaussian(key_of[6], (CH_OUT,), 0.5, 3.0, ((0, 4),), jnp.float32),
        "grad_out": gaussian(key_of[7], (WINDOWS, LEN_OUT, CH_OUT), 1.0, 6.0, ((1, 128), (2, 4))),
    }


EPS = 1e-06
ROOT = math.sqrt(2.0 / math.pi)

def gelu_tanh(z):
    return 0.5 * z * (1.0 + jnp.tanh(ROOT * (z + 0.044715 * z * z * z)))

def gelu_slope(z):
    t = jnp.tanh(ROOT * (z + 0.044715 * z * z * z))
    return 0.5 * (1.0 + t) + 0.5 * z * (1.0 - t * t) * ROOT * (1.0 + 3.0 * 0.044715 * z * z)

def pad_rows(v):
    return jnp.pad(v, ((0, 0), (2, 2), (0, 0)))

def pool_pairs(v):
    return v.reshape(v.shape[0], v.shape[1] // 2, 2, v.shape[2]).sum(axis=2) * 0.5

def repeat_half(v):
    return (jnp.repeat(v.astype(jnp.float32), 2, axis=1) * 0.5).astype(jnp.bfloat16)

def conv_rows(padded, weight, length):
    padded = padded.astype(jnp.float32)
    weight = weight.astype(jnp.float32)
    total = jnp.zeros((padded.shape[0], length, weight.shape[2]), jnp.float32)
    for offset in range(TAPS):
        total = total + jnp.einsum('wtc,co->wto', padded[:, offset:offset + length], weight[offset])
    return total

def conv_back(padded, weight, length):
    padded = padded.astype(jnp.float32)
    weight = weight.astype(jnp.float32)
    total = jnp.zeros((padded.shape[0], length, weight.shape[1]), jnp.float32)
    for offset in range(TAPS):
        start = 4 - offset
        total = total + jnp.einsum('wto,co->wtc', padded[:, start:start + length], weight[offset])
    return total

def norm_back(back, values, scale, gain):
    normed = values * scale
    grad_n = back * gelu_slope(normed * gain) * gain
    inner = lax.optimization_barrier(jnp.mean(grad_n * normed, axis=-1, keepdims=True))
    return scale * (grad_n - normed * inner)

def reference(dna_features, gain_a, conv_a, bias_a, gain_b, conv_b, bias_b, grad_out):
    feat = dna_features.astype(jnp.float32)
    scale_a = lax.rsqrt(lax.optimization_barrier(jnp.mean(feat * feat, axis=-1, keepdims=True)) + EPS)
    act_a = gelu_tanh(feat * scale_a * gain_a).astype(jnp.bfloat16)
    mid = pool_pairs(conv_rows(pad_rows(act_a), conv_a, LEN_IN) + bias_a).astype(jnp.bfloat16)
    mid_f = mid.astype(jnp.float32)
    scale_b = lax.rsqrt(lax.optimization_barrier(jnp.mean(mid_f * mid_f, axis=-1, keepdims=True)) + EPS)
    act_b = gelu_tanh(mid_f * scale_b * gain_b).astype(jnp.bfloat16)
    pooled_out = pool_pairs(conv_rows(pad_rows(act_b), conv_b, LEN_MID) + bias_b).astype(jnp.bfloat16)
    grad_b = repeat_half(grad_out)
    back_b = conv_back(pad_rows(grad_b), conv_b, LEN_MID)
    grad_mid = norm_back(back_b, mid_f, scale_b, gain_b).astype(jnp.bfloat16)
    grad_a = repeat_half(grad_mid)
    back_a = conv_back(pad_rows(grad_a), conv_a, LEN_IN)
    input_grad = norm_back(back_a, feat, scale_a, gain_a).astype(jnp.bfloat16)
    return (pooled_out, input_grad)
```

```python
import math

import jax
import jax.numpy as jnp
import numpy as np
from jax import lax
from jax.experimental import pallas as pl
from jax.experimental.pallas import tpu as pltpu
from jax.sharding import PartitionSpec as P

EPS = 1e-06
ROOT = math.sqrt(2.0 / math.pi)
MESH = pl.DeviceIdType.MESH
BF = jnp.bfloat16
F32 = jnp.float32
NY, NX, NZ, NC = 8, 4, 4, 4
CIN, CMID = 1280, 1408
EDGE = 16
WIDE = 2048
TAPS = 5 * 384


def gelu_tanh(z):
    return 0.5 * z * (1.0 + jnp.tanh(ROOT * (z + 0.044715 * z * z * z)))


def gelu_slope(z):
    t = jnp.tanh(ROOT * (z + 0.044715 * z * z * z))
    return 0.5 * (1.0 + t) + 0.5 * z * (1.0 - t * t) * ROOT * (1.0 + 3.0 * 0.044715 * z * z)


def index_tables():
    lanes = np.full((8, 1536), -100000, np.int32)
    rows = np.full((512, 8), -100000, np.int32)
    for zb in range(NZ):
        for xb in range(NX):
            for yb in range(NY):
                for i in range(10):
                    lanes[0, zb * 384 + xb * 80 + yb * 10 + i] = ((yb * 4 + xb) * 4 + zb) * 10 + i
            for yy in range(2):
                for i in range(11):
                    q = yy * 48 + xb * 11 + i
                    here = ((yy * 4 + xb) * 4 + zb) * 11 + i
                    lanes[1, zb * 128 + q] = here
                    rows[zb * 128 + q, 3] = here
                for i in range(10):
                    q = xb * 20 + yy * 10 + i
                    here = ((yy * 4 + xb) * 4 + zb) * 10 + i
                    lanes[3, zb * 128 + q] = here
                    rows[zb * 128 + q, 4] = here
    for cb in range(NC):
        for xb in range(NX):
            for yy in range(2):
                for i in range(11):
                    lanes[2, cb * 128 + yy * 48 + xb * 11 + i] = (((cb * 2 + yy) * 4 + xb) * 4) * 11 + i
                for i in range(10):
                    rows[cb * 128 + xb * 20 + yy * 10 + i, 0] = xb * 80 + (cb * 2 + yy) * 10 + i
    for k in range(5):
        for yb in range(NY):
            for i in range(10):
                rows[k * 80 + yb * 10 + i, 1] = yb * 64 + k * 10 + i
        for xb in range(NX):
            for i in range(11):
                rows[k * 48 + xb * 11 + i, 2] = xb * 64 + k * 11 + i
    return lanes, rows


def dot(a, b):
    return lax.dot_general(a, b, (((1,), (0,)), ((), ())), preferred_element_type=F32)


def dot_t(a, b):
    return lax.dot_general(a, b, (((1,), (1,)), ((), ())), preferred_element_type=F32)


def one_hot_lanes(table, depth):
    row = lax.broadcasted_iota(jnp.int32, (depth, table.shape[1]), 0)
    return jnp.where(row == table, 1.0, 0.0).astype(BF)


def one_hot_rows(table, depth):
    col = lax.broadcasted_iota(jnp.int32, (table.shape[0], depth), 1)
    return jnp.where(col == table, 1.0, 0.0).astype(BF)


def three_parts(v):
    high = v.astype(BF).astype(F32)
    rest = v - high
    middle = rest.astype(BF).astype(F32)
    return high, middle, rest - middle


def spread_gain(gain, hot):
    high, middle, low = three_parts(gain)
    row = lax.broadcasted_iota(jnp.int32, (16, gain.shape[1]), 0)
    stack = jnp.where(row == 0, high, jnp.where(row == 1, middle, jnp.where(row == 2, low, 0.0)))
    return jnp.sum(dot(stack.astype(BF), hot), axis=0, keepdims=True)


def kernel(
    feat_ref, wa_ref, wb_ref, gain_a_ref, bias_a_ref, gain_b_ref, bias_b_ref, g_ref, lanes_ref, rows_ref,
    pooled_ref, grad_ref,
    first_a, first_b, whole_a, turned_a, whole_b, bias_pad,
    act_slot, act_prev, act_next, act_rows, taps_a, send_act,
    g_slot, g_prev, g_next, g_rows,
    back_rows, back_send, back_recv,
    acc_a, mid_send, mid_recv,
    x_send, x_recv, b_slot, b_prev, b_next, b_rows,
    pool_send, pool_recv, acc_b,
    in_send, in_recv, gm_slot, gm_prev, gm_next, gm_rows,
    out_rows, out_send, out_recv, ia_send, ia_recv,
    s_fa, r_fa, s_fb, r_fb, s_wb, r_wb, s_wa, r_wa, s_col, r_col, s_edge, r_edge,
    s_b, r_b, s_x, r_x, s_o, r_o,
):
    seq = lax.axis_index("seq")
    ch = lax.axis_index("ch")
    zh = seq % NZ
    col = seq // NZ
    xi = col % NX
    yi = col // NX
    own = zh * NC + ch
    pending = []

    def start(src, dst, ssem, rsem, dev):
        copy = pltpu.make_async_remote_copy(
            src_ref=src, dst_ref=dst, send_sem=ssem, recv_sem=rsem, device_id=dev, device_id_type=MESH
        )
        copy.start()
        pending.append(copy)

    def arrived(dst, ssem, rsem):
        pltpu.make_async_remote_copy(
            src_ref=dst, dst_ref=dst, send_sem=ssem, recv_sem=rsem, device_id=(seq, ch), device_id_type=MESH
        ).wait_recv()

    def at_y(d):
        return ((((yi + d + NY) % NY) * NX + xi) * NZ + zh, ch)

    def at_x(d):
        return ((yi * NX + (xi + d + NX) % NX) * NZ + zh, ch)

    def at_z(d):
        return (col * NZ + (zh + d) % NZ, ch)

    def at_c(d):
        return (seq, (ch + d) % NC)

    def at_col(d):
        return (((col + d + 32) % 32) * NZ + zh, ch)

    def member(d):
        t = (own + d) % 16
        return t, (col * NZ + t // NC, t % NC)

    barrier = pltpu.get_barrier_semaphore()

    def greet(dev):
        pl.semaphore_signal(barrier, inc=1, device_id=dev, device_id_type=MESH)

    for d in (1, 2, 3):
        greet(at_x(d))
    for d in (-1, 1):
        greet(at_y(d))
        greet(at_col(d))

    @pl.loop(1, 16)
    def _(d):
        greet(member(d)[1])

    first_a[yi] = jnp.zeros((64, 384), BF)
    bias_pad[...] = jnp.zeros((8, 384), F32)
    bias_pad[0:1, 0:352] = bias_a_ref[...]
    pack_a = jnp.zeros((64, 352), F32)
    pack_b = jnp.zeros((64, 384), F32)
    for k in range(5):
        pick = lax.broadcasted_iota(jnp.int32, (64, 10), 0) == lax.broadcasted_iota(jnp.int32, (64, 10), 1) + 10 * k
        pack_a += dot(jnp.where(pick, 1.0, 0.0).astype(BF), wa_ref[k])
        pick = lax.broadcasted_iota(jnp.int32, (64, 11), 0) == lax.broadcasted_iota(jnp.int32, (64, 11), 1) + 11 * k
        pack_b += dot(jnp.where(pick, 1.0, 0.0).astype(BF), wb_ref[k])
    first_a[yi, :, 0:352] = pack_a.astype(BF)
    first_b[xi] = pack_b.astype(BF)
    whole_a[320:512, :] = jnp.zeros((192, WIDE), BF)
    whole_a[0:320, TAPS:WIDE] = jnp.zeros((320, WIDE - TAPS), BF)
    whole_b[:, TAPS:WIDE] = jnp.zeros((512, WIDE - TAPS), BF)
    for c in range(NC):
        whole_b[c * 128 + 96 : c * 128 + 128, 0:TAPS] = jnp.zeros((32, TAPS), BF)
    taps_a[:, :, 384:512] = jnp.zeros((5, 256, 128), BF)
    pl.semaphore_wait(barrier, 22)

    half = ((0, 32), (32, 32))

    def ring_fa(r, way):
        sign = 1 if way == 0 else -1
        at, n = (0, 64) if r < 3 else half[way]
        b = (yi - sign * r + NY) % NY
        ref = first_a.at[b, pl.ds(at, n), :]
        start(ref, ref, s_fa.at[way, r], r_fa.at[way, r], at_y(sign))

    def ring_fa_done(r, way):
        sign = 1 if way == 0 else -1
        at, n = (0, 64) if r < 3 else half[way]
        b = (yi - sign * (r + 1) + NY) % NY
        arrived(first_a.at[b, pl.ds(at, n), :], s_fa.at[way, r], r_fa.at[way, r])

    for way in (0, 1):
        ring_fa(0, way)
    for d in (1, 2, 3):
        start(first_b.at[xi], first_b.at[xi], s_fb.at[d], r_fb.at[d], at_x(d))

    g_slot[zh] = g_ref[...]
    for d in (1, 2, 3):
        start(g_ref, g_slot.at[zh], s_col.at[0, d], r_col.at[0, d], at_z(d))

    feat = feat_ref[...].astype(F32)
    inv_a = lax.rsqrt(jnp.sum(feat * feat, axis=-1, keepdims=True) * (1.0 / CIN) + EPS)
    act = gelu_tanh(feat * inv_a * gain_a_ref[...]).astype(BF)

    def slot_of(d):
        return (zh - d + NZ) % NZ

    for zb in range(NZ):
        hot = one_hot_lanes(lanes_ref[0:1, zb * 384 : (zb + 1) * 384], CIN)
        send_act[zb] = dot(act, hot).astype(BF)
    act_slot[zh] = send_act[zh]
    for d in (1, 2, 3):
        t = (zh + d) % NZ
        start(send_act.at[t], act_slot.at[zh], s_col.at[1, d], r_col.at[1, d], at_z(d))

    for d in (1, 2, 3):
        arrived(first_b.at[(xi - d + NX) % NX], s_fb.at[d], r_fb.at[d])
    hot_b = one_hot_rows(rows_ref[0:240, 2:3], 256)
    block = dot(hot_b, first_b[...].reshape(256, 384)).astype(BF)

    def place_b(b):
        return pl.multiple_of((b // 2) * 128 + (b % 2) * 48, 16)

    for k in range(5):
        whole_b[pl.ds(place_b(yi), 48), k * 384 : (k + 1) * 384] = block[k * 48 : (k + 1) * 48]
    taps_half = ((0, 1152), (1152, 768))

    def ring_wb(r, way):
        sign = 1 if way == 0 else -1
        at, n = (0, TAPS) if r < 3 else taps_half[way]
        ref = whole_b.at[pl.ds(place_b((yi - sign * r + NY) % NY), 48), pl.ds(at, n)]
        start(ref, ref, s_wb.at[way, r], r_wb.at[way, r], at_y(sign))

    def ring_wb_done(r, way):
        sign = 1 if way == 0 else -1
        at, n = (0, TAPS) if r < 3 else taps_half[way]
        ref = whole_b.at[pl.ds(place_b((yi - sign * (r + 1) + NY) % NY), 48), pl.ds(at, n)]
        arrived(ref, s_wb.at[way, r], r_wb.at[way, r])

    def ring_wa(r, way):
        sign = 1 if way == 0 else -1
        at, n = (0, TAPS) if r < 1 else taps_half[way]
        b = (xi - sign * r + NX) % NX
        ref = whole_a.at[pl.ds(pl.multiple_of(b * 80, 16), 80), pl.ds(at, n)]
        start(ref, ref, s_wa.at[way, r], r_wa.at[way, r], at_x(sign))

    def ring_wa_done(r, way):
        sign = 1 if way == 0 else -1
        at, n = (0, TAPS) if r < 1 else taps_half[way]
        b = (xi - sign * (r + 1) + NX) % NX
        ref = whole_a.at[pl.ds(pl.multiple_of(b * 80, 16), 80), pl.ds(at, n)]
        arrived(ref, s_wa.at[way, r], r_wa.at[way, r])

    for way in (0, 1):
        ring_wb(0, way)
    for r in range(3):
        for way in (0, 1):
            ring_fa_done(r, way)
            ring_fa(r + 1, way)
    for way in (0, 1):
        ring_fa_done(3, way)
    hot_a = one_hot_rows(rows_ref[0:400, 1:2], 512)
    block = dot(hot_a, first_a[...].reshape(512, 384)).astype(BF)
    for k in range(5):
        whole_a[pl.ds(pl.multiple_of(xi * 80, 16), 80), k * 384 : (k + 1) * 384] = block[k * 80 : (k + 1) * 80]
    for way in (0, 1):
        ring_wa(0, way)
    for way in (0, 1):
        ring_wb_done(0, way)
        ring_wb(1, way)

    def edges(slots, rows, prev, nxt, n):
        for w in range(2):
            lo = slots.at[0, pl.ds(w * rows, EDGE), :]
            hi = slots.at[3, pl.ds(w * rows + rows - EDGE, EDGE), :]
            start(hi, prev.at[w], s_edge.at[n, w], r_edge.at[n, w], at_col(1))
            start(lo, nxt.at[w], s_edge.at[n, 2 + w], r_edge.at[n, 2 + w], at_col(-1))

    def edges_done(prev, nxt, n):
        for w in range(2):
            arrived(prev.at[w], s_edge.at[n, w], r_edge.at[n, w])
            arrived(nxt.at[w], s_edge.at[n, 2 + w], r_edge.at[n, 2 + w])

    is_first = jnp.where(col == 0, 0.0, 1.0).astype(F32)
    is_last = jnp.where(col == 31, 0.0, 1.0).astype(F32)

    def lay(slots, rows, prev, nxt, where):
        tiles = where.shape[1]
        for w in range(2):
            for t in range(tiles):
                lanes = slice(t * 128, (t + 1) * 128)
                where[w, t, 0:EDGE, :] = prev[w, :, lanes].astype(F32) * is_first
                for z in range(NZ):
                    at = EDGE + z * rows
                    where[w, t, at : at + rows, :] = slots[z, w * rows : (w + 1) * rows, lanes].astype(F32)
                at = EDGE + NZ * rows
                where[w, t, at : at + EDGE, :] = nxt[w, :, lanes].astype(F32) * is_last

    def pooled_taps(where, rows):
        tiles = where.shape[1]
        parts = [[[where[w, t, pl.ds(EDGE + d, rows, stride=2), :] for t in range(tiles)] for w in range(2)]
                 for d in range(-2, 4)]
        out = []
        for k in range(5):
            wins = []
            for w in range(2):
                wins.append(jnp.concatenate(
                    [((parts[k][w][t] + parts[k + 1][w][t]) * 0.5).astype(BF) for t in range(tiles)], axis=1))
            out.append(jnp.concatenate(wins, axis=0))
        return out

    def shifted(where, rows):
        tiles = where.shape[1]
        return [
            jnp.concatenate([
                jnp.concatenate([where[w, t, EDGE + d : EDGE + d + rows, :].astype(BF) for t in range(tiles)], axis=1)
                for w in range(2)], axis=0)
            for d in (-1, 0, 1)
        ]

    def back_conv(before, here, after, weight, rows, where):
        none = jnp.zeros((2 * rows, WIDE - TAPS), BF)
        even = jnp.concatenate([after, here, here, before, before, none], axis=1)
        odd = jnp.concatenate([after, after, here, here, before, none], axis=1)
        total = dot_t(jnp.concatenate([even, odd], axis=0), weight[...]) * 0.5
        even, odd = total[0 : 2 * rows], total[2 * rows : 4 * rows]
        for w in range(2):
            for t in range(where.shape[1]):
                lanes = slice(t * 128, (t + 1) * 128)
                where[w, t, pl.ds(0, rows, stride=2), :] = even[w * rows : (w + 1) * rows, lanes]
                where[w, t, pl.ds(1, rows, stride=2), :] = odd[w * rows : (w + 1) * rows, lanes]

    for d in (1, 2, 3):
        arrived(g_slot.at[slot_of(d)], s_col.at[0, d], r_col.at[0, d])
    edges(g_slot, 16, g_prev, g_next, 0)
    for d in (1, 2, 3):
        arrived(act_slot.at[slot_of(d)], s_col.at[1, d], r_col.at[1, d])
    edges(act_slot, 64, act_prev, act_next, 1)

    gain_b = jnp.concatenate([gain_b_ref[...], jnp.zeros((1, 128), F32)], axis=1)
    hot = one_hot_lanes(lanes_ref[2:3, 0:512] + zh * 11, CMID + 128)
    gain_b_all = spread_gain(gain_b, hot)
    hot = one_hot_lanes(lanes_ref[1:2, 0:512] + ch * 352, CMID + 128)
    gain_b_own = spread_gain(gain_b, hot)
    hot = one_hot_lanes(lanes_ref[3:4, 0:512] + ch * 320, CIN)
    gain_a_own = spread_gain(gain_a_ref[...], hot)
    feat_own = dot(feat_ref[...], hot)
    normed_a = feat_own * inv_a
    factor_a = gelu_slope(normed_a * gain_a_own) * gain_a_own

    for way in (0, 1):
        ring_wb_done(1, way)
        ring_wb(2, way)
    for way in (0, 1):
        ring_wa_done(0, way)
        ring_wa(1, way)
    edges_done(act_prev, act_next, 1)
    lay(act_slot, 64, act_prev, act_next, act_rows)
    for k, tap in enumerate(pooled_taps(act_rows, 128)):
        taps_a[k, :, 0:384] = tap
    for way in (0, 1):
        ring_wb_done(2, way)
        ring_wb(3, way)
    edges_done(g_prev, g_next, 0)
    lay(g_slot, 16, g_prev, g_next, g_rows)
    for way in (0, 1):
        ring_wa_done(1, way)

    total = dot(taps_a[0], whole_a[:, 0:384])
    for k in range(1, 5):
        total += dot(taps_a[k], whole_a[:, k * 384 : (k + 1) * 384])
    for w in range(2):
        acc_a[w] = total[w * 128 : (w + 1) * 128]
    for z in range(NZ):
        for w in range(2):
            mid_send[z, w * 32 : (w + 1) * 32, :] = total[w * 128 + z * 32 : w * 128 + (z + 1) * 32].astype(BF)
    for d in (1, 2, 3):
        t = (zh + d) % NZ
        start(mid_send.at[t], mid_recv.at[zh], s_col.at[2, d], r_col.at[2, d], at_z(d))

    for way in (0, 1):
        ring_wb_done(3, way)
    before, here, after = shifted(g_rows, 64)
    back_conv(before, here, after, whole_b, 64, back_rows)
    for z in range(NZ):
        for c in range(NC):
            for w in range(2):
                back_send[z * NC + c, w * 32 : (w + 1) * 32, :] = back_rows[w, c, z * 32 : (z + 1) * 32, :].astype(BF)

    def scatter(src, dst, ssem, rsem, whole):
        @pl.loop(1, 16)
        def _(d):
            t, dev = member(d)
            pltpu.make_async_remote_copy(
                src_ref=src.at[t] if whole else src.at[t // NC], dst_ref=dst.at[own], send_sem=ssem.at[d],
                recv_sem=rsem.at[d], device_id=dev, device_id_type=MESH,
            ).start()

    def scattered(dst, ssem, rsem):
        @pl.loop(1, 16)
        def _(d):
            arrived(dst.at[(own - d + 16) % 16], ssem.at[d], rsem.at[d])

    def scatter_sent(src, ssem, rsem):
        @pl.loop(1, 16)
        def _(d):
            pltpu.make_async_remote_copy(
                src_ref=src.at[0], dst_ref=src.at[0], send_sem=ssem.at[d], recv_sem=rsem.at[d],
                device_id=(seq, ch), device_id_type=MESH,
            ).wait_send()

    scatter(back_send, back_recv, s_b, r_b, True)
    back_recv[own] = back_send[own]

    for d in (1, 2, 3):
        arrived(mid_recv.at[slot_of(d)], s_col.at[2, d], r_col.at[2, d])
    total = jnp.concatenate([acc_a[w, pl.ds(pl.multiple_of(zh * 32, 32), 32), :] for w in range(2)], axis=0)
    for d in (1, 2, 3):
        total += mid_recv[slot_of(d)].astype(F32)
    mid = (total + bias_pad[0:1, :]).astype(BF)
    mid_f = mid.astype(F32)
    squares = jnp.sum(mid_f * mid_f, axis=-1, keepdims=True)
    mid_wide = jnp.concatenate([mid, jnp.zeros((64, 128), BF)], axis=1)
    mid_own = dot(mid_wide, one_hot_lanes(lanes_ref[1:2, 0:512], 512))
    lane = lax.broadcasted_iota(jnp.int32, (64, 128), 1)
    high, middle, low = three_parts(squares)
    for z in range(NZ):
        piece = mid_own[:, z * 128 : (z + 1) * 128]
        piece = jnp.where(lane == 96, high, jnp.where(lane == 97, middle, jnp.where(lane == 98, low, piece)))
        x_send[z] = piece.astype(BF)
    scatter(x_send, x_recv, s_x, r_x, False)
    x_recv[own] = x_send[zh]

    hot = one_hot_rows(rows_ref[:, 0:1], 512)
    for k in range(4):
        turned_a[:, k * 512 : (k + 1) * 512] = dot(hot, whole_a[:, k * 512 : (k + 1) * 512]).astype(BF)

    def inverse(z):
        total = jnp.zeros((64, 1), F32)
        for c in range(NC):
            part = x_recv[z * NC + c, :, 96:99].astype(F32)
            total += jnp.sum(part, axis=-1, keepdims=True)
        return lax.rsqrt(total * (1.0 / CMID) + EPS)

    scattered(x_recv, s_x, r_x)
    inv_b = inverse(zh)
    normed_b = mid_own * inv_b
    factor_b = gelu_slope(normed_b * gain_b_own) * gain_b_own
    scattered(back_recv, s_b, r_b)
    back = jnp.concatenate(
        [
            back_recv[z * NC].astype(F32) + back_recv[z * NC + 1].astype(F32)
            + back_recv[z * NC + 2].astype(F32) + back_recv[z * NC + 3].astype(F32)
            for z in range(NZ)
        ],
        axis=1,
    )
    grad_n = back * factor_b
    in_send[...] = jnp.broadcast_to(jnp.sum(grad_n * normed_b, axis=-1, keepdims=True), (64, 128))
    for d in (1, 2, 3):
        start(in_send, in_recv.at[ch], s_col.at[3, d], r_col.at[3, d], at_c(d))

    for z in range(NZ):
        inv = inverse(z)
        values = jnp.concatenate([x_recv[z * NC + c].astype(F32) for c in range(NC)], axis=1)
        b_slot[z] = gelu_tanh(values * inv * gain_b_all).astype(BF)
    edges(b_slot, 32, b_prev, b_next, 2)

    inner = in_send[...]
    for d in (1, 2, 3):
        at = (ch - d + NC) % NC
        arrived(in_recv.at[at], s_col.at[3, d], r_col.at[3, d])
        inner += in_recv[at]
    inner = jnp.concatenate([inner * (1.0 / CMID)] * 4, axis=1)
    grad_mid = (inv_b * (grad_n - normed_b * inner)).astype(BF)
    gm_slot[zh] = dot(grad_mid, one_hot_rows(rows_ref[:, 3:4], 384)).astype(BF)
    for d in (1, 2, 3):
        start(gm_slot.at[zh], gm_slot.at[zh], s_col.at[4, d], r_col.at[4, d], at_z(d))

    edges_done(b_prev, b_next, 2)
    lay(b_slot, 32, b_prev, b_next, b_rows)
    taps = pooled_taps(b_rows, 64)
    total = dot(taps[0], whole_b[:, 0:384])
    for k in range(1, 5):
        total += dot(taps[k], whole_b[:, k * 384 : (k + 1) * 384])
    for w in range(2):
        acc_b[w] = total[w * 64 : (w + 1) * 64]
    for z in range(NZ):
        for w in range(2):
            pool_send[z, w * 16 : (w + 1) * 16, :] = total[w * 64 + z * 16 : w * 64 + (z + 1) * 16].astype(BF)

    for d in (1, 2, 3):
        arrived(gm_slot.at[slot_of(d)], s_col.at[4, d], r_col.at[4, d])
    edges(gm_slot, 32, gm_prev, gm_next, 3)
    for d in (1, 2, 3):
        t = (zh + d) % NZ
        start(pool_send.at[t], pool_recv.at[zh], s_col.at[5, d], r_col.at[5, d], at_z(d))

    edges_done(gm_prev, gm_next, 3)
    lay(gm_slot, 32, gm_prev, gm_next, gm_rows)
    before, here, after = shifted(gm_rows, 128)
    back_conv(before, here, after, turned_a, 128, out_rows)
    for z in range(NZ):
        for c in range(NC):
            for w in range(2):
                out_send[z * NC + c, w * 64 : (w + 1) * 64, :] = out_rows[w, c, z * 64 : (z + 1) * 64, :].astype(BF)
    scatter(out_send, out_recv, s_o, r_o, True)
    out_recv[own] = out_send[own]

    for d in (1, 2, 3):
        arrived(pool_recv.at[slot_of(d)], s_col.at[5, d], r_col.at[5, d])
    total = jnp.concatenate([acc_b[w, pl.ds(pl.multiple_of(zh * 16, 16), 16), :] for w in range(2)], axis=0)
    for d in (1, 2, 3):
        total += pool_recv[slot_of(d)].astype(F32)
    pooled_ref[...] = (total + bias_b_ref[...]).astype(BF)

    scattered(out_recv, s_o, r_o)
    back = jnp.concatenate(
        [
            out_recv[z * NC].astype(F32) + out_recv[z * NC + 1].astype(F32)
            + out_recv[z * NC + 2].astype(F32) + out_recv[z * NC + 3].astype(F32)
            for z in range(NZ)
        ],
        axis=1,
    )
    grad_n = back * factor_a
    ia_send[...] = jnp.broadcast_to(jnp.sum(grad_n * normed_a, axis=-1, keepdims=True), (128, 128))
    for d in (1, 2, 3):
        start(ia_send, ia_recv.at[ch], s_col.at[6, d], r_col.at[6, d], at_c(d))
    hot = one_hot_rows(rows_ref[:, 4:5], 384)
    inner = ia_send[...]
    for d in (1, 2, 3):
        at = (ch - d + NC) % NC
        arrived(ia_recv.at[at], s_col.at[6, d], r_col.at[6, d])
        inner += ia_recv[at]
    inner = jnp.concatenate([inner * (1.0 / CIN)] * 4, axis=1)
    grad = (inv_a * (grad_n - normed_a * inner)).astype(BF)
    grad_ref[...] = dot(grad, hot)[:, 0:320].astype(BF)

    for copy in pending:
        copy.wait_send()
    scatter_sent(back_send, s_b, r_b)
    scatter_sent(x_send, s_x, r_x)
    scatter_sent(out_send, s_o, r_o)


def per_device(dna_features, gain_a, conv_a, bias_a, gain_b, conv_b, bias_b, grad_out):
    lanes, rows = index_tables()
    dma = pltpu.SemaphoreType.DMA
    vmem = pltpu.VMEM
    pooled, grad = pl.pallas_call(
        kernel,
        out_shape=(jax.ShapeDtypeStruct((32, 384), BF), jax.ShapeDtypeStruct((128, 320), BF)),
        in_specs=[pl.BlockSpec(memory_space=vmem)] * 10,
        out_specs=[pl.BlockSpec(memory_space=vmem)] * 2,
        scratch_shapes=[
            vmem((8, 64, 384), BF), vmem((4, 64, 384), BF), vmem((512, WIDE), BF), vmem((512, WIDE), BF),
            vmem((512, WIDE), BF), vmem((8, 384), F32),
            vmem((4, 128, 384), BF), vmem((2, 16, 384), BF), vmem((2, 16, 384), BF), vmem((2, 3, 288, 128), F32),
            vmem((5, 256, 512), BF), vmem((4, 128, 384), BF),
            vmem((4, 32, 384), BF), vmem((2, 16, 384), BF), vmem((2, 16, 384), BF), vmem((2, 3, 96, 128), F32),
            vmem((2, 4, 128, 128), F32), vmem((16, 64, 128), BF), vmem((16, 64, 128), BF),
            vmem((2, 128, 384), F32), vmem((4, 64, 384), BF), vmem((4, 64, 384), BF),
            vmem((4, 64, 128), BF), vmem((16, 64, 128), BF), vmem((4, 64, 512), BF), vmem((2, 16, 512), BF),
            vmem((2, 16, 512), BF), vmem((2, 4, 160, 128), F32),
            vmem((4, 32, 384), BF), vmem((4, 32, 384), BF), vmem((2, 64, 384), F32),
            vmem((64, 128), F32), vmem((4, 64, 128), F32), vmem((4, 64, 384), BF), vmem((2, 16, 384), BF),
            vmem((2, 16, 384), BF), vmem((2, 3, 160, 128), F32),
            vmem((2, 4, 256, 128), F32), vmem((16, 128, 128), BF), vmem((16, 128, 128), BF),
            vmem((128, 128), F32), vmem((4, 128, 128), F32),
            dma((2, 4)), dma((2, 4)), dma((4,)), dma((4,)), dma((2, 4)), dma((2, 4)), dma((2, 2)), dma((2, 2)),
            dma((7, 4)), dma((7, 4)), dma((4, 4)), dma((4, 4)),
            dma((16,)), dma((16,)), dma((16,)), dma((16,)), dma((16,)), dma((16,)),
        ],
        compiler_params=pltpu.CompilerParams(
            collective_id=0, has_side_effects=True, vmem_limit_bytes=48 * 1024 * 1024
        ),
        cost_estimate=pl.CostEstimate(flops=3_000_000_000, bytes_accessed=8_000_000, transcendentals=800_000),
    )(
        dna_features.reshape(128, CIN), conv_a, conv_b, gain_a.reshape(1, CIN), bias_a.reshape(1, 352),
        gain_b.reshape(1, CMID), bias_b.reshape(1, 384), grad_out.reshape(32, 384), jnp.asarray(lanes), jnp.asarray(rows),
    )
    return pooled.reshape(2, 16, 384), grad.reshape(2, 64, 320)


def solution(mesh):
    return jax.shard_map(
        per_device,
        mesh=mesh,
        in_specs=(
            P(None, "seq", None), P(), P(None, "seq", "ch"), P("ch"), P(), P(None, "seq", "ch"), P("ch"),
            P(None, "seq", "ch"),
        ),
        out_specs=(P(None, "seq", "ch"), P(None, "seq", "ch")),
        check_vma=False,
    )
```

```python
import math

import jax
import jax.numpy as jnp
import numpy as np
from jax import lax
from jax.experimental import pallas as pl
from jax.experimental.pallas import tpu as pltpu
from jax.sharding import PartitionSpec as P

EPS = 1e-06
ROOT = math.sqrt(2.0 / math.pi)
MESH = pl.DeviceIdType.MESH
BF = jnp.bfloat16
F32 = jnp.float32
NY, NX, NZ, NC = 8, 4, 4, 4
CIN, CMID = 1280, 1408
EDGE = 16
WIDE = 2048
TAPS = 5 * 384


def gelu_tanh(z):
    return 0.5 * z * (1.0 + jnp.tanh(ROOT * (z + 0.044715 * z * z * z)))


def gelu_slope(z):
    t = jnp.tanh(ROOT * (z + 0.044715 * z * z * z))
    return 0.5 * (1.0 + t) + 0.5 * z * (1.0 - t * t) * ROOT * (1.0 + 3.0 * 0.044715 * z * z)


def index_tables():
    lanes = np.full((8, 1536), -100000, np.int32)
    rows = np.full((512, 8), -100000, np.int32)
    for zb in range(NZ):
        for xb in range(NX):
            for yb in range(NY):
                for i in range(10):
                    lanes[0, zb * 384 + xb * 80 + yb * 10 + i] = ((yb * 4 + xb) * 4 + zb) * 10 + i
            for yy in range(2):
                for i in range(11):
                    q = yy * 48 + xb * 11 + i
                    here = ((yy * 4 + xb) * 4 + zb) * 11 + i
                    lanes[1, zb * 128 + q] = here
                    rows[zb * 128 + q, 3] = here
                for i in range(10):
                    q = xb * 20 + yy * 10 + i
                    here = ((yy * 4 + xb) * 4 + zb) * 10 + i
                    lanes[3, zb * 128 + q] = here
                    rows[zb * 128 + q, 4] = here
    for cb in range(NC):
        for xb in range(NX):
            for yy in range(2):
                for i in range(11):
                    lanes[2, cb * 128 + yy * 48 + xb * 11 + i] = (((cb * 2 + yy) * 4 + xb) * 4) * 11 + i
                for i in range(10):
                    rows[cb * 128 + xb * 20 + yy * 10 + i, 0] = xb * 80 + (cb * 2 + yy) * 10 + i
    for k in range(5):
        for yb in range(NY):
            for i in range(10):
                rows[k * 80 + yb * 10 + i, 1] = yb * 64 + k * 10 + i
        for xb in range(NX):
            for i in range(11):
                rows[k * 48 + xb * 11 + i, 2] = xb * 64 + k * 11 + i
    return lanes, rows


def dot(a, b):
    return lax.dot_general(a, b, (((1,), (0,)), ((), ())), preferred_element_type=F32)


def dot_t(a, b):
    return lax.dot_general(a, b, (((1,), (1,)), ((), ())), preferred_element_type=F32)


def one_hot_lanes(table, depth):
    row = lax.broadcasted_iota(jnp.int32, (depth, table.shape[1]), 0)
    return jnp.where(row == table, 1.0, 0.0).astype(BF)


def one_hot_rows(table, depth):
    col = lax.broadcasted_iota(jnp.int32, (table.shape[0], depth), 1)
    return jnp.where(col == table, 1.0, 0.0).astype(BF)


def three_parts(v):
    high = v.astype(BF).astype(F32)
    rest = v - high
    middle = rest.astype(BF).astype(F32)
    return high, middle, rest - middle


def spread_gain(gain, hot):
    high, middle, low = three_parts(gain)
    row = lax.broadcasted_iota(jnp.int32, (16, gain.shape[1]), 0)
    stack = jnp.where(row == 0, high, jnp.where(row == 1, middle, jnp.where(row == 2, low, 0.0)))
    return jnp.sum(dot(stack.astype(BF), hot), axis=0, keepdims=True)


def kernel(
    feat_in, wa_in, wb_in, gain_a_in, bias_a_in, gain_b_in, bias_b_in, g_in, lanes_in, rows_in,
    pooled_ref, grad_ref,
    feat_ref, wa_ref, wb_ref, gain_a_ref, bias_a_ref, gain_b_ref, bias_b_ref, g_ref, lanes_ref, rows_ref,
    first_a, first_b, whole_a, turned_a, whole_b, bias_pad,
    act_slot, act_prev, act_next, act_rows, taps_a, send_act,
    g_slot, g_send, g_prev, g_next, g_rows,
    back_rows, back_over, back_twin, back_send, back_recv,
    acc_a, mid_send, mid_recv,
    x_send, x_recv, b_slot, b_prev, b_next, b_rows,
    pool_send, pool_recv, acc_b,
    in_send, in_recv, gm_slot, gm_prev, gm_next, gm_rows,
    out_rows, out_over, out_twin, out_send, out_recv, ia_send, ia_recv,
    s_fa, r_fa, s_fb, r_fb, s_wb, r_wb, s_wa, r_wa, s_col, r_col, s_edge, r_edge,
    s_b, r_b, s_x, r_x, s_o, r_o, s_in, s_gm, s_edge_gm, s_af, r_af, s_tw, r_tw,
):
    seq = lax.axis_index("seq")
    ch = lax.axis_index("ch")
    zh = seq % NZ
    col = seq // NZ
    xi = col % NX
    yi = col // NX
    own = zh * NC + ch
    core = ch % 2
    zl = ch // 2
    twin = (seq, ch + 1 - 2 * core)
    own8 = zh * 2 + zl
    pending = []
    loads = [
        pltpu.make_async_copy(src, dst, s_in.at[i])
        for i, (src, dst) in enumerate((
            (wa_in, wa_ref), (wb_in, wb_ref), (rows_in, rows_ref), (lanes_in, lanes_ref), (feat_in, feat_ref),
            (gain_a_in, gain_a_ref), (g_in, g_ref), (bias_a_in, bias_a_ref), (gain_b_in, gain_b_ref),
            (bias_b_in, bias_b_ref),
        ))
    ]
    for load in loads:
        load.start()

    def start(src, dst, ssem, rsem, dev):
        copy = pltpu.make_async_remote_copy(
            src_ref=src, dst_ref=dst, send_sem=ssem, recv_sem=rsem, device_id=dev, device_id_type=MESH
        )
        copy.start()
        pending.append(copy)

    def arrived(dst, ssem, rsem):
        pltpu.make_async_remote_copy(
            src_ref=dst, dst_ref=dst, send_sem=ssem, recv_sem=rsem, device_id=(seq, ch), device_id_type=MESH
        ).wait_recv()

    def at_y(d):
        return ((((yi + d + NY) % NY) * NX + xi) * NZ + zh, ch)

    def at_x(d):
        return ((yi * NX + (xi + d + NX) % NX) * NZ + zh, ch)

    def at_z(d):
        return (col * NZ + (zh + d) % NZ, ch)

    def at_c(d):
        return (seq, (ch + d) % NC)

    def at_col(d):
        return (((col + d + 32) % 32) * NZ + zh, ch)

    def member(d):
        tz, tc = (zh + d // NC) % NZ, (ch + d % NC) % NC
        return tz * NC + tc, (col * NZ + tz, tc)

    def source(d):
        return ((zh - d // NC + NZ) % NZ) * NC + (ch - d % NC + NC) % NC

    def beside(way, z):
        return (((col + way + 32) % 32) * NZ + z, ch)

    barrier = pltpu.get_barrier_semaphore()

    def greet(dev):
        pl.semaphore_signal(barrier, inc=1, device_id=dev, device_id_type=MESH)

    for d in (1, 2, 3):
        greet(at_x(d))
    for d in (-1, 1):
        greet(at_y(d))
        for z in range(NZ):
            greet(beside(d, z))

    @pl.loop(1, 16)
    def _(d):
        greet(member(d)[1])

    for load in loads:
        load.wait()
    gain_a = gain_a_ref[...].reshape(1, CIN)
    gain_b = gain_b_ref[...].reshape(1, CMID)

    first_a[yi] = jnp.zeros((64, 384), BF)
    bias_pad[...] = jnp.zeros((8, 384), F32)
    bias_pad[0:1, 0:352] = bias_a_ref[...].reshape(1, 352)
    pack_a = jnp.zeros((64, 352), F32)
    pack_b = jnp.zeros((64, 384), F32)
    for k in range(5):
        pick = lax.broadcasted_iota(jnp.int32, (64, 10), 0) == lax.broadcasted_iota(jnp.int32, (64, 10), 1) + 10 * k
        pack_a += dot(jnp.where(pick, 1.0, 0.0).astype(BF), wa_ref[k])
        pick = lax.broadcasted_iota(jnp.int32, (64, 11), 0) == lax.broadcasted_iota(jnp.int32, (64, 11), 1) + 11 * k
        pack_b += dot(jnp.where(pick, 1.0, 0.0).astype(BF), wb_ref[k])
    first_a[yi, :, 0:352] = pack_a.astype(BF)
    first_b[xi] = pack_b.astype(BF)
    whole_a[320:512, :] = jnp.zeros((192, WIDE), BF)
    whole_a[0:320, TAPS:WIDE] = jnp.zeros((320, WIDE - TAPS), BF)
    whole_b[:, TAPS:WIDE] = jnp.zeros((512, WIDE - TAPS), BF)
    for c in range(NC):
        whole_b[c * 128 + 96 : c * 128 + 128, 0:TAPS] = jnp.zeros((32, TAPS), BF)
    taps_a[:, :, 384:512] = jnp.zeros((5, 256, 128), BF)
    pl.semaphore_wait(barrier, 28)

    half = ((0, 32), (32, 32))
    parts = ((0, 1152), (1152, 768))

    def ring_fa(r, way):
        sign = 1 if way == 0 else -1
        at, n = (0, 64) if r < 3 else half[way]
        b = (yi - sign * r + NY) % NY
        ref = first_a.at[b, pl.ds(at, n), :]
        start(ref, ref, s_fa.at[way, r], r_fa.at[way, r], at_y(sign))

    def ring_fa_done(r, way):
        sign = 1 if way == 0 else -1
        at, n = (0, 64) if r < 3 else half[way]
        b = (yi - sign * (r + 1) + NY) % NY
        arrived(first_a.at[b, pl.ds(at, n), :], s_fa.at[way, r], r_fa.at[way, r])

    def place_a(b):
        return pl.multiple_of(b * 80, 16)

    def place_b(b):
        return pl.multiple_of((b // 2) * 128 + (b % 2) * 48, 16)

    def ring_wb(r, way, c):
        sign = 1 if way == 0 else -1
        ref = whole_b.at[pl.ds(place_b((yi - sign * r + NY) % NY), 48), pl.ds(*parts[c])]
        start(ref, ref, s_wb.at[way, r, c], r_wb.at[way, r, c], at_y(sign))

    def ring_wb_done(r, way, c):
        sign = 1 if way == 0 else -1
        ref = whole_b.at[pl.ds(place_b((yi - sign * (r + 1) + NY) % NY), 48), pl.ds(*parts[c])]
        arrived(ref, s_wb.at[way, r, c], r_wb.at[way, r, c])

    def ring_wa(r, way, c):
        sign = 1 if way == 0 else -1
        ref = whole_a.at[pl.ds(place_a((xi - sign * r + NX) % NX), 80), pl.ds(*parts[c])]
        start(ref, ref, s_wa.at[way, r, c], r_wa.at[way, r, c], at_x(sign))

    def ring_wa_done(r, way, c):
        sign = 1 if way == 0 else -1
        ref = whole_a.at[pl.ds(place_a((xi - sign * (r + 1) + NX) % NX), 80), pl.ds(*parts[c])]
        arrived(ref, s_wa.at[way, r, c], r_wa.at[way, r, c])

    def pass_on(ring, done, r, last, rank):
        for way in (0, 1):
            c = way if rank == 0 else 1 - way
            done(r, way, c)
            if r + 1 < last or (r + 1 == last and rank == 0):
                ring(r + 1, way, c)

    for way in (0, 1):
        ring_fa(0, way)
    for d in (1, 2, 3):
        start(first_b.at[xi], first_b.at[xi], s_fb.at[d], r_fb.at[d], at_x(d))

    def slot_of(d):
        return (zh - d + NZ) % NZ

    def inverse_a(v):
        return lax.rsqrt(jnp.sum(v * v, axis=-1, keepdims=True) * (1.0 / CIN) + EPS)

    feat = feat_ref[core].astype(F32)
    act = gelu_tanh(feat * inverse_a(feat) * gain_a).astype(BF)
    mine = pl.ds(pl.multiple_of(core * 64, 64), 64)
    others = pl.ds(pl.multiple_of(64 - core * 64, 64), 64)

    def subset(d):
        t = (zh + d) % NZ
        hot = one_hot_lanes(lanes_ref[0:1, pl.ds(pl.multiple_of(t * 384, 128), 384)], CIN)
        part = dot(act, hot).astype(BF)
        if d == 0:
            act_slot[zh, mine, :] = part
            share_act(0)
        else:
            send_act[d] = part
            start(send_act.at[d], act_slot.at[zh, mine, :], s_col.at[1, d], r_col.at[1, d], at_z(d))

    def share_act(d):
        ref = act_slot.at[slot_of(d), mine, :]
        start(ref, ref, s_af.at[d], r_af.at[d], twin)

    def fa_on(r):
        for way in (0, 1):
            ring_fa_done(r, way)
            ring_fa(r + 1, way)

    subset(2)

    for d in (1, 2, 3):
        arrived(first_b.at[(xi - d + NX) % NX], s_fb.at[d], r_fb.at[d])
    hot_b = one_hot_rows(rows_ref[0:240, 2:3], 256)
    block = dot(hot_b, first_b[...].reshape(256, 384)).astype(BF)
    for k in range(5):
        whole_b[pl.ds(place_b(yi), 48), k * 384 : (k + 1) * 384] = block[k * 48 : (k + 1) * 48]
    for rank in (0, 1):
        for way in (0, 1):
            ring_wb(0, way, way if rank == 0 else 1 - way)
    fa_on(0)
    subset(1)
    fa_on(1)
    subset(3)
    fa_on(2)
    subset(0)
    g_own = g_ref[...].reshape(32, 384)
    g_slot[zh] = g_own
    g_send[...] = g_own
    for d in (1, 2, 3):
        start(g_send, g_slot.at[zh], s_col.at[0, d], r_col.at[0, d], at_z(d))
    hot_a = one_hot_rows(rows_ref[0:400, 1:2], 512)
    for way in (0, 1):
        ring_fa_done(3, way)
    block = dot(hot_a, first_a[...].reshape(512, 384)).astype(BF)
    for k in range(5):
        whole_a[pl.ds(place_a(xi), 80), k * 384 : (k + 1) * 384] = block[k * 80 : (k + 1) * 80]
    for rank in (0, 1):
        for way in (0, 1):
            ring_wa(0, way, way if rank == 0 else 1 - way)
    pass_on(ring_wb, ring_wb_done, 0, 3, 0)
    for d in (1, 3, 2):
        arrived(act_slot.at[slot_of(d), mine, :], s_col.at[1, d], r_col.at[1, d])
        share_act(d)
    pass_on(ring_wb, ring_wb_done, 0, 3, 1)

    def edges(slots, rows, prev, nxt, n):
        for w in range(2):
            lo = slots.at[0, pl.ds(w * rows, EDGE), :]
            hi = slots.at[3, pl.ds(w * rows + rows - EDGE, EDGE), :]
            start(hi, prev.at[w], s_edge.at[n, w], r_edge.at[n, w], at_col(1))
            start(lo, nxt.at[w], s_edge.at[n, 2 + w], r_edge.at[n, 2 + w], at_col(-1))

    def edges_done(prev, nxt, n):
        for w in range(2):
            arrived(prev.at[w], s_edge.at[n, w], r_edge.at[n, w])
            arrived(nxt.at[w], s_edge.at[n, 2 + w], r_edge.at[n, 2 + w])

    is_first = jnp.where(col == 0, 0.0, 1.0).astype(F32)
    is_last = jnp.where(col == 31, 0.0, 1.0).astype(F32)

    def lay(slots, rows, prev, nxt, where):
        tiles = where.shape[1]
        for w in range(2):
            for t in range(tiles):
                lanes = slice(t * 128, (t + 1) * 128)
                where[w, t, 0:EDGE, :] = prev[w, :, lanes].astype(F32) * is_first
                for z in range(NZ):
                    at = EDGE + z * rows
                    where[w, t, at : at + rows, :] = slots[z, w * rows : (w + 1) * rows, lanes].astype(F32)
                at = EDGE + NZ * rows
                where[w, t, at : at + EDGE, :] = nxt[w, :, lanes].astype(F32) * is_last

    def pooled_taps(where, rows):
        tiles = where.shape[1]
        parts = [[[where[w, t, pl.ds(EDGE + d, rows, stride=2), :] for t in range(tiles)] for w in range(2)]
                 for d in range(-2, 4)]
        out = []
        for k in range(5):
            wins = []
            for w in range(2):
                wins.append(jnp.concatenate(
                    [((parts[k][w][t] + parts[k + 1][w][t]) * 0.5).astype(BF) for t in range(tiles)], axis=1))
            out.append(jnp.concatenate(wins, axis=0))
        return out

    def shifted(where, rows):
        tiles = where.shape[1]
        return [
            jnp.concatenate([
                jnp.concatenate([where[w, t, EDGE + d : EDGE + d + rows, :].astype(BF) for t in range(tiles)], axis=1)
                for w in range(2)], axis=0)
            for d in (-1, 0, 1)
        ]

    def back_conv(before, here, after, weight, rows, where):
        none = jnp.zeros((2 * rows, WIDE - TAPS), BF)
        even = jnp.concatenate([after, here, here, before, before, none], axis=1)
        odd = jnp.concatenate([after, after, here, here, before, none], axis=1)
        total = dot_t(jnp.concatenate([even, odd], axis=0), weight[...]) * 0.5
        even, odd = total[0 : 2 * rows], total[2 * rows : 4 * rows]
        for w in range(2):
            for t in range(where.shape[1]):
                lanes = slice(t * 128, (t + 1) * 128)
                where[w, t, pl.ds(0, rows, stride=2), :] = even[w * rows : (w + 1) * rows, lanes]
                where[w, t, pl.ds(1, rows, stride=2), :] = odd[w * rows : (w + 1) * rows, lanes]

    gain_b = jnp.concatenate([gain_b, jnp.zeros((1, 128), F32)], axis=1)
    hot = one_hot_lanes(lanes_ref[2:3, 0:512] + zh * 11, CMID + 128)
    gain_b_all = spread_gain(gain_b, hot)
    pass_on(ring_wb, ring_wb_done, 1, 3, 0)
    pass_on(ring_wa, ring_wa_done, 0, 1, 0)
    hot = one_hot_lanes(lanes_ref[1:2, 0:512] + ch * 352, CMID + 128)
    gain_b_own = spread_gain(gain_b, hot)
    for d in (1, 2, 3):
        arrived(g_slot.at[slot_of(d)], s_col.at[0, d], r_col.at[0, d])
    edges(g_slot, 16, g_prev, g_next, 0)
    pass_on(ring_wb, ring_wb_done, 1, 3, 1)
    for d in range(NZ):
        arrived(act_slot.at[slot_of(d), others, :], s_af.at[d], r_af.at[d])
    edges(act_slot, 64, act_prev, act_next, 1)
    hot = one_hot_lanes(lanes_ref[3:4, 0:512] + ch * 320, CIN)
    gain_a_own = spread_gain(gain_a, hot)
    feat_bf = feat_ref[...].reshape(128, CIN)
    inv_a = inverse_a(feat_bf.astype(F32))
    feat_own = dot(feat_bf, hot)
    pass_on(ring_wb, ring_wb_done, 2, 3, 0)
    normed_a = feat_own * inv_a
    factor_a = gelu_slope(normed_a * gain_a_own) * gain_a_own
    edges_done(g_prev, g_next, 0)
    lay(g_slot, 16, g_prev, g_next, g_rows)
    edges_done(act_prev, act_next, 1)
    lay(act_slot, 64, act_prev, act_next, act_rows)
    for k, tap in enumerate(pooled_taps(act_rows, 128)):
        taps_a[k, :, 0:384] = tap
    pass_on(ring_wa, ring_wa_done, 0, 1, 1)
    for way in (0, 1):
        ring_wa_done(1, way, way)

    total = dot(taps_a[0], whole_a[:, 0:384])
    for k in range(1, 5):
        total += dot(taps_a[k], whole_a[:, k * 384 : (k + 1) * 384])
    for w in range(2):
        acc_a[w] = total[w * 128 : (w + 1) * 128]
    for z in range(NZ):
        for w in range(2):
            mid_send[z, w * 32 : (w + 1) * 32, :] = total[w * 128 + z * 32 : w * 128 + (z + 1) * 32].astype(BF)
    for d in (1, 2, 3):
        t = (zh + d) % NZ
        start(mid_send.at[t], mid_recv.at[zh], s_col.at[2, d], r_col.at[2, d], at_z(d))

    pass_on(ring_wb, ring_wb_done, 2, 3, 1)
    for way in (0, 1):
        ring_wb_done(3, way, way)
    before, here, after = shifted(g_rows, 64)
    back_conv(before, here, after, whole_b, 64, back_rows)
    def to_twin(where, per, send, recv, n):
        for z in range(NZ):
            for b in range(2):
                for w in range(2):
                    piece = where[w, b * 2 + 1 - core, z * per : (z + 1) * per, :]
                    send[z * 2 + b, w * per : (w + 1) * per, :] = piece.astype(BF)
        start(send, recv, s_tw.at[n], r_tw.at[n], twin)

    def from_twin(where, per, recv, send, n):
        arrived(recv, s_tw.at[n], r_tw.at[n])
        for z in range(NZ):
            for b in range(2):
                for w in range(2):
                    piece = where[w, b * 2 + core, z * per : (z + 1) * per, :]
                    rows = slice(w * per, (w + 1) * per)
                    send[z * 2 + b, rows, :] = (piece + recv[z * 2 + b, rows, :].astype(F32)).astype(BF)

    def scatter(src, dst, ssem, rsem):
        @pl.loop(1, 8)
        def _(d):
            tz, tb = (zh + d // 2) % NZ, (zl + d % 2) % 2
            pltpu.make_async_remote_copy(
                src_ref=src.at[tz * 2 + tb], dst_ref=dst.at[own8], send_sem=ssem.at[d], recv_sem=rsem.at[d],
                device_id=(col * NZ + tz, tb * 2 + core), device_id_type=MESH,
            ).start()

        dst[own8] = src[own8]

    def scattered(dst, ssem, rsem):
        @pl.loop(1, 8)
        def _(d):
            arrived(dst.at[((zh - d // 2 + NZ) % NZ) * 2 + (zl - d % 2 + 2) % 2], ssem.at[d], rsem.at[d])

    def scatter_sent(src, ssem, rsem):
        @pl.loop(1, 8)
        def _(d):
            pltpu.make_async_remote_copy(
                src_ref=src.at[0], dst_ref=src.at[0], send_sem=ssem.at[d], recv_sem=rsem.at[d],
                device_id=(seq, ch), device_id_type=MESH,
            ).wait_send()

    def to_row(v):
        wide = jnp.broadcast_to(v, (v.shape[0], 128))
        if v.shape[0] < 128:
            wide = jnp.concatenate([wide, jnp.zeros((128 - v.shape[0], 128), F32)], axis=0)
        return jnp.transpose(wide)[0:8]

    def to_column(v, rows):
        return jnp.transpose(jnp.concatenate([v] * 16, axis=0))[0:rows]

    def two_shares(recv):
        return jnp.concatenate(
            [recv[z * 2].astype(F32) + recv[z * 2 + 1].astype(F32) for z in range(NZ)], axis=1)

    to_twin(back_rows, 32, back_over, back_twin, 0)
    from_twin(back_rows, 32, back_twin, back_send, 0)
    scatter(back_send, back_recv, s_b, r_b)

    for d in (1, 2, 3):
        arrived(mid_recv.at[slot_of(d)], s_col.at[2, d], r_col.at[2, d])
    total = jnp.concatenate([acc_a[w, pl.ds(pl.multiple_of(zh * 32, 32), 32), :] for w in range(2)], axis=0)
    for d in (1, 2, 3):
        total += mid_recv[slot_of(d)].astype(F32)
    mid = (total + bias_pad[0:1, :]).astype(BF)
    mid_f = mid.astype(F32)
    squares = jnp.sum(mid_f * mid_f, axis=-1, keepdims=True)
    mid_wide = jnp.concatenate([mid, jnp.zeros((64, 128), BF)], axis=1)
    mid_own = dot(mid_wide, one_hot_lanes(lanes_ref[1:2, 0:512], 512))
    lane = lax.broadcasted_iota(jnp.int32, (64, 128), 1)
    high, middle, low = three_parts(squares)
    for z in range(NZ):
        piece = mid_own[:, z * 128 : (z + 1) * 128]
        piece = jnp.where(lane == 96, high, jnp.where(lane == 97, middle, jnp.where(lane == 98, low, piece)))
        x_send[z] = piece.astype(BF)
    for d in (1, 2, 3):
        start(x_send.at[zh], x_recv.at[own], s_x.at[d], r_x.at[d], at_c(d))
    x_recv[own] = x_send[zh]
    far = [(dz, db) for dz in (2, 1, 3) for db in (0, 1)]
    for n, (dz, db) in enumerate(far):
        tz, tb = (zh + dz) % NZ, (zl + db) % 2
        start(x_send.at[tz], x_recv.at[own], s_x.at[4 + n], r_x.at[4 + n], (col * NZ + tz, tb * 2 + core))

    def x_slot(dz, db, side):
        return x_recv.at[slot_of(dz) * NC + ((zl - db + 2) % 2) * 2 + side]

    hot = one_hot_rows(rows_ref[:, 0:1], 512)
    for k in range(4):
        turned_a[:, k * 512 : (k + 1) * 512] = dot(hot, whole_a[:, k * 512 : (k + 1) * 512]).astype(BF)

    def inverse(z):
        total = jnp.zeros((64, 1), F32)
        for c in range(NC):
            part = x_recv[z * NC + c, :, 96:99].astype(F32)
            total += jnp.sum(part, axis=-1, keepdims=True)
        return lax.rsqrt(total * (1.0 / CMID) + EPS)

    for d in (1, 2, 3):
        arrived(x_recv.at[zh * NC + (ch - d + NC) % NC], s_x.at[d], r_x.at[d])
    inv_b = inverse(zh)
    normed_b = mid_own * inv_b
    factor_b = gelu_slope(normed_b * gain_b_own) * gain_b_own
    scattered(back_recv, s_b, r_b)
    grad_n = two_shares(back_recv) * factor_b
    in_send[...] = to_row(jnp.sum(grad_n * normed_b, axis=-1, keepdims=True))
    for d in (1, 2, 3):
        start(in_send, in_recv.at[ch], s_col.at[3, d], r_col.at[3, d], at_c(d))

    for n, (dz, db) in enumerate(far):
        arrived(x_slot(dz, db, core), s_x.at[4 + n], r_x.at[4 + n])
        start(x_slot(dz, db, core), x_slot(dz, db, core), s_x.at[10 + n], r_x.at[10 + n], twin)
    inner = in_send[...]
    for d in (1, 2, 3):
        at = (ch - d + NC) % NC
        arrived(in_recv.at[at], s_col.at[3, d], r_col.at[3, d])
        inner += in_recv[at]
    inner = jnp.concatenate([to_column(inner * (1.0 / CMID), 64)] * 4, axis=1)
    grad_mid = (inv_b * (grad_n - normed_b * inner)).astype(BF)
    gm_slot[zh] = dot(grad_mid, one_hot_rows(rows_ref[:, 3:4], 384)).astype(BF)
    for d in (1, 2, 3):
        start(gm_slot.at[zh], gm_slot.at[zh], s_col.at[4, d], r_col.at[4, d], at_z(d))

    def last_rows(z, w):
        return pltpu.make_async_remote_copy(
            src_ref=gm_slot.at[3, pl.ds(w * 32 + 16, EDGE), :], dst_ref=gm_prev.at[w], send_sem=s_gm.at[0, z, w],
            recv_sem=s_edge_gm.at[0, w], device_id=beside(1, z), device_id_type=MESH)

    def first_rows(z, w):
        return pltpu.make_async_remote_copy(
            src_ref=gm_slot.at[0, pl.ds(w * 32, EDGE), :], dst_ref=gm_next.at[w], send_sem=s_gm.at[1, z, w],
            recv_sem=s_edge_gm.at[1, w], device_id=beside(-1, z), device_id_type=MESH)

    @pl.when(zh == NZ - 1)
    def _():
        for z in range(NZ):
            for w in range(2):
                last_rows(z, w).start()

    @pl.when(zh == 0)
    def _():
        for z in range(NZ):
            for w in range(2):
                first_rows(z, w).start()

    for n, (dz, db) in enumerate(far):
        arrived(x_slot(dz, db, 1 - core), s_x.at[10 + n], r_x.at[10 + n])
    for z in range(NZ):
        inv = inverse(z)
        values = jnp.concatenate([x_recv[z * NC + c].astype(F32) for c in range(NC)], axis=1)
        b_slot[z] = gelu_tanh(values * inv * gain_b_all).astype(BF)
    edges(b_slot, 32, b_prev, b_next, 2)

    for d in (1, 2, 3):
        arrived(gm_slot.at[slot_of(d)], s_col.at[4, d], r_col.at[4, d])

    for w in range(2):
        arrived(gm_prev.at[w], s_gm.at[0, 0, w], s_edge_gm.at[0, w])
        arrived(gm_next.at[w], s_gm.at[1, 0, w], s_edge_gm.at[1, w])
    lay(gm_slot, 32, gm_prev, gm_next, gm_rows)
    before, here, after = shifted(gm_rows, 128)
    back_conv(before, here, after, turned_a, 128, out_rows)
    to_twin(out_rows, 64, out_over, out_twin, 1)
    from_twin(out_rows, 64, out_twin, out_send, 1)
    scatter(out_send, out_recv, s_o, r_o)

    edges_done(b_prev, b_next, 2)
    lay(b_slot, 32, b_prev, b_next, b_rows)
    taps = pooled_taps(b_rows, 64)
    total = dot(taps[0], whole_b[:, 0:384])
    for k in range(1, 5):
        total += dot(taps[k], whole_b[:, k * 384 : (k + 1) * 384])
    for w in range(2):
        acc_b[w] = total[w * 64 : (w + 1) * 64]
    for z in range(NZ):
        for w in range(2):
            pool_send[z, w * 16 : (w + 1) * 16, :] = total[w * 64 + z * 16 : w * 64 + (z + 1) * 16].astype(BF)

    for d in (1, 2, 3):
        t = (zh + d) % NZ
        start(pool_send.at[t], pool_recv.at[zh], s_col.at[5, d], r_col.at[5, d], at_z(d))

    for d in (1, 2, 3):
        arrived(pool_recv.at[slot_of(d)], s_col.at[5, d], r_col.at[5, d])
    total = jnp.concatenate([acc_b[w, pl.ds(pl.multiple_of(zh * 16, 16), 16), :] for w in range(2)], axis=0)
    for d in (1, 2, 3):
        total += pool_recv[slot_of(d)].astype(F32)
    pooled_ref[...] = (total + bias_b_ref[...].reshape(1, 384)).astype(BF).reshape(2, 16, 384)

    scattered(out_recv, s_o, r_o)
    grad_n = two_shares(out_recv) * factor_a
    ia_send[...] = to_row(jnp.sum(grad_n * normed_a, axis=-1, keepdims=True))
    for d in (1, 2, 3):
        start(ia_send, ia_recv.at[ch], s_col.at[6, d], r_col.at[6, d], at_c(d))
    hot = one_hot_rows(rows_ref[:, 4:5], 384)
    inner = ia_send[...]
    for d in (1, 2, 3):
        at = (ch - d + NC) % NC
        arrived(ia_recv.at[at], s_col.at[6, d], r_col.at[6, d])
        inner += ia_recv[at]
    inner = jnp.concatenate([to_column(inner * (1.0 / CIN), 128)] * 4, axis=1)
    grad = (inv_a * (grad_n - normed_a * inner)).astype(BF)
    grad_ref[...] = dot(grad, hot)[:, 0:320].astype(BF).reshape(2, 64, 320)

    for copy in pending:
        copy.wait_send()
    scatter_sent(back_send, s_b, r_b)
    scatter_sent(out_send, s_o, r_o)

    @pl.when(zh == NZ - 1)
    def _():
        for z in range(NZ):
            for w in range(2):
                last_rows(z, w).wait_send()

    @pl.when(zh == 0)
    def _():
        for z in range(NZ):
            for w in range(2):
                first_rows(z, w).wait_send()


def per_device(dna_features, gain_a, conv_a, bias_a, gain_b, conv_b, bias_b, grad_out):
    lanes, rows = index_tables()
    dma = pltpu.SemaphoreType.DMA
    vmem = pltpu.VMEM
    pooled, grad = pl.pallas_call(
        kernel,
        out_shape=(jax.ShapeDtypeStruct((2, 16, 384), BF), jax.ShapeDtypeStruct((2, 64, 320), BF)),
        in_specs=[pl.BlockSpec(memory_space=pl.ANY)] * 10,
        out_specs=[pl.BlockSpec(memory_space=vmem)] * 2,
        scratch_shapes=[
            vmem((2, 64, CIN), BF), vmem((5, 10, 352), BF), vmem((5, 11, 384), BF), vmem((CIN,), F32), vmem((352,), F32),
            vmem((CMID,), F32), vmem((384,), F32), vmem((2, 16, 384), BF), vmem((8, 1536), jnp.int32), vmem((512, 8), jnp.int32),
            vmem((8, 64, 384), BF), vmem((4, 64, 384), BF), vmem((512, WIDE), BF), vmem((512, WIDE), BF),
            vmem((512, WIDE), BF), vmem((8, 384), F32),
            vmem((4, 128, 384), BF), vmem((2, 16, 384), BF), vmem((2, 16, 384), BF), vmem((2, 3, 288, 128), F32),
            vmem((5, 256, 512), BF), vmem((4, 64, 384), BF),
            vmem((4, 32, 384), BF), vmem((32, 384), BF), vmem((2, 16, 384), BF), vmem((2, 16, 384), BF), vmem((2, 3, 96, 128), F32),
            vmem((2, 4, 128, 128), F32), vmem((8, 64, 128), BF), vmem((8, 64, 128), BF), vmem((8, 64, 128), BF),
            vmem((8, 64, 128), BF), vmem((2, 128, 384), F32), vmem((4, 64, 384), BF), vmem((4, 64, 384), BF),
            vmem((4, 64, 128), BF), vmem((16, 64, 128), BF), vmem((4, 64, 512), BF), vmem((2, 16, 512), BF),
            vmem((2, 16, 512), BF), vmem((2, 4, 160, 128), F32),
            vmem((4, 32, 384), BF), vmem((4, 32, 384), BF), vmem((2, 64, 384), F32),
            vmem((8, 128), F32), vmem((4, 8, 128), F32), vmem((4, 64, 384), BF), vmem((2, 16, 384), BF),
            vmem((2, 16, 384), BF), vmem((2, 3, 160, 128), F32),
            vmem((2, 4, 256, 128), F32), vmem((8, 128, 128), BF), vmem((8, 128, 128), BF), vmem((8, 128, 128), BF),
            vmem((8, 128, 128), BF),
            vmem((8, 128), F32), vmem((4, 8, 128), F32),
            dma((2, 4)), dma((2, 4)), dma((4,)), dma((4,)), dma((2, 4, 2)), dma((2, 4, 2)), dma((2, 2, 2)), dma((2, 2, 2)),
            dma((7, 4)), dma((7, 4)), dma((4, 4)), dma((4, 4)),
            dma((16,)), dma((16,)), dma((16,)), dma((16,)), dma((16,)), dma((16,)), dma((10,)), dma((2, 4, 2)), dma((2, 2)), dma((4,)), dma((4,)),
            dma((2,)), dma((2,)),
        ],
        compiler_params=pltpu.CompilerParams(
            collective_id=0, has_side_effects=True, vmem_limit_bytes=60 * 1024 * 1024
        ),
        cost_estimate=pl.CostEstimate(flops=3_000_000_000, bytes_accessed=8_000_000, transcendentals=800_000),
    )(
        dna_features, conv_a, conv_b, gain_a, bias_a, gain_b, bias_b, grad_out, jnp.asarray(lanes), jnp.asarray(rows),
    )
    return pooled, grad


def solution(mesh):
    return jax.shard_map(
        per_device,
        mesh=mesh,
        in_specs=(
            P(None, "seq", None), P(), P(None, "seq", "ch"), P("ch"), P(), P(None, "seq", "ch"), P("ch"),
            P(None, "seq", "ch"),
        ),
        out_specs=(P(None, "seq", "ch"), P(None, "seq", "ch")),
        check_vma=False,
    )
```

```python
import math

import jax
import jax.numpy as jnp
import numpy as np
from jax import lax
from jax.experimental import pallas as pl
from jax.experimental.pallas import tpu as pltpu
from jax.sharding import PartitionSpec as P

EPS = 1e-06
ROOT = math.sqrt(2.0 / math.pi)
MESH = pl.DeviceIdType.MESH
BF = jnp.bfloat16
F32 = jnp.float32
NY, NX, NZ, NC = 8, 4, 4, 4
CIN, CMID = 1280, 1408
EDGE = 16
WIDE = 2048
TAPS = 5 * 384


def gelu_tanh(z):
    return 0.5 * z * (1.0 + jnp.tanh(ROOT * (z + 0.044715 * z * z * z)))


def gelu_slope(z):
    t = jnp.tanh(ROOT * (z + 0.044715 * z * z * z))
    return 0.5 * (1.0 + t) + 0.5 * z * (1.0 - t * t) * ROOT * (1.0 + 3.0 * 0.044715 * z * z)


def index_tables():
    lanes = np.full((8, 1536), -100000, np.int32)
    rows = np.full((512, 8), -100000, np.int32)
    for zb in range(NZ):
        for xb in range(NX):
            for yb in range(NY):
                for i in range(10):
                    lanes[0, zb * 384 + xb * 80 + yb * 10 + i] = ((yb * 4 + xb) * 4 + zb) * 10 + i
            for yy in range(2):
                for i in range(11):
                    q = yy * 48 + xb * 11 + i
                    here = ((yy * 4 + xb) * 4 + zb) * 11 + i
                    lanes[1, zb * 128 + q] = here
                    rows[zb * 128 + q, 3] = here
                for i in range(10):
                    q = xb * 20 + yy * 10 + i
                    here = ((yy * 4 + xb) * 4 + zb) * 10 + i
                    lanes[3, zb * 128 + q] = here
                    rows[zb * 128 + q, 4] = here
    for cb in range(NC):
        for xb in range(NX):
            for yy in range(2):
                for i in range(11):
                    lanes[2, cb * 128 + yy * 48 + xb * 11 + i] = (((cb * 2 + yy) * 4 + xb) * 4) * 11 + i
                for i in range(10):
                    rows[cb * 128 + xb * 20 + yy * 10 + i, 0] = xb * 80 + (cb * 2 + yy) * 10 + i
    for k in range(5):
        for yb in range(NY):
            for i in range(10):
                rows[k * 80 + yb * 10 + i, 1] = yb * 64 + k * 10 + i
        for xb in range(NX):
            for i in range(11):
                rows[k * 48 + xb * 11 + i, 2] = xb * 64 + k * 11 + i
    return lanes, rows


def dot(a, b):
    return lax.dot_general(a, b, (((1,), (0,)), ((), ())), preferred_element_type=F32)


def dot_t(a, b):
    return lax.dot_general(a, b, (((1,), (1,)), ((), ())), preferred_element_type=F32)


def one_hot_lanes(table, depth):
    row = lax.broadcasted_iota(jnp.int32, (depth, table.shape[1]), 0)
    return jnp.where(row == table, 1.0, 0.0).astype(BF)


def one_hot_rows(table, depth):
    col = lax.broadcasted_iota(jnp.int32, (table.shape[0], depth), 1)
    return jnp.where(col == table, 1.0, 0.0).astype(BF)


def three_parts(v):
    high = v.astype(BF).astype(F32)
    rest = v - high
    middle = rest.astype(BF).astype(F32)
    return high, middle, rest - middle


def spread_gain(gain, hot):
    high, middle, low = three_parts(gain)
    row = lax.broadcasted_iota(jnp.int32, (16, gain.shape[1]), 0)
    stack = jnp.where(row == 0, high, jnp.where(row == 1, middle, jnp.where(row == 2, low, 0.0)))
    return jnp.sum(dot(stack.astype(BF), hot), axis=0, keepdims=True)


def kernel(
    feat_in, wa_in, wb_in, gain_a_in, bias_a_in, gain_b_in, bias_b_in, g_in, lanes_in, rows_in,
    pooled_ref, grad_ref,
    feat_ref, wa_ref, wb_ref, gain_a_ref, bias_a_ref, gain_b_ref, bias_b_ref, g_ref, lanes_ref, rows_ref,
    first_a, first_b, whole_a, turned_a, whole_b, bias_pad,
    act_slot, act_prev, act_next, act_rows, taps_a, send_act,
    g_slot, g_send, g_prev, g_next, g_rows,
    back_rows, back_over, back_twin, back_send, back_recv,
    acc_a, mid_send, mid_recv,
    x_send, x_recv, b_slot, b_prev, b_next, b_rows,
    pool_send, pool_recv, acc_b,
    in_send, in_recv, gm_slot, gm_prev, gm_next, gm_rows,
    out_rows, out_over, out_twin, out_send, out_recv, ia_send, ia_recv,
    s_fa, r_fa, s_fb, r_fb, s_wb, r_wb, s_wa, r_wa, s_col, r_col, s_edge, r_edge,
    s_b, r_b, s_x, r_x, s_o, r_o, s_in, s_gm, s_edge_gm, s_af, r_af, s_tw, r_tw,
):
    seq = lax.axis_index("seq")
    ch = lax.axis_index("ch")
    zh = seq % NZ
    col = seq // NZ
    xi = col % NX
    yi = col // NX
    own = zh * NC + ch
    core = ch % 2
    zl = ch // 2
    twin = (seq, ch + 1 - 2 * core)
    own8 = zh * 2 + zl
    pending = []
    loads = [
        pltpu.make_async_copy(src, dst, s_in.at[i])
        for i, (src, dst) in enumerate((
            (wa_in, wa_ref), (wb_in, wb_ref), (rows_in, rows_ref), (lanes_in, lanes_ref), (feat_in, feat_ref),
            (gain_a_in, gain_a_ref), (g_in, g_ref), (bias_a_in, bias_a_ref), (gain_b_in, gain_b_ref),
            (bias_b_in, bias_b_ref),
        ))
    ]
    for load in loads:
        load.start()

    def start(src, dst, ssem, rsem, dev):
        copy = pltpu.make_async_remote_copy(
            src_ref=src, dst_ref=dst, send_sem=ssem, recv_sem=rsem, device_id=dev, device_id_type=MESH
        )
        copy.start()
        pending.append(copy)

    def arrived(dst, ssem, rsem):
        pltpu.make_async_remote_copy(
            src_ref=dst, dst_ref=dst, send_sem=ssem, recv_sem=rsem, device_id=(seq, ch), device_id_type=MESH
        ).wait_recv()

    def at_y(d):
        return ((((yi + d + NY) % NY) * NX + xi) * NZ + zh, ch)

    def at_x(d):
        return ((yi * NX + (xi + d + NX) % NX) * NZ + zh, ch)

    def at_z(d):
        return (col * NZ + (zh + d) % NZ, ch)

    def at_c(d):
        return (seq, (ch + d) % NC)

    def at_col(d):
        return (((col + d + 32) % 32) * NZ + zh, ch)

    def member(d):
        tz, tc = (zh + d // NC) % NZ, (ch + d % NC) % NC
        return tz * NC + tc, (col * NZ + tz, tc)

    def source(d):
        return ((zh - d // NC + NZ) % NZ) * NC + (ch - d % NC + NC) % NC

    def beside(way, z):
        return (((col + way + 32) % 32) * NZ + z, ch)

    barrier = pltpu.get_barrier_semaphore()

    def greet(dev):
        pl.semaphore_signal(barrier, inc=1, device_id=dev, device_id_type=MESH)

    for d in (1, 2, 3):
        greet(at_x(d))
    for d in (-1, 1):
        greet(at_y(d))
        greet(at_y(2 * d))
        for z in range(NZ):
            greet(beside(d, z))

    @pl.loop(1, 16)
    def _(d):
        greet(member(d)[1])

    for load in loads:
        load.wait()
    gain_a = gain_a_ref[...].reshape(1, CIN)
    gain_b = gain_b_ref[...].reshape(1, CMID)

    first_a[yi] = jnp.zeros((64, 384), BF)
    bias_pad[...] = jnp.zeros((8, 384), F32)
    bias_pad[0:1, 0:352] = bias_a_ref[...].reshape(1, 352)
    pack_a = jnp.zeros((64, 352), F32)
    pack_b = jnp.zeros((64, 384), F32)
    for k in range(5):
        pick = lax.broadcasted_iota(jnp.int32, (64, 10), 0) == lax.broadcasted_iota(jnp.int32, (64, 10), 1) + 10 * k
        pack_a += dot(jnp.where(pick, 1.0, 0.0).astype(BF), wa_ref[k])
        pick = lax.broadcasted_iota(jnp.int32, (64, 11), 0) == lax.broadcasted_iota(jnp.int32, (64, 11), 1) + 11 * k
        pack_b += dot(jnp.where(pick, 1.0, 0.0).astype(BF), wb_ref[k])
    first_a[yi, :, 0:352] = pack_a.astype(BF)
    first_b[xi] = pack_b.astype(BF)
    whole_a[320:512, :] = jnp.zeros((192, WIDE), BF)
    whole_a[0:320, TAPS:WIDE] = jnp.zeros((320, WIDE - TAPS), BF)
    whole_b[:, TAPS:WIDE] = jnp.zeros((512, WIDE - TAPS), BF)
    for c in range(NC):
        whole_b[c * 128 + 96 : c * 128 + 128, 0:TAPS] = jnp.zeros((32, TAPS), BF)
    taps_a[:, :, 384:512] = jnp.zeros((5, 256, 128), BF)
    pl.semaphore_wait(barrier, 30)

    parts = ((0, 1152), (1152, 768))

    def first_block(d, at=0, n=64):
        return first_a.at[(yi + d + NY) % NY, pl.ds(at, n), :]

    hops = (
        ((0, 1, 0, 64), (0, -1, 0, 64), (0, 2, 0, 64), (0, -2, 0, 64)),
        ((-2, 1, 0, 64), (2, -1, 0, 64), (-2, 2, 0, 32), (2, -2, 32, 32)),
    )

    def send_first(step):
        for n, (b, to, at, rows) in enumerate(hops[step]):
            ref = first_block(b, at, rows)
            start(ref, ref, s_fa.at[step, n], r_fa.at[step, n], at_y(to))

    def first_done(step, which):
        for n in which:
            b, to, at, rows = hops[step][n]
            arrived(first_block(b - to, at, rows), s_fa.at[step, n], r_fa.at[step, n])

    def place_a(b):
        return pl.multiple_of(b * 80, 16)

    def place_b(b):
        return pl.multiple_of((b // 2) * 128 + (b % 2) * 48, 16)

    def ring_wb(r, way, c):
        sign = 1 if way == 0 else -1
        ref = whole_b.at[pl.ds(place_b((yi - sign * r + NY) % NY), 48), pl.ds(*parts[c])]
        start(ref, ref, s_wb.at[way, r, c], r_wb.at[way, r, c], at_y(sign))

    def ring_wb_done(r, way, c):
        sign = 1 if way == 0 else -1
        ref = whole_b.at[pl.ds(place_b((yi - sign * (r + 1) + NY) % NY), 48), pl.ds(*parts[c])]
        arrived(ref, s_wb.at[way, r, c], r_wb.at[way, r, c])

    def ring_wa(r, way, c):
        sign = 1 if way == 0 else -1
        ref = whole_a.at[pl.ds(place_a((xi - sign * r + NX) % NX), 80), pl.ds(*parts[c])]
        start(ref, ref, s_wa.at[way, r, c], r_wa.at[way, r, c], at_x(sign))

    def ring_wa_done(r, way, c):
        sign = 1 if way == 0 else -1
        ref = whole_a.at[pl.ds(place_a((xi - sign * (r + 1) + NX) % NX), 80), pl.ds(*parts[c])]
        arrived(ref, s_wa.at[way, r, c], r_wa.at[way, r, c])

    def pass_on(ring, done, r, last, rank):
        for way in (0, 1):
            c = way if rank == 0 else 1 - way
            done(r, way, c)
            if r + 1 < last or (r + 1 == last and rank == 0):
                ring(r + 1, way, c)

    send_first(0)
    for d in (1, 2, 3):
        start(first_b.at[xi], first_b.at[xi], s_fb.at[d], r_fb.at[d], at_x(d))

    def slot_of(d):
        return (zh - d + NZ) % NZ

    def inverse_a(v):
        return lax.rsqrt(jnp.sum(v * v, axis=-1, keepdims=True) * (1.0 / CIN) + EPS)

    feat = feat_ref[core].astype(F32)
    act = gelu_tanh(feat * inverse_a(feat) * gain_a).astype(BF)
    mine = pl.ds(pl.multiple_of(core * 64, 64), 64)
    others = pl.ds(pl.multiple_of(64 - core * 64, 64), 64)

    def subset(d):
        t = (zh + d) % NZ
        hot = one_hot_lanes(lanes_ref[0:1, pl.ds(pl.multiple_of(t * 384, 128), 384)], CIN)
        part = dot(act, hot).astype(BF)
        if d == 0:
            act_slot[zh, mine, :] = part
            share_act(0)
        else:
            send_act[d] = part
            start(send_act.at[d], act_slot.at[zh, mine, :], s_col.at[1, d], r_col.at[1, d], at_z(d))

    def share_act(d):
        ref = act_slot.at[slot_of(d), mine, :]
        start(ref, ref, s_af.at[d], r_af.at[d], twin)

    subset(2)
    subset(1)

    for d in (1, 2, 3):
        arrived(first_b.at[(xi - d + NX) % NX], s_fb.at[d], r_fb.at[d])
    hot_b = one_hot_rows(rows_ref[0:240, 2:3], 256)
    block = dot(hot_b, first_b[...].reshape(256, 384)).astype(BF)
    for k in range(5):
        whole_b[pl.ds(place_b(yi), 48), k * 384 : (k + 1) * 384] = block[k * 48 : (k + 1) * 48]
    for rank in (0, 1):
        for way in (0, 1):
            ring_wb(0, way, way if rank == 0 else 1 - way)
    first_done(0, (2, 3))
    send_first(1)
    subset(3)
    subset(0)
    g_own = g_ref[...].reshape(32, 384)
    g_slot[zh] = g_own
    g_send[...] = g_own
    for d in (1, 2, 3):
        start(g_send, g_slot.at[zh], s_col.at[0, d], r_col.at[0, d], at_z(d))
    hot_a = one_hot_rows(rows_ref[0:400, 1:2], 512)
    first_done(0, (0, 1))
    first_done(1, range(4))
    block = dot(hot_a, first_a[...].reshape(512, 384)).astype(BF)
    for k in range(5):
        whole_a[pl.ds(place_a(xi), 80), k * 384 : (k + 1) * 384] = block[k * 80 : (k + 1) * 80]
    for rank in (0, 1):
        for way in (0, 1):
            ring_wa(0, way, way if rank == 0 else 1 - way)
    pass_on(ring_wb, ring_wb_done, 0, 3, 0)
    for d in (1, 3, 2):
        arrived(act_slot.at[slot_of(d), mine, :], s_col.at[1, d], r_col.at[1, d])
        share_act(d)
    pass_on(ring_wb, ring_wb_done, 0, 3, 1)

    def edges(slots, rows, prev, nxt, n):
        for w in range(2):
            lo = slots.at[0, pl.ds(w * rows, EDGE), :]
            hi = slots.at[3, pl.ds(w * rows + rows - EDGE, EDGE), :]
            start(hi, prev.at[w], s_edge.at[n, w], r_edge.at[n, w], at_col(1))
            start(lo, nxt.at[w], s_edge.at[n, 2 + w], r_edge.at[n, 2 + w], at_col(-1))

    def edges_done(prev, nxt, n):
        for w in range(2):
            arrived(prev.at[w], s_edge.at[n, w], r_edge.at[n, w])
            arrived(nxt.at[w], s_edge.at[n, 2 + w], r_edge.at[n, 2 + w])

    is_first = jnp.where(col == 0, 0.0, 1.0).astype(F32)
    is_last = jnp.where(col == 31, 0.0, 1.0).astype(F32)

    def lay(slots, rows, prev, nxt, where):
        tiles = where.shape[1]
        for w in range(2):
            for t in range(tiles):
                lanes = slice(t * 128, (t + 1) * 128)
                where[w, t, 0:EDGE, :] = prev[w, :, lanes].astype(F32) * is_first
                for z in range(NZ):
                    at = EDGE + z * rows
                    where[w, t, at : at + rows, :] = slots[z, w * rows : (w + 1) * rows, lanes].astype(F32)
                at = EDGE + NZ * rows
                where[w, t, at : at + EDGE, :] = nxt[w, :, lanes].astype(F32) * is_last

    def pooled_taps(where, rows):
        tiles = where.shape[1]
        parts = [[[where[w, t, pl.ds(EDGE + d, rows, stride=2), :] for t in range(tiles)] for w in range(2)]
                 for d in range(-2, 4)]
        out = []
        for k in range(5):
            wins = []
            for w in range(2):
                wins.append(jnp.concatenate(
                    [((parts[k][w][t] + parts[k + 1][w][t]) * 0.5).astype(BF) for t in range(tiles)], axis=1))
            out.append(jnp.concatenate(wins, axis=0))
        return out

    def shifted(where, rows):
        tiles = where.shape[1]
        return [
            jnp.concatenate([
                jnp.concatenate([where[w, t, EDGE + d : EDGE + d + rows, :].astype(BF) for t in range(tiles)], axis=1)
                for w in range(2)], axis=0)
            for d in (-1, 0, 1)
        ]

    def back_conv(before, here, after, weight, rows, where):
        none = jnp.zeros((2 * rows, WIDE - TAPS), BF)
        even = jnp.concatenate([after, here, here, before, before, none], axis=1)
        odd = jnp.concatenate([after, after, here, here, before, none], axis=1)
        total = dot_t(jnp.concatenate([even, odd], axis=0), weight[...]) * 0.5
        even, odd = total[0 : 2 * rows], total[2 * rows : 4 * rows]
        for w in range(2):
            for t in range(where.shape[1]):
                lanes = slice(t * 128, (t + 1) * 128)
                where[w, t, pl.ds(0, rows, stride=2), :] = even[w * rows : (w + 1) * rows, lanes]
                where[w, t, pl.ds(1, rows, stride=2), :] = odd[w * rows : (w + 1) * rows, lanes]

    pass_on(ring_wb, ring_wb_done, 1, 3, 0)
    pass_on(ring_wa, ring_wa_done, 0, 1, 0)
    for d in (1, 2, 3):
        arrived(g_slot.at[slot_of(d)], s_col.at[0, d], r_col.at[0, d])
    edges(g_slot, 16, g_prev, g_next, 0)
    pass_on(ring_wb, ring_wb_done, 1, 3, 1)
    for d in range(NZ):
        arrived(act_slot.at[slot_of(d), others, :], s_af.at[d], r_af.at[d])
    edges(act_slot, 64, act_prev, act_next, 1)
    pass_on(ring_wb, ring_wb_done, 2, 3, 0)
    edges_done(g_prev, g_next, 0)
    lay(g_slot, 16, g_prev, g_next, g_rows)
    edges_done(act_prev, act_next, 1)
    lay(act_slot, 64, act_prev, act_next, act_rows)
    for k, tap in enumerate(pooled_taps(act_rows, 128)):
        taps_a[k, :, 0:384] = tap
    pass_on(ring_wa, ring_wa_done, 0, 1, 1)
    for way in (0, 1):
        ring_wa_done(1, way, way)

    total = dot(taps_a[0], whole_a[:, 0:384])
    for k in range(1, 5):
        total += dot(taps_a[k], whole_a[:, k * 384 : (k + 1) * 384])
    for w in range(2):
        acc_a[w] = total[w * 128 : (w + 1) * 128]
    for z in range(NZ):
        for w in range(2):
            mid_send[z, w * 32 : (w + 1) * 32, :] = total[w * 128 + z * 32 : w * 128 + (z + 1) * 32].astype(BF)
    for d in (1, 2, 3):
        t = (zh + d) % NZ
        start(mid_send.at[t], mid_recv.at[zh], s_col.at[2, d], r_col.at[2, d], at_z(d))

    pass_on(ring_wb, ring_wb_done, 2, 3, 1)
    for way in (0, 1):
        ring_wb_done(3, way, way)
    before, here, after = shifted(g_rows, 64)
    back_conv(before, here, after, whole_b, 64, back_rows)
    def to_twin(where, per, send, recv, n):
        for z in range(NZ):
            for b in range(2):
                for w in range(2):
                    piece = where[w, b * 2 + 1 - core, z * per : (z + 1) * per, :]
                    send[z * 2 + b, w * per : (w + 1) * per, :] = piece.astype(BF)
        start(send, recv, s_tw.at[n], r_tw.at[n], twin)

    def from_twin(where, per, recv, send, n):
        arrived(recv, s_tw.at[n], r_tw.at[n])
        for z in range(NZ):
            for b in range(2):
                for w in range(2):
                    piece = where[w, b * 2 + core, z * per : (z + 1) * per, :]
                    rows = slice(w * per, (w + 1) * per)
                    send[z * 2 + b, rows, :] = (piece + recv[z * 2 + b, rows, :].astype(F32)).astype(BF)

    def scatter(src, dst, ssem, rsem):
        @pl.loop(1, 8)
        def _(d):
            tz, tb = (zh + d // 2) % NZ, (zl + d % 2) % 2
            pltpu.make_async_remote_copy(
                src_ref=src.at[tz * 2 + tb], dst_ref=dst.at[own8], send_sem=ssem.at[d], recv_sem=rsem.at[d],
                device_id=(col * NZ + tz, tb * 2 + core), device_id_type=MESH,
            ).start()

        dst[own8] = src[own8]

    def scattered(dst, ssem, rsem):
        @pl.loop(1, 8)
        def _(d):
            arrived(dst.at[((zh - d // 2 + NZ) % NZ) * 2 + (zl - d % 2 + 2) % 2], ssem.at[d], rsem.at[d])

    def scatter_sent(src, ssem, rsem):
        @pl.loop(1, 8)
        def _(d):
            pltpu.make_async_remote_copy(
                src_ref=src.at[0], dst_ref=src.at[0], send_sem=ssem.at[d], recv_sem=rsem.at[d],
                device_id=(seq, ch), device_id_type=MESH,
            ).wait_send()

    def to_row(v):
        wide = jnp.broadcast_to(v, (v.shape[0], 128))
        if v.shape[0] < 128:
            wide = jnp.concatenate([wide, jnp.zeros((128 - v.shape[0], 128), F32)], axis=0)
        return jnp.transpose(wide)[0:8]

    def to_column(v, rows):
        return jnp.transpose(jnp.concatenate([v] * 16, axis=0))[0:rows]

    def two_shares(recv):
        return jnp.concatenate(
            [recv[z * 2].astype(F32) + recv[z * 2 + 1].astype(F32) for z in range(NZ)], axis=1)

    to_twin(back_rows, 32, back_over, back_twin, 0)
    from_twin(back_rows, 32, back_twin, back_send, 0)
    scatter(back_send, back_recv, s_b, r_b)

    gain_b = jnp.concatenate([gain_b, jnp.zeros((1, 128), F32)], axis=1)
    hot = one_hot_lanes(lanes_ref[1:2, 0:512] + ch * 352, CMID + 128)
    gain_b_own = spread_gain(gain_b, hot)

    for d in (1, 2, 3):
        arrived(mid_recv.at[slot_of(d)], s_col.at[2, d], r_col.at[2, d])
    total = jnp.concatenate([acc_a[w, pl.ds(pl.multiple_of(zh * 32, 32), 32), :] for w in range(2)], axis=0)
    for d in (1, 2, 3):
        total += mid_recv[slot_of(d)].astype(F32)
    mid = (total + bias_pad[0:1, :]).astype(BF)
    mid_f = mid.astype(F32)
    squares = jnp.sum(mid_f * mid_f, axis=-1, keepdims=True)
    mid_wide = jnp.concatenate([mid, jnp.zeros((64, 128), BF)], axis=1)
    mid_own = dot(mid_wide, one_hot_lanes(lanes_ref[1:2, 0:512], 512))
    lane = lax.broadcasted_iota(jnp.int32, (64, 128), 1)
    high, middle, low = three_parts(squares)
    for z in range(NZ):
        piece = mid_own[:, z * 128 : (z + 1) * 128]
        piece = jnp.where(lane == 96, high, jnp.where(lane == 97, middle, jnp.where(lane == 98, low, piece)))
        x_send[z] = piece.astype(BF)
    for d in (1, 2, 3):
        start(x_send.at[zh], x_recv.at[own], s_x.at[d], r_x.at[d], at_c(d))
    x_recv[own] = x_send[zh]
    far = [(dz, db) for dz in (2, 1, 3) for db in (0, 1)]
    for n, (dz, db) in enumerate(far):
        tz, tb = (zh + dz) % NZ, (zl + db) % 2
        start(x_send.at[tz], x_recv.at[own], s_x.at[4 + n], r_x.at[4 + n], (col * NZ + tz, tb * 2 + core))

    def x_slot(dz, db, side):
        return x_recv.at[slot_of(dz) * NC + ((zl - db + 2) % 2) * 2 + side]

    hot = one_hot_lanes(lanes_ref[2:3, 0:512] + zh * 11, CMID + 128)
    gain_b_all = spread_gain(gain_b, hot)

    hot = one_hot_rows(rows_ref[:, 0:1], 512)
    for k in range(4):
        turned_a[:, k * 512 : (k + 1) * 512] = dot(hot, whole_a[:, k * 512 : (k + 1) * 512]).astype(BF)

    def inverse(z):
        total = jnp.zeros((64, 1), F32)
        for c in range(NC):
            part = x_recv[z * NC + c, :, 96:99].astype(F32)
            total += jnp.sum(part, axis=-1, keepdims=True)
        return lax.rsqrt(total * (1.0 / CMID) + EPS)

    for d in (1, 2, 3):
        arrived(x_recv.at[zh * NC + (ch - d + NC) % NC], s_x.at[d], r_x.at[d])
    inv_b = inverse(zh)
    normed_b = mid_own * inv_b
    factor_b = gelu_slope(normed_b * gain_b_own) * gain_b_own
    scattered(back_recv, s_b, r_b)
    grad_n = two_shares(back_recv) * factor_b
    in_send[...] = to_row(jnp.sum(grad_n * normed_b, axis=-1, keepdims=True))
    for d in (1, 2, 3):
        start(in_send, in_recv.at[ch], s_col.at[3, d], r_col.at[3, d], at_c(d))

    for n, (dz, db) in enumerate(far):
        arrived(x_slot(dz, db, core), s_x.at[4 + n], r_x.at[4 + n])
        start(x_slot(dz, db, core), x_slot(dz, db, core), s_x.at[10 + n], r_x.at[10 + n], twin)
    inner = in_send[...]
    for d in (1, 2, 3):
        at = (ch - d + NC) % NC
        arrived(in_recv.at[at], s_col.at[3, d], r_col.at[3, d])
        inner += in_recv[at]
    inner = jnp.concatenate([to_column(inner * (1.0 / CMID), 64)] * 4, axis=1)
    grad_mid = (inv_b * (grad_n - normed_b * inner)).astype(BF)
    gm_slot[zh] = dot(grad_mid, one_hot_rows(rows_ref[:, 3:4], 384)).astype(BF)
    for d in (1, 2, 3):
        start(gm_slot.at[zh], gm_slot.at[zh], s_col.at[4, d], r_col.at[4, d], at_z(d))

    def last_rows(z, w):
        return pltpu.make_async_remote_copy(
            src_ref=gm_slot.at[3, pl.ds(w * 32 + 16, EDGE), :], dst_ref=gm_prev.at[w], send_sem=s_gm.at[0, z, w],
            recv_sem=s_edge_gm.at[0, w], device_id=beside(1, z), device_id_type=MESH)

    def first_rows(z, w):
        return pltpu.make_async_remote_copy(
            src_ref=gm_slot.at[0, pl.ds(w * 32, EDGE), :], dst_ref=gm_next.at[w], send_sem=s_gm.at[1, z, w],
            recv_sem=s_edge_gm.at[1, w], device_id=beside(-1, z), device_id_type=MESH)

    @pl.when(zh == NZ - 1)
    def _():
        for z in range(NZ):
            for w in range(2):
                last_rows(z, w).start()

    @pl.when(zh == 0)
    def _():
        for z in range(NZ):
            for w in range(2):
                first_rows(z, w).start()

    hot = one_hot_lanes(lanes_ref[3:4, 0:512] + ch * 320, CIN)
    gain_a_own = spread_gain(gain_a, hot)
    feat_bf = feat_ref[...].reshape(128, CIN)
    inv_a = inverse_a(feat_bf.astype(F32))
    feat_own = dot(feat_bf, hot)
    normed_a = feat_own * inv_a
    factor_a = gelu_slope(normed_a * gain_a_own) * gain_a_own

    for n, (dz, db) in enumerate(far):
        arrived(x_slot(dz, db, 1 - core), s_x.at[10 + n], r_x.at[10 + n])
    for z in range(NZ):
        inv = inverse(z)
        values = jnp.concatenate([x_recv[z * NC + c].astype(F32) for c in range(NC)], axis=1)
        b_slot[z] = gelu_tanh(values * inv * gain_b_all).astype(BF)
    edges(b_slot, 32, b_prev, b_next, 2)

    for d in (1, 2, 3):
        arrived(gm_slot.at[slot_of(d)], s_col.at[4, d], r_col.at[4, d])

    for w in range(2):
        arrived(gm_prev.at[w], s_gm.at[0, 0, w], s_edge_gm.at[0, w])
        arrived(gm_next.at[w], s_gm.at[1, 0, w], s_edge_gm.at[1, w])
    lay(gm_slot, 32, gm_prev, gm_next, gm_rows)
    before, here, after = shifted(gm_rows, 128)
    back_conv(before, here, after, turned_a, 128, out_rows)
    to_twin(out_rows, 64, out_over, out_twin, 1)
    edges_done(b_prev, b_next, 2)
    lay(b_slot, 32, b_prev, b_next, b_rows)
    taps = pooled_taps(b_rows, 64)
    total = dot(taps[0], whole_b[:, 0:384])
    for k in range(1, 5):
        total += dot(taps[k], whole_b[:, k * 384 : (k + 1) * 384])
    for w in range(2):
        acc_b[w] = total[w * 64 : (w + 1) * 64]
    for z in range(NZ):
        for w in range(2):
            pool_send[z, w * 16 : (w + 1) * 16, :] = total[w * 64 + z * 16 : w * 64 + (z + 1) * 16].astype(BF)

    from_twin(out_rows, 64, out_twin, out_send, 1)
    scatter(out_send, out_recv, s_o, r_o)

    for d in (1, 2, 3):
        t = (zh + d) % NZ
        start(pool_send.at[t], pool_recv.at[zh], s_col.at[5, d], r_col.at[5, d], at_z(d))

    for d in (1, 2, 3):
        arrived(pool_recv.at[slot_of(d)], s_col.at[5, d], r_col.at[5, d])
    total = jnp.concatenate([acc_b[w, pl.ds(pl.multiple_of(zh * 16, 16), 16), :] for w in range(2)], axis=0)
    for d in (1, 2, 3):
        total += pool_recv[slot_of(d)].astype(F32)
    pooled_ref[...] = (total + bias_b_ref[...].reshape(1, 384)).astype(BF).reshape(2, 16, 384)

    scattered(out_recv, s_o, r_o)
    grad_n = two_shares(out_recv) * factor_a
    ia_send[...] = to_row(jnp.sum(grad_n * normed_a, axis=-1, keepdims=True))
    for d in (1, 2, 3):
        start(ia_send, ia_recv.at[ch], s_col.at[6, d], r_col.at[6, d], at_c(d))
    hot = one_hot_rows(rows_ref[:, 4:5], 384)
    inner = ia_send[...]
    for d in (1, 2, 3):
        at = (ch - d + NC) % NC
        arrived(ia_recv.at[at], s_col.at[6, d], r_col.at[6, d])
        inner += ia_recv[at]
    inner = jnp.concatenate([to_column(inner * (1.0 / CIN), 128)] * 4, axis=1)
    grad = (inv_a * (grad_n - normed_a * inner)).astype(BF)
    grad_ref[...] = dot(grad, hot)[:, 0:320].astype(BF).reshape(2, 64, 320)

    for copy in pending:
        copy.wait_send()
    scatter_sent(back_send, s_b, r_b)
    scatter_sent(out_send, s_o, r_o)

    @pl.when(zh == NZ - 1)
    def _():
        for z in range(NZ):
            for w in range(2):
                last_rows(z, w).wait_send()

    @pl.when(zh == 0)
    def _():
        for z in range(NZ):
            for w in range(2):
                first_rows(z, w).wait_send()


def per_device(dna_features, gain_a, conv_a, bias_a, gain_b, conv_b, bias_b, grad_out):
    lanes, rows = index_tables()
    dma = pltpu.SemaphoreType.DMA
    vmem = pltpu.VMEM
    pooled, grad = pl.pallas_call(
        kernel,
        out_shape=(jax.ShapeDtypeStruct((2, 16, 384), BF), jax.ShapeDtypeStruct((2, 64, 320), BF)),
        in_specs=[pl.BlockSpec(memory_space=pl.ANY)] * 10,
        out_specs=[pl.BlockSpec(memory_space=vmem)] * 2,
        scratch_shapes=[
            vmem((2, 64, CIN), BF), vmem((5, 10, 352), BF), vmem((5, 11, 384), BF), vmem((CIN,), F32), vmem((352,), F32),
            vmem((CMID,), F32), vmem((384,), F32), vmem((2, 16, 384), BF), vmem((8, 1536), jnp.int32), vmem((512, 8), jnp.int32),
            vmem((8, 64, 384), BF), vmem((4, 64, 384), BF), vmem((512, WIDE), BF), vmem((512, WIDE), BF),
            vmem((512, WIDE), BF), vmem((8, 384), F32),
            vmem((4, 128, 384), BF), vmem((2, 16, 384), BF), vmem((2, 16, 384), BF), vmem((2, 3, 288, 128), F32),
            vmem((5, 256, 512), BF), vmem((4, 64, 384), BF),
            vmem((4, 32, 384), BF), vmem((32, 384), BF), vmem((2, 16, 384), BF), vmem((2, 16, 384), BF), vmem((2, 3, 96, 128), F32),
            vmem((2, 4, 128, 128), F32), vmem((8, 64, 128), BF), vmem((8, 64, 128), BF), vmem((8, 64, 128), BF),
            vmem((8, 64, 128), BF), vmem((2, 128, 384), F32), vmem((4, 64, 384), BF), vmem((4, 64, 384), BF),
            vmem((4, 64, 128), BF), vmem((16, 64, 128), BF), vmem((4, 64, 512), BF), vmem((2, 16, 512), BF),
            vmem((2, 16, 512), BF), vmem((2, 4, 160, 128), F32),
            vmem((4, 32, 384), BF), vmem((4, 32, 384), BF), vmem((2, 64, 384), F32),
            vmem((8, 128), F32), vmem((4, 8, 128), F32), vmem((4, 64, 384), BF), vmem((2, 16, 384), BF),
            vmem((2, 16, 384), BF), vmem((2, 3, 160, 128), F32),
            vmem((2, 4, 256, 128), F32), vmem((8, 128, 128), BF), vmem((8, 128, 128), BF), vmem((8, 128, 128), BF),
            vmem((8, 128, 128), BF),
            vmem((8, 128), F32), vmem((4, 8, 128), F32),
            dma((2, 4)), dma((2, 4)), dma((4,)), dma((4,)), dma((2, 4, 2)), dma((2, 4, 2)), dma((2, 2, 2)), dma((2, 2, 2)),
            dma((7, 4)), dma((7, 4)), dma((4, 4)), dma((4, 4)),
            dma((16,)), dma((16,)), dma((16,)), dma((16,)), dma((16,)), dma((16,)), dma((10,)), dma((2, 4, 2)), dma((2, 2)), dma((4,)), dma((4,)),
            dma((2,)), dma((2,)),
        ],
        compiler_params=pltpu.CompilerParams(
            collective_id=0, has_side_effects=True, vmem_limit_bytes=60 * 1024 * 1024
        ),
        cost_estimate=pl.CostEstimate(flops=3_000_000_000, bytes_accessed=8_000_000, transcendentals=800_000),
    )(
        dna_features, conv_a, conv_b, gain_a, bias_a, gain_b, bias_b, grad_out, jnp.asarray(lanes), jnp.asarray(rows),
    )
    return pooled, grad


def solution(mesh):
    return jax.shard_map(
        per_device,
        mesh=mesh,
        in_specs=(
            P(None, "seq", None), P(), P(None, "seq", "ch"), P("ch"), P(), P(None, "seq", "ch"), P("ch"),
            P(None, "seq", "ch"),
        ),
        out_specs=(P(None, "seq", "ch"), P(None, "seq", "ch")),
        check_vma=False,
    )
```

```python
import math

import jax
import jax.numpy as jnp
import numpy as np
from jax import lax
from jax.experimental import pallas as pl
from jax.experimental.pallas import tpu as pltpu
from jax.sharding import PartitionSpec as P

EPS = 1e-06
ROOT = math.sqrt(2.0 / math.pi)
MESH = pl.DeviceIdType.MESH
BF = jnp.bfloat16
F32 = jnp.float32
NY, NX, NZ, NC = 8, 4, 4, 4
CIN, CMID = 1280, 1408
EDGE = 16
WIDE = 2048
TAPS = 5 * 384


def gelu_tanh(z):
    return 0.5 * z * (1.0 + jnp.tanh(ROOT * (z + 0.044715 * z * z * z)))


def gelu_slope(z):
    t = jnp.tanh(ROOT * (z + 0.044715 * z * z * z))
    return 0.5 * (1.0 + t) + 0.5 * z * (1.0 - t * t) * ROOT * (1.0 + 3.0 * 0.044715 * z * z)


def index_tables():
    lanes = np.full((8, 1536), -100000, np.int32)
    rows = np.full((512, 8), -100000, np.int32)
    for zb in range(NZ):
        for xb in range(NX):
            for yb in range(NY):
                for i in range(10):
                    lanes[0, zb * 384 + xb * 80 + yb * 10 + i] = ((yb * 4 + xb) * 4 + zb) * 10 + i
            for yy in range(2):
                for i in range(11):
                    q = yy * 48 + xb * 11 + i
                    here = ((yy * 4 + xb) * 4 + zb) * 11 + i
                    lanes[1, zb * 128 + q] = here
                    rows[zb * 128 + q, 3] = here
                for i in range(10):
                    q = xb * 20 + yy * 10 + i
                    here = ((yy * 4 + xb) * 4 + zb) * 10 + i
                    lanes[3, zb * 128 + q] = here
                    rows[zb * 128 + q, 4] = here
    for cb in range(NC):
        for xb in range(NX):
            for yy in range(2):
                for i in range(11):
                    lanes[2, cb * 128 + yy * 48 + xb * 11 + i] = (((cb * 2 + yy) * 4 + xb) * 4) * 11 + i
                for i in range(10):
                    rows[cb * 128 + xb * 20 + yy * 10 + i, 0] = xb * 80 + (cb * 2 + yy) * 10 + i
    for k in range(5):
        for yb in range(NY):
            for i in range(10):
                rows[k * 80 + yb * 10 + i, 1] = yb * 64 + k * 10 + i
        for xb in range(NX):
            for i in range(11):
                rows[k * 48 + xb * 11 + i, 2] = xb * 64 + k * 11 + i
    return lanes, rows


def dot(a, b):
    return lax.dot_general(a, b, (((1,), (0,)), ((), ())), preferred_element_type=F32)


def dot_t(a, b):
    return lax.dot_general(a, b, (((1,), (1,)), ((), ())), preferred_element_type=F32)


def one_hot_lanes(table, depth):
    row = lax.broadcasted_iota(jnp.int32, (depth, table.shape[1]), 0)
    return jnp.where(row == table, 1.0, 0.0).astype(BF)


def one_hot_rows(table, depth):
    col = lax.broadcasted_iota(jnp.int32, (table.shape[0], depth), 1)
    return jnp.where(col == table, 1.0, 0.0).astype(BF)


def three_parts(v):
    high = v.astype(BF).astype(F32)
    rest = v - high
    middle = rest.astype(BF).astype(F32)
    return high, middle, rest - middle


def spread_gain(gain, hot):
    high, middle, low = three_parts(gain)
    row = lax.broadcasted_iota(jnp.int32, (16, gain.shape[1]), 0)
    stack = jnp.where(row == 0, high, jnp.where(row == 1, middle, jnp.where(row == 2, low, 0.0)))
    return jnp.sum(dot(stack.astype(BF), hot), axis=0, keepdims=True)


def kernel(
    feat_in, wa_in, wb_in, gain_a_in, bias_a_in, gain_b_in, bias_b_in, g_in, lanes_in, rows_in,
    pooled_ref, grad_ref,
    feat_ref, wa_ref, wb_ref, gain_a_ref, bias_a_ref, gain_b_ref, bias_b_ref, g_ref, lanes_ref, rows_ref,
    first_a, first_b, whole_a, turned_a, whole_b, bias_pad,
    act_slot, act_prev, act_next, act_rows, taps_a, send_act,
    g_slot, g_send, g_prev, g_next, g_rows,
    back_rows, back_over, back_twin, back_send, back_recv,
    acc_a, mid_send, mid_recv,
    x_send, x_recv, b_slot, b_prev, b_next, b_rows,
    pool_send, pool_recv, acc_b,
    in_send, in_recv, gm_slot, gm_prev, gm_next, gm_rows,
    out_rows, out_over, out_twin, out_send, out_recv, ia_send, ia_recv,
    s_fa, r_fa, s_fb, r_fb, s_wb, r_wb, s_wa, r_wa, s_col, r_col, s_edge, r_edge,
    s_b, r_b, s_x, r_x, s_o, r_o, s_in, s_gm, s_edge_gm, s_af, r_af, s_tw, r_tw,
):
    seq = lax.axis_index("seq")
    ch = lax.axis_index("ch")
    zh = seq % NZ
    col = seq // NZ
    xi = col % NX
    yi = col // NX
    own = zh * NC + ch
    core = ch % 2
    zl = ch // 2
    twin = (seq, ch + 1 - 2 * core)
    own8 = zh * 2 + zl
    pending = []
    loads = [
        pltpu.make_async_copy(src, dst, s_in.at[i])
        for i, (src, dst) in enumerate((
            (wa_in, wa_ref), (wb_in, wb_ref), (rows_in, rows_ref), (lanes_in, lanes_ref), (feat_in, feat_ref),
            (gain_a_in, gain_a_ref), (g_in, g_ref), (bias_a_in, bias_a_ref), (gain_b_in, gain_b_ref),
            (bias_b_in, bias_b_ref),
        ))
    ]
    for load in loads:
        load.start()

    def start(src, dst, ssem, rsem, dev):
        copy = pltpu.make_async_remote_copy(
            src_ref=src, dst_ref=dst, send_sem=ssem, recv_sem=rsem, device_id=dev, device_id_type=MESH
        )
        copy.start()
        pending.append(copy)

    def arrived(dst, ssem, rsem):
        pltpu.make_async_remote_copy(
            src_ref=dst, dst_ref=dst, send_sem=ssem, recv_sem=rsem, device_id=(seq, ch), device_id_type=MESH
        ).wait_recv()

    def at_y(d):
        return ((((yi + d + NY) % NY) * NX + xi) * NZ + zh, ch)

    def at_x(d):
        return ((yi * NX + (xi + d + NX) % NX) * NZ + zh, ch)

    def at_z(d):
        return (col * NZ + (zh + d) % NZ, ch)

    def at_c(d):
        return (seq, (ch + d) % NC)

    def at_col(d):
        return (((col + d + 32) % 32) * NZ + zh, ch)

    def member(d):
        tz, tc = (zh + d // NC) % NZ, (ch + d % NC) % NC
        return tz * NC + tc, (col * NZ + tz, tc)

    def source(d):
        return ((zh - d // NC + NZ) % NZ) * NC + (ch - d % NC + NC) % NC

    def beside(way, z):
        return (((col + way + 32) % 32) * NZ + z, ch)

    barrier = pltpu.get_barrier_semaphore()

    def greet(dev):
        pl.semaphore_signal(barrier, inc=1, device_id=dev, device_id_type=MESH)

    for d in (1, 2, 3):
        greet(at_x(d))
    for d in (-1, 1):
        greet(at_y(d))
        greet(at_y(2 * d))
        for z in range(NZ):
            greet(beside(d, z))

    @pl.loop(1, 16)
    def _(d):
        greet(member(d)[1])

    for load in loads:
        load.wait()
    gain_a = gain_a_ref[...].reshape(1, CIN)
    gain_b = gain_b_ref[...].reshape(1, CMID)

    first_a[yi] = jnp.zeros((64, 384), BF)
    bias_pad[...] = jnp.zeros((8, 384), F32)
    bias_pad[0:1, 0:352] = bias_a_ref[...].reshape(1, 352)
    pack_a = jnp.zeros((64, 352), F32)
    pack_b = jnp.zeros((64, 384), F32)
    for k in range(5):
        pick = lax.broadcasted_iota(jnp.int32, (64, 10), 0) == lax.broadcasted_iota(jnp.int32, (64, 10), 1) + 10 * k
        pack_a += dot(jnp.where(pick, 1.0, 0.0).astype(BF), wa_ref[k])
        pick = lax.broadcasted_iota(jnp.int32, (64, 11), 0) == lax.broadcasted_iota(jnp.int32, (64, 11), 1) + 11 * k
        pack_b += dot(jnp.where(pick, 1.0, 0.0).astype(BF), wb_ref[k])
    first_a[yi, :, 0:352] = pack_a.astype(BF)
    first_b[xi] = pack_b.astype(BF)
    whole_a[320:512, :] = jnp.zeros((192, WIDE), BF)
    whole_a[0:320, TAPS:WIDE] = jnp.zeros((320, WIDE - TAPS), BF)
    whole_b[:, TAPS:WIDE] = jnp.zeros((512, WIDE - TAPS), BF)
    for c in range(NC):
        whole_b[c * 128 + 96 : c * 128 + 128, 0:TAPS] = jnp.zeros((32, TAPS), BF)
    taps_a[:, :, 384:512] = jnp.zeros((5, 256, 128), BF)
    pl.semaphore_wait(barrier, 30)

    parts = ((0, 1152), (1152, 768))

    def first_block(d, at=0, n=64):
        return first_a.at[(yi + d + NY) % NY, pl.ds(at, n), :]

    hops = (
        ((0, 1, 0, 64), (0, -1, 0, 64), (0, 2, 0, 64), (0, -2, 0, 64)),
        ((-2, 1, 0, 64), (2, -1, 0, 64), (-2, 2, 0, 32), (2, -2, 32, 32)),
    )

    def send_first(step):
        for n, (b, to, at, rows) in enumerate(hops[step]):
            ref = first_block(b, at, rows)
            start(ref, ref, s_fa.at[step, n], r_fa.at[step, n], at_y(to))

    def first_done(step, which):
        for n in which:
            b, to, at, rows = hops[step][n]
            arrived(first_block(b - to, at, rows), s_fa.at[step, n], r_fa.at[step, n])

    def place_a(b):
        return pl.multiple_of(b * 80, 16)

    def place_b(b):
        return pl.multiple_of((b // 2) * 128 + (b % 2) * 48, 16)

    def ring_wb(r, way, c):
        sign = 1 if way == 0 else -1
        ref = whole_b.at[pl.ds(place_b((yi - sign * r + NY) % NY), 48), pl.ds(*parts[c])]
        start(ref, ref, s_wb.at[way, r, c], r_wb.at[way, r, c], at_y(sign))

    def ring_wb_done(r, way, c):
        sign = 1 if way == 0 else -1
        ref = whole_b.at[pl.ds(place_b((yi - sign * (r + 1) + NY) % NY), 48), pl.ds(*parts[c])]
        arrived(ref, s_wb.at[way, r, c], r_wb.at[way, r, c])

    def ring_wa(r, way, c):
        sign = 1 if way == 0 else -1
        ref = whole_a.at[pl.ds(place_a((xi - sign * r + NX) % NX), 80), pl.ds(*parts[c])]
        start(ref, ref, s_wa.at[way, r, c], r_wa.at[way, r, c], at_x(sign))

    def ring_wa_done(r, way, c):
        sign = 1 if way == 0 else -1
        ref = whole_a.at[pl.ds(place_a((xi - sign * (r + 1) + NX) % NX), 80), pl.ds(*parts[c])]
        arrived(ref, s_wa.at[way, r, c], r_wa.at[way, r, c])

    def pass_on(ring, done, r, last, rank):
        for way in (0, 1):
            c = way if rank == 0 else 1 - way
            done(r, way, c)
            if r + 1 < last or (r + 1 == last and rank == 0):
                ring(r + 1, way, c)

    send_first(0)
    for d in (1, 2, 3):
        start(first_b.at[xi], first_b.at[xi], s_fb.at[d], r_fb.at[d], at_x(d))

    def slot_of(d):
        return (zh - d + NZ) % NZ

    def inverse_a(v):
        return lax.rsqrt(jnp.sum(v * v, axis=-1, keepdims=True) * (1.0 / CIN) + EPS)

    feat = feat_ref[core].astype(F32)
    act = gelu_tanh(feat * inverse_a(feat) * gain_a).astype(BF)
    mine = pl.ds(pl.multiple_of(core * 64, 64), 64)
    others = pl.ds(pl.multiple_of(64 - core * 64, 64), 64)

    def subset(d):
        t = (zh + d) % NZ
        hot = one_hot_lanes(lanes_ref[0:1, pl.ds(pl.multiple_of(t * 384, 128), 384)], CIN)
        part = dot(act, hot).astype(BF)
        if d == 0:
            act_slot[zh, mine, :] = part
            share_act(0)
        else:
            send_act[d] = part
            start(send_act.at[d], act_slot.at[zh, mine, :], s_col.at[1, d], r_col.at[1, d], at_z(d))

    def share_act(d):
        ref = act_slot.at[slot_of(d), mine, :]
        start(ref, ref, s_af.at[d], r_af.at[d], twin)

    subset(2)
    subset(1)

    for d in (1, 2, 3):
        arrived(first_b.at[(xi - d + NX) % NX], s_fb.at[d], r_fb.at[d])
    hot_b = one_hot_rows(rows_ref[0:240, 2:3], 256)
    block = dot(hot_b, first_b[...].reshape(256, 384)).astype(BF)
    for k in range(5):
        whole_b[pl.ds(place_b(yi), 48), k * 384 : (k + 1) * 384] = block[k * 48 : (k + 1) * 48]
    for rank in (0, 1):
        for way in (0, 1):
            ring_wb(0, way, way if rank == 0 else 1 - way)
    first_done(0, (2, 3))
    send_first(1)
    subset(3)
    subset(0)
    g_own = g_ref[...].reshape(32, 384)
    g_slot[zh] = g_own
    g_send[...] = g_own
    for d in (1, 2, 3):
        start(g_send, g_slot.at[zh], s_col.at[0, d], r_col.at[0, d], at_z(d))
    pass_on(ring_wb, ring_wb_done, 0, 3, 0)
    hot_a = one_hot_rows(rows_ref[0:400, 1:2], 512)
    first_done(0, (0, 1))
    first_done(1, range(4))
    block = dot(hot_a, first_a[...].reshape(512, 384)).astype(BF)
    for k in range(5):
        whole_a[pl.ds(place_a(xi), 80), k * 384 : (k + 1) * 384] = block[k * 80 : (k + 1) * 80]
    for rank in (0, 1):
        for way in (0, 1):
            ring_wa(0, way, way if rank == 0 else 1 - way)
    for d in (1, 3, 2):
        arrived(act_slot.at[slot_of(d), mine, :], s_col.at[1, d], r_col.at[1, d])
        share_act(d)
    pass_on(ring_wb, ring_wb_done, 0, 3, 1)

    def edges(slots, rows, prev, nxt, n):
        for w in range(2):
            lo = slots.at[0, pl.ds(w * rows, EDGE), :]
            hi = slots.at[3, pl.ds(w * rows + rows - EDGE, EDGE), :]
            start(hi, prev.at[w], s_edge.at[n, w], r_edge.at[n, w], at_col(1))
            start(lo, nxt.at[w], s_edge.at[n, 2 + w], r_edge.at[n, 2 + w], at_col(-1))

    def edges_done(prev, nxt, n):
        for w in range(2):
            arrived(prev.at[w], s_edge.at[n, w], r_edge.at[n, w])
            arrived(nxt.at[w], s_edge.at[n, 2 + w], r_edge.at[n, 2 + w])

    is_first = jnp.where(col == 0, 0.0, 1.0).astype(F32)
    is_last = jnp.where(col == 31, 0.0, 1.0).astype(F32)

    def lay(slots, rows, prev, nxt, where):
        tiles = where.shape[1]
        for w in range(2):
            for t in range(tiles):
                lanes = slice(t * 128, (t + 1) * 128)
                where[w, t, 0:EDGE, :] = prev[w, :, lanes].astype(F32) * is_first
                for z in range(NZ):
                    at = EDGE + z * rows
                    where[w, t, at : at + rows, :] = slots[z, w * rows : (w + 1) * rows, lanes].astype(F32)
                at = EDGE + NZ * rows
                where[w, t, at : at + EDGE, :] = nxt[w, :, lanes].astype(F32) * is_last

    def pooled_taps(where, rows):
        tiles = where.shape[1]
        parts = [[[where[w, t, pl.ds(EDGE + d, rows, stride=2), :] for t in range(tiles)] for w in range(2)]
                 for d in range(-2, 4)]
        out = []
        for k in range(5):
            wins = []
            for w in range(2):
                wins.append(jnp.concatenate(
                    [((parts[k][w][t] + parts[k + 1][w][t]) * 0.5).astype(BF) for t in range(tiles)], axis=1))
            out.append(jnp.concatenate(wins, axis=0))
        return out

    def shifted(where, rows):
        tiles = where.shape[1]
        return [
            jnp.concatenate([
                jnp.concatenate([where[w, t, EDGE + d : EDGE + d + rows, :].astype(BF) for t in range(tiles)], axis=1)
                for w in range(2)], axis=0)
            for d in (-1, 0, 1)
        ]

    def back_conv(before, here, after, weight, rows, where):
        none = jnp.zeros((2 * rows, WIDE - TAPS), BF)
        even = jnp.concatenate([after, here, here, before, before, none], axis=1)
        odd = jnp.concatenate([after, after, here, here, before, none], axis=1)
        total = dot_t(jnp.concatenate([even, odd], axis=0), weight[...]) * 0.5
        even, odd = total[0 : 2 * rows], total[2 * rows : 4 * rows]
        for w in range(2):
            for t in range(where.shape[1]):
                lanes = slice(t * 128, (t + 1) * 128)
                where[w, t, pl.ds(0, rows, stride=2), :] = even[w * rows : (w + 1) * rows, lanes]
                where[w, t, pl.ds(1, rows, stride=2), :] = odd[w * rows : (w + 1) * rows, lanes]

    pass_on(ring_wb, ring_wb_done, 1, 3, 0)
    pass_on(ring_wa, ring_wa_done, 0, 1, 0)
    for d in (1, 2, 3):
        arrived(g_slot.at[slot_of(d)], s_col.at[0, d], r_col.at[0, d])
    edges(g_slot, 16, g_prev, g_next, 0)
    pass_on(ring_wb, ring_wb_done, 1, 3, 1)
    for d in range(NZ):
        arrived(act_slot.at[slot_of(d), others, :], s_af.at[d], r_af.at[d])
    edges(act_slot, 64, act_prev, act_next, 1)
    pass_on(ring_wb, ring_wb_done, 2, 3, 0)
    edges_done(g_prev, g_next, 0)
    lay(g_slot, 16, g_prev, g_next, g_rows)
    edges_done(act_prev, act_next, 1)
    lay(act_slot, 64, act_prev, act_next, act_rows)
    for k, tap in enumerate(pooled_taps(act_rows, 128)):
        taps_a[k, :, 0:384] = tap
    pass_on(ring_wa, ring_wa_done, 0, 1, 1)
    for way in (0, 1):
        ring_wa_done(1, way, way)

    total = dot(taps_a[0], whole_a[:, 0:384])
    for k in range(1, 5):
        total += dot(taps_a[k], whole_a[:, k * 384 : (k + 1) * 384])
    for w in range(2):
        acc_a[w] = total[w * 128 : (w + 1) * 128]
    for z in range(NZ):
        for w in range(2):
            mid_send[z, w * 32 : (w + 1) * 32, :] = total[w * 128 + z * 32 : w * 128 + (z + 1) * 32].astype(BF)
    for d in (1, 2, 3):
        t = (zh + d) % NZ
        start(mid_send.at[t], mid_recv.at[zh], s_col.at[2, d], r_col.at[2, d], at_z(d))

    pass_on(ring_wb, ring_wb_done, 2, 3, 1)
    for way in (0, 1):
        ring_wb_done(3, way, way)
    before, here, after = shifted(g_rows, 64)
    back_conv(before, here, after, whole_b, 64, back_rows)
    def to_twin(where, per, send, recv, n):
        for z in range(NZ):
            for b in range(2):
                for w in range(2):
                    piece = where[w, b * 2 + 1 - core, z * per : (z + 1) * per, :]
                    send[z * 2 + b, w * per : (w + 1) * per, :] = piece.astype(BF)
        start(send, recv, s_tw.at[n], r_tw.at[n], twin)

    def from_twin(where, per, recv, send, n):
        arrived(recv, s_tw.at[n], r_tw.at[n])
        for z in range(NZ):
            for b in range(2):
                for w in range(2):
                    piece = where[w, b * 2 + core, z * per : (z + 1) * per, :]
                    rows = slice(w * per, (w + 1) * per)
                    send[z * 2 + b, rows, :] = (piece + recv[z * 2 + b, rows, :].astype(F32)).astype(BF)

    def scatter(src, dst, ssem, rsem):
        @pl.loop(1, 8)
        def _(d):
            tz, tb = (zh + d // 2) % NZ, (zl + d % 2) % 2
            pltpu.make_async_remote_copy(
                src_ref=src.at[tz * 2 + tb], dst_ref=dst.at[own8], send_sem=ssem.at[d], recv_sem=rsem.at[d],
                device_id=(col * NZ + tz, tb * 2 + core), device_id_type=MESH,
            ).start()

        dst[own8] = src[own8]

    def scattered(dst, ssem, rsem):
        @pl.loop(1, 8)
        def _(d):
            arrived(dst.at[((zh - d // 2 + NZ) % NZ) * 2 + (zl - d % 2 + 2) % 2], ssem.at[d], rsem.at[d])

    def scatter_sent(src, ssem, rsem):
        @pl.loop(1, 8)
        def _(d):
            pltpu.make_async_remote_copy(
                src_ref=src.at[0], dst_ref=src.at[0], send_sem=ssem.at[d], recv_sem=rsem.at[d],
                device_id=(seq, ch), device_id_type=MESH,
            ).wait_send()

    def to_row(v):
        wide = jnp.broadcast_to(v, (v.shape[0], 128))
        if v.shape[0] < 128:
            wide = jnp.concatenate([wide, jnp.zeros((128 - v.shape[0], 128), F32)], axis=0)
        return jnp.transpose(wide)[0:8]

    def to_column(v, rows):
        return jnp.transpose(jnp.concatenate([v] * 16, axis=0))[0:rows]

    def two_shares(recv):
        return jnp.concatenate(
            [recv[z * 2].astype(F32) + recv[z * 2 + 1].astype(F32) for z in range(NZ)], axis=1)

    to_twin(back_rows, 32, back_over, back_twin, 0)
    from_twin(back_rows, 32, back_twin, back_send, 0)
    scatter(back_send, back_recv, s_b, r_b)

    gain_b = jnp.concatenate([gain_b, jnp.zeros((1, 128), F32)], axis=1)
    hot = one_hot_lanes(lanes_ref[1:2, 0:512] + ch * 352, CMID + 128)
    gain_b_own = spread_gain(gain_b, hot)

    for d in (1, 2, 3):
        arrived(mid_recv.at[slot_of(d)], s_col.at[2, d], r_col.at[2, d])
    total = jnp.concatenate([acc_a[w, pl.ds(pl.multiple_of(zh * 32, 32), 32), :] for w in range(2)], axis=0)
    for d in (1, 2, 3):
        total += mid_recv[slot_of(d)].astype(F32)
    mid = (total + bias_pad[0:1, :]).astype(BF)
    mid_f = mid.astype(F32)
    squares = jnp.sum(mid_f * mid_f, axis=-1, keepdims=True)
    mid_wide = jnp.concatenate([mid, jnp.zeros((64, 128), BF)], axis=1)
    mid_own = dot(mid_wide, one_hot_lanes(lanes_ref[1:2, 0:512], 512))
    lane = lax.broadcasted_iota(jnp.int32, (64, 128), 1)
    high, middle, low = three_parts(squares)
    for z in range(NZ):
        piece = mid_own[:, z * 128 : (z + 1) * 128]
        piece = jnp.where(lane == 96, high, jnp.where(lane == 97, middle, jnp.where(lane == 98, low, piece)))
        x_send[z] = piece.astype(BF)
    for d in (1, 2, 3):
        start(x_send.at[zh], x_recv.at[own], s_x.at[d], r_x.at[d], at_c(d))
    x_recv[own] = x_send[zh]
    far = [(dz, db) for dz in (2, 1, 3) for db in (0, 1)]
    for n, (dz, db) in enumerate(far):
        tz, tb = (zh + dz) % NZ, (zl + db) % 2
        start(x_send.at[tz], x_recv.at[own], s_x.at[4 + n], r_x.at[4 + n], (col * NZ + tz, tb * 2 + core))

    def x_slot(dz, db, side):
        return x_recv.at[slot_of(dz) * NC + ((zl - db + 2) % 2) * 2 + side]

    hot = one_hot_lanes(lanes_ref[2:3, 0:512] + zh * 11, CMID + 128)
    gain_b_all = spread_gain(gain_b, hot)

    hot = one_hot_rows(rows_ref[:, 0:1], 512)
    for k in range(4):
        turned_a[:, k * 512 : (k + 1) * 512] = dot(hot, whole_a[:, k * 512 : (k + 1) * 512]).astype(BF)

    def inverse(z):
        total = jnp.zeros((64, 1), F32)
        for c in range(NC):
            part = x_recv[z * NC + c, :, 96:99].astype(F32)
            total += jnp.sum(part, axis=-1, keepdims=True)
        return lax.rsqrt(total * (1.0 / CMID) + EPS)

    for d in (1, 2, 3):
        arrived(x_recv.at[zh * NC + (ch - d + NC) % NC], s_x.at[d], r_x.at[d])
    inv_b = inverse(zh)
    normed_b = mid_own * inv_b
    factor_b = gelu_slope(normed_b * gain_b_own) * gain_b_own
    scattered(back_recv, s_b, r_b)
    grad_n = two_shares(back_recv) * factor_b
    in_send[...] = to_row(jnp.sum(grad_n * normed_b, axis=-1, keepdims=True))
    for d in (1, 2, 3):
        start(in_send, in_recv.at[ch], s_col.at[3, d], r_col.at[3, d], at_c(d))

    for n, (dz, db) in enumerate(far):
        arrived(x_slot(dz, db, core), s_x.at[4 + n], r_x.at[4 + n])
        start(x_slot(dz, db, core), x_slot(dz, db, core), s_x.at[10 + n], r_x.at[10 + n], twin)
    inner = in_send[...]
    for d in (1, 2, 3):
        at = (ch - d + NC) % NC
        arrived(in_recv.at[at], s_col.at[3, d], r_col.at[3, d])
        inner += in_recv[at]
    inner = jnp.concatenate([to_column(inner * (1.0 / CMID), 64)] * 4, axis=1)
    grad_mid = (inv_b * (grad_n - normed_b * inner)).astype(BF)
    gm_slot[zh] = dot(grad_mid, one_hot_rows(rows_ref[:, 3:4], 384)).astype(BF)
    for d in (1, 2, 3):
        start(gm_slot.at[zh], gm_slot.at[zh], s_col.at[4, d], r_col.at[4, d], at_z(d))

    def last_rows(z, w):
        return pltpu.make_async_remote_copy(
            src_ref=gm_slot.at[3, pl.ds(w * 32 + 16, EDGE), :], dst_ref=gm_prev.at[w], send_sem=s_gm.at[0, z, w],
            recv_sem=s_edge_gm.at[0, w], device_id=beside(1, z), device_id_type=MESH)

    def first_rows(z, w):
        return pltpu.make_async_remote_copy(
            src_ref=gm_slot.at[0, pl.ds(w * 32, EDGE), :], dst_ref=gm_next.at[w], send_sem=s_gm.at[1, z, w],
            recv_sem=s_edge_gm.at[1, w], device_id=beside(-1, z), device_id_type=MESH)

    @pl.when(zh == NZ - 1)
    def _():
        for z in range(NZ):
            for w in range(2):
                last_rows(z, w).start()

    @pl.when(zh == 0)
    def _():
        for z in range(NZ):
            for w in range(2):
                first_rows(z, w).start()

    hot = one_hot_lanes(lanes_ref[3:4, 0:512] + ch * 320, CIN)
    gain_a_own = spread_gain(gain_a, hot)
    feat_bf = feat_ref[...].reshape(128, CIN)
    inv_a = inverse_a(feat_bf.astype(F32))
    feat_own = dot(feat_bf, hot)
    normed_a = feat_own * inv_a
    factor_a = gelu_slope(normed_a * gain_a_own) * gain_a_own

    for n, (dz, db) in enumerate(far):
        arrived(x_slot(dz, db, 1 - core), s_x.at[10 + n], r_x.at[10 + n])
    for z in range(NZ):
        inv = inverse(z)
        values = jnp.concatenate([x_recv[z * NC + c].astype(F32) for c in range(NC)], axis=1)
        b_slot[z] = gelu_tanh(values * inv * gain_b_all).astype(BF)
    edges(b_slot, 32, b_prev, b_next, 2)

    for d in (1, 2, 3):
        arrived(gm_slot.at[slot_of(d)], s_col.at[4, d], r_col.at[4, d])

    for w in range(2):
        arrived(gm_prev.at[w], s_gm.at[0, 0, w], s_edge_gm.at[0, w])
        arrived(gm_next.at[w], s_gm.at[1, 0, w], s_edge_gm.at[1, w])
    lay(gm_slot, 32, gm_prev, gm_next, gm_rows)
    before, here, after = shifted(gm_rows, 128)
    back_conv(before, here, after, turned_a, 128, out_rows)
    to_twin(out_rows, 64, out_over, out_twin, 1)
    edges_done(b_prev, b_next, 2)
    lay(b_slot, 32, b_prev, b_next, b_rows)
    taps = pooled_taps(b_rows, 64)
    total = dot(taps[0], whole_b[:, 0:384])
    for k in range(1, 5):
        total += dot(taps[k], whole_b[:, k * 384 : (k + 1) * 384])
    for w in range(2):
        acc_b[w] = total[w * 64 : (w + 1) * 64]
    for z in range(NZ):
        for w in range(2):
            pool_send[z, w * 16 : (w + 1) * 16, :] = total[w * 64 + z * 16 : w * 64 + (z + 1) * 16].astype(BF)

    from_twin(out_rows, 64, out_twin, out_send, 1)
    scatter(out_send, out_recv, s_o, r_o)

    for d in (1, 2, 3):
        t = (zh + d) % NZ
        start(pool_send.at[t], pool_recv.at[zh], s_col.at[5, d], r_col.at[5, d], at_z(d))

    for d in (1, 2, 3):
        arrived(pool_recv.at[slot_of(d)], s_col.at[5, d], r_col.at[5, d])
    total = jnp.concatenate([acc_b[w, pl.ds(pl.multiple_of(zh * 16, 16), 16), :] for w in range(2)], axis=0)
    for d in (1, 2, 3):
        total += pool_recv[slot_of(d)].astype(F32)
    pooled_ref[...] = (total + bias_b_ref[...].reshape(1, 384)).astype(BF).reshape(2, 16, 384)

    scattered(out_recv, s_o, r_o)
    grad_n = two_shares(out_recv) * factor_a
    ia_send[...] = to_row(jnp.sum(grad_n * normed_a, axis=-1, keepdims=True))
    for d in (1, 2, 3):
        start(ia_send, ia_recv.at[ch], s_col.at[6, d], r_col.at[6, d], at_c(d))
    hot = one_hot_rows(rows_ref[:, 4:5], 384)
    inner = ia_send[...]
    for d in (1, 2, 3):
        at = (ch - d + NC) % NC
        arrived(ia_recv.at[at], s_col.at[6, d], r_col.at[6, d])
        inner += ia_recv[at]
    inner = jnp.concatenate([to_column(inner * (1.0 / CIN), 128)] * 4, axis=1)
    grad = (inv_a * (grad_n - normed_a * inner)).astype(BF)
    grad_ref[...] = dot(grad, hot)[:, 0:320].astype(BF).reshape(2, 64, 320)

    for copy in pending:
        copy.wait_send()
    scatter_sent(back_send, s_b, r_b)
    scatter_sent(out_send, s_o, r_o)

    @pl.when(zh == NZ - 1)
    def _():
        for z in range(NZ):
            for w in range(2):
                last_rows(z, w).wait_send()

    @pl.when(zh == 0)
    def _():
        for z in range(NZ):
            for w in range(2):
                first_rows(z, w).wait_send()


def per_device(dna_features, gain_a, conv_a, bias_a, gain_b, conv_b, bias_b, grad_out):
    lanes, rows = index_tables()
    dma = pltpu.SemaphoreType.DMA
    vmem = pltpu.VMEM
    pooled, grad = pl.pallas_call(
        kernel,
        out_shape=(jax.ShapeDtypeStruct((2, 16, 384), BF), jax.ShapeDtypeStruct((2, 64, 320), BF)),
        in_specs=[pl.BlockSpec(memory_space=pl.ANY)] * 10,
        out_specs=[pl.BlockSpec(memory_space=vmem)] * 2,
        scratch_shapes=[
            vmem((2, 64, CIN), BF), vmem((5, 10, 352), BF), vmem((5, 11, 384), BF), vmem((CIN,), F32), vmem((352,), F32),
            vmem((CMID,), F32), vmem((384,), F32), vmem((2, 16, 384), BF), vmem((8, 1536), jnp.int32), vmem((512, 8), jnp.int32),
            vmem((8, 64, 384), BF), vmem((4, 64, 384), BF), vmem((512, WIDE), BF), vmem((512, WIDE), BF),
            vmem((512, WIDE), BF), vmem((8, 384), F32),
            vmem((4, 128, 384), BF), vmem((2, 16, 384), BF), vmem((2, 16, 384), BF), vmem((2, 3, 288, 128), F32),
            vmem((5, 256, 512), BF), vmem((4, 64, 384), BF),
            vmem((4, 32, 384), BF), vmem((32, 384), BF), vmem((2, 16, 384), BF), vmem((2, 16, 384), BF), vmem((2, 3, 96, 128), F32),
            vmem((2, 4, 128, 128), F32), vmem((8, 64, 128), BF), vmem((8, 64, 128), BF), vmem((8, 64, 128), BF),
            vmem((8, 64, 128), BF), vmem((2, 128, 384), F32), vmem((4, 64, 384), BF), vmem((4, 64, 384), BF),
            vmem((4, 64, 128), BF), vmem((16, 64, 128), BF), vmem((4, 64, 512), BF), vmem((2, 16, 512), BF),
            vmem((2, 16, 512), BF), vmem((2, 4, 160, 128), F32),
            vmem((4, 32, 384), BF), vmem((4, 32, 384), BF), vmem((2, 64, 384), F32),
            vmem((8, 128), F32), vmem((4, 8, 128), F32), vmem((4, 64, 384), BF), vmem((2, 16, 384), BF),
            vmem((2, 16, 384), BF), vmem((2, 3, 160, 128), F32),
            vmem((2, 4, 256, 128), F32), vmem((8, 128, 128), BF), vmem((8, 128, 128), BF), vmem((8, 128, 128), BF),
            vmem((8, 128, 128), BF),
            vmem((8, 128), F32), vmem((4, 8, 128), F32),
            dma((2, 4)), dma((2, 4)), dma((4,)), dma((4,)), dma((2, 4, 2)), dma((2, 4, 2)), dma((2, 2, 2)), dma((2, 2, 2)),
            dma((7, 4)), dma((7, 4)), dma((4, 4)), dma((4, 4)),
            dma((16,)), dma((16,)), dma((16,)), dma((16,)), dma((16,)), dma((16,)), dma((10,)), dma((2, 4, 2)), dma((2, 2)), dma((4,)), dma((4,)),
            dma((2,)), dma((2,)),
        ],
        compiler_params=pltpu.CompilerParams(
            collective_id=0, has_side_effects=True, vmem_limit_bytes=60 * 1024 * 1024
        ),
        cost_estimate=pl.CostEstimate(flops=3_000_000_000, bytes_accessed=8_000_000, transcendentals=800_000),
    )(
        dna_features, conv_a, conv_b, gain_a, bias_a, gain_b, bias_b, grad_out, jnp.asarray(lanes), jnp.asarray(rows),
    )
    return pooled, grad


def solution(mesh):
    return jax.shard_map(
        per_device,
        mesh=mesh,
        in_specs=(
            P(None, "seq", None), P(), P(None, "seq", "ch"), P("ch"), P(), P(None, "seq", "ch"), P("ch"),
            P(None, "seq", "ch"),
        ),
        out_specs=(P(None, "seq", "ch"), P(None, "seq", "ch")),
        check_vma=False,
    )
```

```python
import math

import jax
import jax.numpy as jnp
import numpy as np
from jax import lax
from jax.experimental import pallas as pl
from jax.experimental.pallas import tpu as pltpu
from jax.sharding import PartitionSpec as P

EPS = 1e-06
ROOT = math.sqrt(2.0 / math.pi)
MESH = pl.DeviceIdType.MESH
BF = jnp.bfloat16
F32 = jnp.float32
NY, NX, NZ, NC = 8, 4, 4, 4
CIN, CMID = 1280, 1408
EDGE = 16
WIDE = 2048
TAPS = 5 * 384


def gelu_tanh(z):
    return 0.5 * z * (1.0 + jnp.tanh(ROOT * (z + 0.044715 * z * z * z)))


def gelu_slope(z):
    t = jnp.tanh(ROOT * (z + 0.044715 * z * z * z))
    return 0.5 * (1.0 + t) + 0.5 * z * (1.0 - t * t) * ROOT * (1.0 + 3.0 * 0.044715 * z * z)


def index_tables():
    lanes = np.full((8, 1536), -100000, np.int32)
    rows = np.full((512, 8), -100000, np.int32)
    for zb in range(NZ):
        for xb in range(NX):
            for yb in range(NY):
                for i in range(10):
                    lanes[0, zb * 384 + xb * 80 + yb * 10 + i] = ((yb * 4 + xb) * 4 + zb) * 10 + i
            for yy in range(2):
                for i in range(11):
                    q = yy * 48 + xb * 11 + i
                    here = ((yy * 4 + xb) * 4 + zb) * 11 + i
                    lanes[1, zb * 128 + q] = here
                    rows[zb * 128 + q, 3] = here
                for i in range(10):
                    q = xb * 20 + yy * 10 + i
                    here = ((yy * 4 + xb) * 4 + zb) * 10 + i
                    lanes[3, zb * 128 + q] = here
                    rows[zb * 128 + q, 4] = here
    for cb in range(NC):
        for xb in range(NX):
            for yy in range(2):
                for i in range(11):
                    lanes[2, cb * 128 + yy * 48 + xb * 11 + i] = (((cb * 2 + yy) * 4 + xb) * 4) * 11 + i
                for i in range(10):
                    rows[cb * 128 + xb * 20 + yy * 10 + i, 0] = xb * 80 + (cb * 2 + yy) * 10 + i
    for k in range(5):
        for yb in range(NY):
            for i in range(10):
                rows[k * 80 + yb * 10 + i, 1] = yb * 64 + k * 10 + i
        for xb in range(NX):
            for i in range(11):
                rows[k * 48 + xb * 11 + i, 2] = xb * 64 + k * 11 + i
    return lanes, rows


def dot(a, b):
    return lax.dot_general(a, b, (((1,), (0,)), ((), ())), preferred_element_type=F32)


def dot_t(a, b):
    return lax.dot_general(a, b, (((1,), (1,)), ((), ())), preferred_element_type=F32)


def one_hot_lanes(table, depth):
    row = lax.broadcasted_iota(jnp.int32, (depth, table.shape[1]), 0)
    return jnp.where(row == table, 1.0, 0.0).astype(BF)


def one_hot_rows(table, depth):
    col = lax.broadcasted_iota(jnp.int32, (table.shape[0], depth), 1)
    return jnp.where(col == table, 1.0, 0.0).astype(BF)


def three_parts(v):
    high = v.astype(BF).astype(F32)
    rest = v - high
    middle = rest.astype(BF).astype(F32)
    return high, middle, rest - middle


def spread_gain(gain, hot):
    high, middle, low = three_parts(gain)
    row = lax.broadcasted_iota(jnp.int32, (16, gain.shape[1]), 0)
    stack = jnp.where(row == 0, high, jnp.where(row == 1, middle, jnp.where(row == 2, low, 0.0)))
    return jnp.sum(dot(stack.astype(BF), hot), axis=0, keepdims=True)


def kernel(
    feat_in, wa_in, wb_in, gain_a_in, bias_a_in, gain_b_in, bias_b_in, g_in, lanes_in, rows_in,
    pooled_ref, grad_ref,
    feat_ref, wa_ref, wb_ref, gain_a_ref, bias_a_ref, gain_b_ref, bias_b_ref, g_ref, lanes_ref, rows_ref,
    first_a, first_b, whole_a, turned_a, whole_b, bias_pad,
    act_slot, act_prev, act_next, act_rows, taps_a, send_act,
    g_slot, g_send, g_prev, g_next, g_rows,
    back_rows, back_over, back_twin, back_send, back_recv,
    acc_a, mid_send, mid_recv,
    x_send, x_recv, b_slot, b_prev, b_next, b_rows,
    pool_send, pool_recv, acc_b,
    in_send, in_recv, gm_slot, gm_prev, gm_next, gm_rows,
    out_rows, out_over, out_twin, out_send, out_recv, ia_send, ia_recv,
    s_fa, r_fa, s_fb, r_fb, s_wb, r_wb, s_wa, r_wa, s_col, r_col, s_edge, r_edge,
    s_b, r_b, s_x, r_x, s_o, r_o, s_in, s_gm, s_edge_gm, s_af, r_af, s_tw, r_tw,
):
    seq = lax.axis_index("seq")
    ch = lax.axis_index("ch")
    zh = seq % NZ
    col = seq // NZ
    xi = col % NX
    yi = col // NX
    own = zh * NC + ch
    core = ch % 2
    zl = ch // 2
    twin = (seq, ch + 1 - 2 * core)
    own8 = zh * 2 + zl
    pending = []
    loads = [
        pltpu.make_async_copy(src, dst, s_in.at[i])
        for i, (src, dst) in enumerate((
            (wa_in, wa_ref), (wb_in, wb_ref), (rows_in, rows_ref), (lanes_in, lanes_ref), (feat_in, feat_ref),
            (gain_a_in, gain_a_ref), (g_in, g_ref), (bias_a_in, bias_a_ref), (gain_b_in, gain_b_ref),
            (bias_b_in, bias_b_ref),
        ))
    ]
    for load in loads:
        load.start()

    def start(src, dst, ssem, rsem, dev):
        copy = pltpu.make_async_remote_copy(
            src_ref=src, dst_ref=dst, send_sem=ssem, recv_sem=rsem, device_id=dev, device_id_type=MESH
        )
        copy.start()
        pending.append(copy)

    def arrived(dst, ssem, rsem):
        pltpu.make_async_remote_copy(
            src_ref=dst, dst_ref=dst, send_sem=ssem, recv_sem=rsem, device_id=(seq, ch), device_id_type=MESH
        ).wait_recv()

    def at_y(d):
        return ((((yi + d + NY) % NY) * NX + xi) * NZ + zh, ch)

    def at_x(d):
        return ((yi * NX + (xi + d + NX) % NX) * NZ + zh, ch)

    def at_z(d):
        return (col * NZ + (zh + d) % NZ, ch)

    def at_c(d):
        return (seq, (ch + d) % NC)

    def at_col(d):
        return (((col + d + 32) % 32) * NZ + zh, ch)

    def member(d):
        tz, tc = (zh + d // NC) % NZ, (ch + d % NC) % NC
        return tz * NC + tc, (col * NZ + tz, tc)

    def source(d):
        return ((zh - d // NC + NZ) % NZ) * NC + (ch - d % NC + NC) % NC

    def beside(way, z):
        return (((col + way + 32) % 32) * NZ + z, ch)

    barrier = pltpu.get_barrier_semaphore()

    def greet(dev):
        pl.semaphore_signal(barrier, inc=1, device_id=dev, device_id_type=MESH)

    for d in (1, 2, 3):
        greet(at_x(d))
    for d in (-1, 1):
        greet(at_y(d))
        greet(at_y(2 * d))
        for z in range(NZ):
            greet(beside(d, z))

    @pl.loop(1, 16)
    def _(d):
        greet(member(d)[1])

    for load in loads:
        load.wait()
    gain_a = gain_a_ref[...].reshape(1, CIN)
    gain_b = gain_b_ref[...].reshape(1, CMID)

    first_a[yi] = jnp.zeros((64, 384), BF)
    bias_pad[...] = jnp.zeros((8, 384), F32)
    bias_pad[0:1, 0:352] = bias_a_ref[...].reshape(1, 352)
    pack_a = jnp.zeros((64, 352), F32)
    pack_b = jnp.zeros((64, 384), F32)
    for k in range(5):
        pick = lax.broadcasted_iota(jnp.int32, (64, 10), 0) == lax.broadcasted_iota(jnp.int32, (64, 10), 1) + 10 * k
        pack_a += dot(jnp.where(pick, 1.0, 0.0).astype(BF), wa_ref[k])
        pick = lax.broadcasted_iota(jnp.int32, (64, 11), 0) == lax.broadcasted_iota(jnp.int32, (64, 11), 1) + 11 * k
        pack_b += dot(jnp.where(pick, 1.0, 0.0).astype(BF), wb_ref[k])
    first_a[yi, :, 0:352] = pack_a.astype(BF)
    first_b[xi] = pack_b.astype(BF)
    whole_a[320:512, :] = jnp.zeros((192, WIDE), BF)
    whole_a[0:320, TAPS:WIDE] = jnp.zeros((320, WIDE - TAPS), BF)
    whole_b[:, TAPS:WIDE] = jnp.zeros((512, WIDE - TAPS), BF)
    for c in range(NC):
        whole_b[c * 128 + 96 : c * 128 + 128, 0:TAPS] = jnp.zeros((32, TAPS), BF)
    taps_a[:, :, 384:512] = jnp.zeros((5, 256, 128), BF)
    pl.semaphore_wait(barrier, 30)

    parts = ((0, 1152), (1152, 768))

    def first_block(d, at=0, n=64):
        return first_a.at[(yi + d + NY) % NY, pl.ds(at, n), :]

    hops = (
        ((0, 1, 0, 64), (0, -1, 0, 64), (0, 2, 0, 64), (0, -2, 0, 64)),
        ((-2, 1, 0, 64), (2, -1, 0, 64), (-2, 2, 0, 32), (2, -2, 32, 32)),
    )

    def send_first(step):
        for n, (b, to, at, rows) in enumerate(hops[step]):
            ref = first_block(b, at, rows)
            start(ref, ref, s_fa.at[step, n], r_fa.at[step, n], at_y(to))

    def first_done(step, which):
        for n in which:
            b, to, at, rows = hops[step][n]
            arrived(first_block(b - to, at, rows), s_fa.at[step, n], r_fa.at[step, n])

    def place_a(b):
        return pl.multiple_of(b * 80, 16)

    def place_b(b):
        return pl.multiple_of((b // 2) * 128 + (b % 2) * 48, 16)

    def ring_wb(r, way, c):
        sign = 1 if way == 0 else -1
        ref = whole_b.at[pl.ds(place_b((yi - sign * r + NY) % NY), 48), pl.ds(*parts[c])]
        start(ref, ref, s_wb.at[way, r, c], r_wb.at[way, r, c], at_y(sign))

    def ring_wb_done(r, way, c):
        sign = 1 if way == 0 else -1
        ref = whole_b.at[pl.ds(place_b((yi - sign * (r + 1) + NY) % NY), 48), pl.ds(*parts[c])]
        arrived(ref, s_wb.at[way, r, c], r_wb.at[way, r, c])

    def ring_wa(r, way, c):
        sign = 1 if way == 0 else -1
        ref = whole_a.at[pl.ds(place_a((xi - sign * r + NX) % NX), 80), pl.ds(*parts[c])]
        start(ref, ref, s_wa.at[way, r, c], r_wa.at[way, r, c], at_x(sign))

    def ring_wa_done(r, way, c):
        sign = 1 if way == 0 else -1
        ref = whole_a.at[pl.ds(place_a((xi - sign * (r + 1) + NX) % NX), 80), pl.ds(*parts[c])]
        arrived(ref, s_wa.at[way, r, c], r_wa.at[way, r, c])

    def pass_on(ring, done, r, last, rank):
        for way in (0, 1):
            c = way if rank == 0 else 1 - way
            done(r, way, c)
            if r + 1 < last or (r + 1 == last and rank == 0):
                ring(r + 1, way, c)

    send_first(0)
    for d in (1, 2, 3):
        start(first_b.at[xi], first_b.at[xi], s_fb.at[d], r_fb.at[d], at_x(d))

    def slot_of(d):
        return (zh - d + NZ) % NZ

    def inverse_a(v):
        return lax.rsqrt(jnp.sum(v * v, axis=-1, keepdims=True) * (1.0 / CIN) + EPS)

    feat = feat_ref[core].astype(F32)
    act = gelu_tanh(feat * inverse_a(feat) * gain_a).astype(BF)
    mine = pl.ds(pl.multiple_of(core * 64, 64), 64)
    others = pl.ds(pl.multiple_of(64 - core * 64, 64), 64)

    def subset(d):
        t = (zh + d) % NZ
        hot = one_hot_lanes(lanes_ref[0:1, pl.ds(pl.multiple_of(t * 384, 128), 384)], CIN)
        part = dot(act, hot).astype(BF)
        if d == 0:
            act_slot[zh, mine, :] = part
            share_act(0)
        else:
            send_act[d] = part
            start(send_act.at[d], act_slot.at[zh, mine, :], s_col.at[1, d], r_col.at[1, d], at_z(d))

    def share_act(d):
        ref = act_slot.at[slot_of(d), mine, :]
        start(ref, ref, s_af.at[d], r_af.at[d], twin)

    subset(2)
    first_done(0, (2, 3))
    send_first(1)

    for d in (1, 2, 3):
        arrived(first_b.at[(xi - d + NX) % NX], s_fb.at[d], r_fb.at[d])
    hot_b = one_hot_rows(rows_ref[0:240, 2:3], 256)
    block = dot(hot_b, first_b[...].reshape(256, 384)).astype(BF)
    for k in range(5):
        whole_b[pl.ds(place_b(yi), 48), k * 384 : (k + 1) * 384] = block[k * 48 : (k + 1) * 48]
    for rank in (0, 1):
        for way in (0, 1):
            ring_wb(0, way, way if rank == 0 else 1 - way)
    subset(1)
    subset(3)
    subset(0)
    g_own = g_ref[...].reshape(32, 384)
    g_slot[zh] = g_own
    g_send[...] = g_own
    for d in (1, 2, 3):
        start(g_send, g_slot.at[zh], s_col.at[0, d], r_col.at[0, d], at_z(d))
    hot_a = one_hot_rows(rows_ref[0:400, 1:2], 512)
    first_done(0, (0, 1))
    first_done(1, range(4))
    block = dot(hot_a, first_a[...].reshape(512, 384)).astype(BF)
    for k in range(5):
        whole_a[pl.ds(place_a(xi), 80), k * 384 : (k + 1) * 384] = block[k * 80 : (k + 1) * 80]
    for rank in (0, 1):
        for way in (0, 1):
            ring_wa(0, way, way if rank == 0 else 1 - way)
    pass_on(ring_wb, ring_wb_done, 0, 3, 0)
    for d in (1, 3, 2):
        arrived(act_slot.at[slot_of(d), mine, :], s_col.at[1, d], r_col.at[1, d])
        share_act(d)
    pass_on(ring_wb, ring_wb_done, 0, 3, 1)

    def edges(slots, rows, prev, nxt, n):
        for w in range(2):
            lo = slots.at[0, pl.ds(w * rows, EDGE), :]
            hi = slots.at[3, pl.ds(w * rows + rows - EDGE, EDGE), :]
            start(hi, prev.at[w], s_edge.at[n, w], r_edge.at[n, w], at_col(1))
            start(lo, nxt.at[w], s_edge.at[n, 2 + w], r_edge.at[n, 2 + w], at_col(-1))

    def edges_done(prev, nxt, n):
        for w in range(2):
            arrived(prev.at[w], s_edge.at[n, w], r_edge.at[n, w])
            arrived(nxt.at[w], s_edge.at[n, 2 + w], r_edge.at[n, 2 + w])

    is_first = jnp.where(col == 0, 0.0, 1.0).astype(F32)
    is_last = jnp.where(col == 31, 0.0, 1.0).astype(F32)

    def lay(slots, rows, prev, nxt, where):
        tiles = where.shape[1]
        for w in range(2):
            for t in range(tiles):
                lanes = slice(t * 128, (t + 1) * 128)
                where[w, t, 0:EDGE, :] = prev[w, :, lanes].astype(F32) * is_first
                for z in range(NZ):
                    at = EDGE + z * rows
                    where[w, t, at : at + rows, :] = slots[z, w * rows : (w + 1) * rows, lanes].astype(F32)
                at = EDGE + NZ * rows
                where[w, t, at : at + EDGE, :] = nxt[w, :, lanes].astype(F32) * is_last

    def pooled_taps(where, rows):
        tiles = where.shape[1]
        parts = [[[where[w, t, pl.ds(EDGE + d, rows, stride=2), :] for t in range(tiles)] for w in range(2)]
                 for d in range(-2, 4)]
        out = []
        for k in range(5):
            wins = []
            for w in range(2):
                wins.append(jnp.concatenate(
                    [((parts[k][w][t] + parts[k + 1][w][t]) * 0.5).astype(BF) for t in range(tiles)], axis=1))
            out.append(jnp.concatenate(wins, axis=0))
        return out

    def shifted(where, rows):
        tiles = where.shape[1]
        return [
            jnp.concatenate([
                jnp.concatenate([where[w, t, EDGE + d : EDGE + d + rows, :].astype(BF) for t in range(tiles)], axis=1)
                for w in range(2)], axis=0)
            for d in (-1, 0, 1)
        ]

    def back_conv(before, here, after, weight, rows, where):
        none = jnp.zeros((2 * rows, WIDE - TAPS), BF)
        even = jnp.concatenate([after, here, here, before, before, none], axis=1)
        odd = jnp.concatenate([after, after, here, here, before, none], axis=1)
        total = dot_t(jnp.concatenate([even, odd], axis=0), weight[...]) * 0.5
        even, odd = total[0 : 2 * rows], total[2 * rows : 4 * rows]
        for w in range(2):
            for t in range(where.shape[1]):
                lanes = slice(t * 128, (t + 1) * 128)
                where[w, t, pl.ds(0, rows, stride=2), :] = even[w * rows : (w + 1) * rows, lanes]
                where[w, t, pl.ds(1, rows, stride=2), :] = odd[w * rows : (w + 1) * rows, lanes]

    pass_on(ring_wb, ring_wb_done, 1, 3, 0)
    pass_on(ring_wa, ring_wa_done, 0, 1, 0)
    for d in (1, 2, 3):
        arrived(g_slot.at[slot_of(d)], s_col.at[0, d], r_col.at[0, d])
    edges(g_slot, 16, g_prev, g_next, 0)
    pass_on(ring_wb, ring_wb_done, 1, 3, 1)
    for d in range(NZ):
        arrived(act_slot.at[slot_of(d), others, :], s_af.at[d], r_af.at[d])
    edges(act_slot, 64, act_prev, act_next, 1)
    pass_on(ring_wb, ring_wb_done, 2, 3, 0)
    edges_done(g_prev, g_next, 0)
    lay(g_slot, 16, g_prev, g_next, g_rows)
    edges_done(act_prev, act_next, 1)
    lay(act_slot, 64, act_prev, act_next, act_rows)
    for k, tap in enumerate(pooled_taps(act_rows, 128)):
        taps_a[k, :, 0:384] = tap
    pass_on(ring_wa, ring_wa_done, 0, 1, 1)
    for way in (0, 1):
        ring_wa_done(1, way, way)

    total = dot(taps_a[0], whole_a[:, 0:384])
    for k in range(1, 5):
        total += dot(taps_a[k], whole_a[:, k * 384 : (k + 1) * 384])
    for w in range(2):
        acc_a[w] = total[w * 128 : (w + 1) * 128]
    for z in range(NZ):
        for w in range(2):
            mid_send[z, w * 32 : (w + 1) * 32, :] = total[w * 128 + z * 32 : w * 128 + (z + 1) * 32].astype(BF)
    for d in (1, 2, 3):
        t = (zh + d) % NZ
        start(mid_send.at[t], mid_recv.at[zh], s_col.at[2, d], r_col.at[2, d], at_z(d))

    pass_on(ring_wb, ring_wb_done, 2, 3, 1)
    for way in (0, 1):
        ring_wb_done(3, way, way)
    before, here, after = shifted(g_rows, 64)
    back_conv(before, here, after, whole_b, 64, back_rows)
    def to_twin(where, per, send, recv, n):
        for z in range(NZ):
            for b in range(2):
                for w in range(2):
                    piece = where[w, b * 2 + 1 - core, z * per : (z + 1) * per, :]
                    send[z * 2 + b, w * per : (w + 1) * per, :] = piece.astype(BF)
        start(send, recv, s_tw.at[n], r_tw.at[n], twin)

    def from_twin(where, per, recv, send, n):
        arrived(recv, s_tw.at[n], r_tw.at[n])
        for z in range(NZ):
            for b in range(2):
                for w in range(2):
                    piece = where[w, b * 2 + core, z * per : (z + 1) * per, :]
                    rows = slice(w * per, (w + 1) * per)
                    send[z * 2 + b, rows, :] = (piece + recv[z * 2 + b, rows, :].astype(F32)).astype(BF)

    def scatter(src, dst, ssem, rsem):
        @pl.loop(1, 8)
        def _(d):
            tz, tb = (zh + d // 2) % NZ, (zl + d % 2) % 2
            pltpu.make_async_remote_copy(
                src_ref=src.at[tz * 2 + tb], dst_ref=dst.at[own8], send_sem=ssem.at[d], recv_sem=rsem.at[d],
                device_id=(col * NZ + tz, tb * 2 + core), device_id_type=MESH,
            ).start()

        dst[own8] = src[own8]

    def scattered(dst, ssem, rsem):
        @pl.loop(1, 8)
        def _(d):
            arrived(dst.at[((zh - d // 2 + NZ) % NZ) * 2 + (zl - d % 2 + 2) % 2], ssem.at[d], rsem.at[d])

    def scatter_sent(src, ssem, rsem):
        @pl.loop(1, 8)
        def _(d):
            pltpu.make_async_remote_copy(
                src_ref=src.at[0], dst_ref=src.at[0], send_sem=ssem.at[d], recv_sem=rsem.at[d],
                device_id=(seq, ch), device_id_type=MESH,
            ).wait_send()

    def to_row(v):
        wide = jnp.broadcast_to(v, (v.shape[0], 128))
        if v.shape[0] < 128:
            wide = jnp.concatenate([wide, jnp.zeros((128 - v.shape[0], 128), F32)], axis=0)
        return jnp.transpose(wide)[0:8]

    def to_column(v, rows):
        return jnp.transpose(jnp.concatenate([v] * 16, axis=0))[0:rows]

    def two_shares(recv):
        return jnp.concatenate(
            [recv[z * 2].astype(F32) + recv[z * 2 + 1].astype(F32) for z in range(NZ)], axis=1)

    to_twin(back_rows, 32, back_over, back_twin, 0)
    from_twin(back_rows, 32, back_twin, back_send, 0)
    scatter(back_send, back_recv, s_b, r_b)

    gain_b = jnp.concatenate([gain_b, jnp.zeros((1, 128), F32)], axis=1)
    hot = one_hot_lanes(lanes_ref[1:2, 0:512] + ch * 352, CMID + 128)
    gain_b_own = spread_gain(gain_b, hot)

    for d in (1, 2, 3):
        arrived(mid_recv.at[slot_of(d)], s_col.at[2, d], r_col.at[2, d])
    total = jnp.concatenate([acc_a[w, pl.ds(pl.multiple_of(zh * 32, 32), 32), :] for w in range(2)], axis=0)
    for d in (1, 2, 3):
        total += mid_recv[slot_of(d)].astype(F32)
    mid = (total + bias_pad[0:1, :]).astype(BF)
    mid_f = mid.astype(F32)
    squares = jnp.sum(mid_f * mid_f, axis=-1, keepdims=True)
    mid_wide = jnp.concatenate([mid, jnp.zeros((64, 128), BF)], axis=1)
    mid_own = dot(mid_wide, one_hot_lanes(lanes_ref[1:2, 0:512], 512))
    lane = lax.broadcasted_iota(jnp.int32, (64, 128), 1)
    high, middle, low = three_parts(squares)
    for z in range(NZ):
        piece = mid_own[:, z * 128 : (z + 1) * 128]
        piece = jnp.where(lane == 96, high, jnp.where(lane == 97, middle, jnp.where(lane == 98, low, piece)))
        x_send[z] = piece.astype(BF)
    for d in (1, 2, 3):
        start(x_send.at[zh], x_recv.at[own], s_x.at[d], r_x.at[d], at_c(d))
    x_recv[own] = x_send[zh]
    far = [(dz, db) for dz in (2, 1, 3) for db in (0, 1)]
    for n, (dz, db) in enumerate(far):
        tz, tb = (zh + dz) % NZ, (zl + db) % 2
        start(x_send.at[tz], x_recv.at[own], s_x.at[4 + n], r_x.at[4 + n], (col * NZ + tz, tb * 2 + core))

    def x_slot(dz, db, side):
        return x_recv.at[slot_of(dz) * NC + ((zl - db + 2) % 2) * 2 + side]

    hot = one_hot_lanes(lanes_ref[2:3, 0:512] + zh * 11, CMID + 128)
    gain_b_all = spread_gain(gain_b, hot)

    hot = one_hot_rows(rows_ref[:, 0:1], 512)
    for k in range(4):
        turned_a[:, k * 512 : (k + 1) * 512] = dot(hot, whole_a[:, k * 512 : (k + 1) * 512]).astype(BF)

    def inverse(z):
        total = jnp.zeros((64, 1), F32)
        for c in range(NC):
            part = x_recv[z * NC + c, :, 96:99].astype(F32)
            total += jnp.sum(part, axis=-1, keepdims=True)
        return lax.rsqrt(total * (1.0 / CMID) + EPS)

    for d in (1, 2, 3):
        arrived(x_recv.at[zh * NC + (ch - d + NC) % NC], s_x.at[d], r_x.at[d])
    inv_b = inverse(zh)
    normed_b = mid_own * inv_b
    factor_b = gelu_slope(normed_b * gain_b_own) * gain_b_own
    scattered(back_recv, s_b, r_b)
    grad_n = two_shares(back_recv) * factor_b
    in_send[...] = to_row(jnp.sum(grad_n * normed_b, axis=-1, keepdims=True))
    for d in (1, 2, 3):
        start(in_send, in_recv.at[ch], s_col.at[3, d], r_col.at[3, d], at_c(d))

    for n, (dz, db) in enumerate(far):
        arrived(x_slot(dz, db, core), s_x.at[4 + n], r_x.at[4 + n])
        start(x_slot(dz, db, core), x_slot(dz, db, core), s_x.at[10 + n], r_x.at[10 + n], twin)
    inner = in_send[...]
    for d in (1, 2, 3):
        at = (ch - d + NC) % NC
        arrived(in_recv.at[at], s_col.at[3, d], r_col.at[3, d])
        inner += in_recv[at]
    inner = jnp.concatenate([to_column(inner * (1.0 / CMID), 64)] * 4, axis=1)
    grad_mid = (inv_b * (grad_n - normed_b * inner)).astype(BF)
    gm_slot[zh] = dot(grad_mid, one_hot_rows(rows_ref[:, 3:4], 384)).astype(BF)
    for d in (1, 2, 3):
        start(gm_slot.at[zh], gm_slot.at[zh], s_col.at[4, d], r_col.at[4, d], at_z(d))

    def last_rows(z, w):
        return pltpu.make_async_remote_copy(
            src_ref=gm_slot.at[3, pl.ds(w * 32 + 16, EDGE), :], dst_ref=gm_prev.at[w], send_sem=s_gm.at[0, z, w],
            recv_sem=s_edge_gm.at[0, w], device_id=beside(1, z), device_id_type=MESH)

    def first_rows(z, w):
        return pltpu.make_async_remote_copy(
            src_ref=gm_slot.at[0, pl.ds(w * 32, EDGE), :], dst_ref=gm_next.at[w], send_sem=s_gm.at[1, z, w],
            recv_sem=s_edge_gm.at[1, w], device_id=beside(-1, z), device_id_type=MESH)

    @pl.when(zh == NZ - 1)
    def _():
        for z in range(NZ):
            for w in range(2):
                last_rows(z, w).start()

    @pl.when(zh == 0)
    def _():
        for z in range(NZ):
            for w in range(2):
                first_rows(z, w).start()

    hot = one_hot_lanes(lanes_ref[3:4, 0:512] + ch * 320, CIN)
    gain_a_own = spread_gain(gain_a, hot)
    feat_bf = feat_ref[...].reshape(128, CIN)
    inv_a = inverse_a(feat_bf.astype(F32))
    feat_own = dot(feat_bf, hot)
    normed_a = feat_own * inv_a
    factor_a = gelu_slope(normed_a * gain_a_own) * gain_a_own

    for n, (dz, db) in enumerate(far):
        arrived(x_slot(dz, db, 1 - core), s_x.at[10 + n], r_x.at[10 + n])
    for z in range(NZ):
        inv = inverse(z)
        values = jnp.concatenate([x_recv[z * NC + c].astype(F32) for c in range(NC)], axis=1)
        b_slot[z] = gelu_tanh(values * inv * gain_b_all).astype(BF)
    edges(b_slot, 32, b_prev, b_next, 2)

    for d in (1, 2, 3):
        arrived(gm_slot.at[slot_of(d)], s_col.at[4, d], r_col.at[4, d])

    for w in range(2):
        arrived(gm_prev.at[w], s_gm.at[0, 0, w], s_edge_gm.at[0, w])
        arrived(gm_next.at[w], s_gm.at[1, 0, w], s_edge_gm.at[1, w])
    lay(gm_slot, 32, gm_prev, gm_next, gm_rows)
    before, here, after = shifted(gm_rows, 128)
    back_conv(before, here, after, turned_a, 128, out_rows)
    to_twin(out_rows, 64, out_over, out_twin, 1)
    edges_done(b_prev, b_next, 2)
    lay(b_slot, 32, b_prev, b_next, b_rows)
    taps = pooled_taps(b_rows, 64)
    total = dot(taps[0], whole_b[:, 0:384])
    for k in range(1, 5):
        total += dot(taps[k], whole_b[:, k * 384 : (k + 1) * 384])
    for w in range(2):
        acc_b[w] = total[w * 64 : (w + 1) * 64]
    for z in range(NZ):
        for w in range(2):
            pool_send[z, w * 16 : (w + 1) * 16, :] = total[w * 64 + z * 16 : w * 64 + (z + 1) * 16].astype(BF)

    from_twin(out_rows, 64, out_twin, out_send, 1)
    scatter(out_send, out_recv, s_o, r_o)

    for d in (1, 2, 3):
        t = (zh + d) % NZ
        start(pool_send.at[t], pool_recv.at[zh], s_col.at[5, d], r_col.at[5, d], at_z(d))

    for d in (1, 2, 3):
        arrived(pool_recv.at[slot_of(d)], s_col.at[5, d], r_col.at[5, d])
    total = jnp.concatenate([acc_b[w, pl.ds(pl.multiple_of(zh * 16, 16), 16), :] for w in range(2)], axis=0)
    for d in (1, 2, 3):
        total += pool_recv[slot_of(d)].astype(F32)
    pooled_ref[...] = (total + bias_b_ref[...].reshape(1, 384)).astype(BF).reshape(2, 16, 384)

    scattered(out_recv, s_o, r_o)
    grad_n = two_shares(out_recv) * factor_a
    ia_send[...] = to_row(jnp.sum(grad_n * normed_a, axis=-1, keepdims=True))
    for d in (1, 2, 3):
        start(ia_send, ia_recv.at[ch], s_col.at[6, d], r_col.at[6, d], at_c(d))
    hot = one_hot_rows(rows_ref[:, 4:5], 384)
    inner = ia_send[...]
    for d in (1, 2, 3):
        at = (ch - d + NC) % NC
        arrived(ia_recv.at[at], s_col.at[6, d], r_col.at[6, d])
        inner += ia_recv[at]
    inner = jnp.concatenate([to_column(inner * (1.0 / CIN), 128)] * 4, axis=1)
    grad = (inv_a * (grad_n - normed_a * inner)).astype(BF)
    grad_ref[...] = dot(grad, hot)[:, 0:320].astype(BF).reshape(2, 64, 320)

    for copy in pending:
        copy.wait_send()
    scatter_sent(back_send, s_b, r_b)
    scatter_sent(out_send, s_o, r_o)

    @pl.when(zh == NZ - 1)
    def _():
        for z in range(NZ):
            for w in range(2):
                last_rows(z, w).wait_send()

    @pl.when(zh == 0)
    def _():
        for z in range(NZ):
            for w in range(2):
                first_rows(z, w).wait_send()


def per_device(dna_features, gain_a, conv_a, bias_a, gain_b, conv_b, bias_b, grad_out):
    lanes, rows = index_tables()
    dma = pltpu.SemaphoreType.DMA
    vmem = pltpu.VMEM
    pooled, grad = pl.pallas_call(
        kernel,
        out_shape=(jax.ShapeDtypeStruct((2, 16, 384), BF), jax.ShapeDtypeStruct((2, 64, 320), BF)),
        in_specs=[pl.BlockSpec(memory_space=pl.ANY)] * 10,
        out_specs=[pl.BlockSpec(memory_space=vmem)] * 2,
        scratch_shapes=[
            vmem((2, 64, CIN), BF), vmem((5, 10, 352), BF), vmem((5, 11, 384), BF), vmem((CIN,), F32), vmem((352,), F32),
            vmem((CMID,), F32), vmem((384,), F32), vmem((2, 16, 384), BF), vmem((8, 1536), jnp.int32), vmem((512, 8), jnp.int32),
            vmem((8, 64, 384), BF), vmem((4, 64, 384), BF), vmem((512, WIDE), BF), vmem((512, WIDE), BF),
            vmem((512, WIDE), BF), vmem((8, 384), F32),
            vmem((4, 128, 384), BF), vmem((2, 16, 384), BF), vmem((2, 16, 384), BF), vmem((2, 3, 288, 128), F32),
            vmem((5, 256, 512), BF), vmem((4, 64, 384), BF),
            vmem((4, 32, 384), BF), vmem((32, 384), BF), vmem((2, 16, 384), BF), vmem((2, 16, 384), BF), vmem((2, 3, 96, 128), F32),
            vmem((2, 4, 128, 128), F32), vmem((8, 64, 128), BF), vmem((8, 64, 128), BF), vmem((8, 64, 128), BF),
            vmem((8, 64, 128), BF), vmem((2, 128, 384), F32), vmem((4, 64, 384), BF), vmem((4, 64, 384), BF),
            vmem((4, 64, 128), BF), vmem((16, 64, 128), BF), vmem((4, 64, 512), BF), vmem((2, 16, 512), BF),
            vmem((2, 16, 512), BF), vmem((2, 4, 160, 128), F32),
            vmem((4, 32, 384), BF), vmem((4, 32, 384), BF), vmem((2, 64, 384), F32),
            vmem((8, 128), F32), vmem((4, 8, 128), F32), vmem((4, 64, 384), BF), vmem((2, 16, 384), BF),
            vmem((2, 16, 384), BF), vmem((2, 3, 160, 128), F32),
            vmem((2, 4, 256, 128), F32), vmem((8, 128, 128), BF), vmem((8, 128, 128), BF), vmem((8, 128, 128), BF),
            vmem((8, 128, 128), BF),
            vmem((8, 128), F32), vmem((4, 8, 128), F32),
            dma((2, 4)), dma((2, 4)), dma((4,)), dma((4,)), dma((2, 4, 2)), dma((2, 4, 2)), dma((2, 2, 2)), dma((2, 2, 2)),
            dma((7, 4)), dma((7, 4)), dma((4, 4)), dma((4, 4)),
            dma((16,)), dma((16,)), dma((16,)), dma((16,)), dma((16,)), dma((16,)), dma((10,)), dma((2, 4, 2)), dma((2, 2)), dma((4,)), dma((4,)),
            dma((2,)), dma((2,)),
        ],
        compiler_params=pltpu.CompilerParams(
            collective_id=0, has_side_effects=True, vmem_limit_bytes=60 * 1024 * 1024
        ),
        cost_estimate=pl.CostEstimate(flops=3_000_000_000, bytes_accessed=8_000_000, transcendentals=800_000),
    )(
        dna_features, conv_a, conv_b, gain_a, bias_a, gain_b, bias_b, grad_out, jnp.asarray(lanes), jnp.asarray(rows),
    )
    return pooled, grad


def solution(mesh):
    return jax.shard_map(
        per_device,
        mesh=mesh,
        in_specs=(
            P(None, "seq", None), P(), P(None, "seq", "ch"), P("ch"), P(), P(None, "seq", "ch"), P("ch"),
            P(None, "seq", "ch"),
        ),
        out_specs=(P(None, "seq", "ch"), P(None, "seq", "ch")),
        check_vma=False,
    )
```

```python
import math

import jax
import jax.numpy as jnp
import numpy as np
from jax import lax
from jax.experimental import pallas as pl
from jax.experimental.pallas import tpu as pltpu
from jax.sharding import PartitionSpec as P

EPS = 1e-06
ROOT = math.sqrt(2.0 / math.pi)
MESH = pl.DeviceIdType.MESH
BF = jnp.bfloat16
F32 = jnp.float32
NY, NX, NZ, NC = 8, 4, 4, 4
CIN, CMID = 1280, 1408
EDGE = 16
WIDE = 2048
TAPS = 5 * 384


def gelu_tanh(z):
    return 0.5 * z * (1.0 + jnp.tanh(ROOT * (z + 0.044715 * z * z * z)))


def gelu_slope(z):
    t = jnp.tanh(ROOT * (z + 0.044715 * z * z * z))
    return 0.5 * (1.0 + t) + 0.5 * z * (1.0 - t * t) * ROOT * (1.0 + 3.0 * 0.044715 * z * z)


def index_tables():
    lanes = np.full((8, 1536), -100000, np.int32)
    rows = np.full((512, 8), -100000, np.int32)
    for zb in range(NZ):
        for xb in range(NX):
            for yb in range(NY):
                for i in range(10):
                    lanes[0, zb * 384 + xb * 80 + yb * 10 + i] = ((yb * 4 + xb) * 4 + zb) * 10 + i
            for yy in range(2):
                for i in range(11):
                    q = yy * 48 + xb * 11 + i
                    here = ((yy * 4 + xb) * 4 + zb) * 11 + i
                    lanes[1, zb * 128 + q] = here
                    rows[zb * 128 + q, 3] = here
                for i in range(10):
                    q = xb * 20 + yy * 10 + i
                    here = ((yy * 4 + xb) * 4 + zb) * 10 + i
                    lanes[3, zb * 128 + q] = here
                    rows[zb * 128 + q, 4] = here
    for cb in range(NC):
        for xb in range(NX):
            for yy in range(2):
                for i in range(11):
                    lanes[2, cb * 128 + yy * 48 + xb * 11 + i] = (((cb * 2 + yy) * 4 + xb) * 4) * 11 + i
                for i in range(10):
                    rows[cb * 128 + xb * 20 + yy * 10 + i, 0] = xb * 80 + (cb * 2 + yy) * 10 + i
    for k in range(5):
        for yb in range(NY):
            for i in range(10):
                rows[k * 80 + yb * 10 + i, 1] = yb * 64 + k * 10 + i
        for xb in range(NX):
            for i in range(11):
                rows[k * 48 + xb * 11 + i, 2] = xb * 64 + k * 11 + i
    return lanes, rows


def dot(a, b):
    return lax.dot_general(a, b, (((1,), (0,)), ((), ())), preferred_element_type=F32)


def dot_t(a, b):
    return lax.dot_general(a, b, (((1,), (1,)), ((), ())), preferred_element_type=F32)


def one_hot_lanes(table, depth):
    row = lax.broadcasted_iota(jnp.int32, (depth, table.shape[1]), 0)
    return jnp.where(row == table, 1.0, 0.0).astype(BF)


def one_hot_rows(table, depth):
    col = lax.broadcasted_iota(jnp.int32, (table.shape[0], depth), 1)
    return jnp.where(col == table, 1.0, 0.0).astype(BF)


def three_parts(v):
    high = v.astype(BF).astype(F32)
    rest = v - high
    middle = rest.astype(BF).astype(F32)
    return high, middle, rest - middle


def spread_gain(gain, hot):
    high, middle, low = three_parts(gain)
    row = lax.broadcasted_iota(jnp.int32, (16, gain.shape[1]), 0)
    stack = jnp.where(row == 0, high, jnp.where(row == 1, middle, jnp.where(row == 2, low, 0.0)))
    return jnp.sum(dot(stack.astype(BF), hot), axis=0, keepdims=True)


def kernel(
    feat_in, wa_in, wb_in, gain_a_in, bias_a_in, gain_b_in, bias_b_in, g_in, lanes_in, rows_in,
    pooled_ref, grad_ref,
    feat_ref, wa_ref, wb_ref, gain_a_ref, bias_a_ref, gain_b_ref, bias_b_ref, g_ref, lanes_ref, rows_ref,
    first_a, first_b, whole_a, turned_a, whole_b, bias_pad,
    act_slot, act_prev, act_next, act_rows, taps_a, send_act,
    g_slot, g_send, g_prev, g_next, g_rows,
    back_rows, back_over, back_twin, back_send, back_recv,
    acc_a, mid_send, mid_recv,
    x_send, x_recv, b_slot, b_prev, b_next, b_rows,
    pool_send, pool_recv, acc_b,
    in_send, in_recv, gm_slot, gm_prev, gm_next, gm_rows,
    out_rows, out_over, out_twin, out_send, out_recv, ia_send, ia_recv,
    s_fa, r_fa, s_fb, r_fb, s_wb, r_wb, s_wa, r_wa, s_col, r_col, s_edge, r_edge,
    s_b, r_b, s_x, r_x, s_o, r_o, s_in, s_gm, s_edge_gm, s_af, r_af, s_tw, r_tw,
):
    seq = lax.axis_index("seq")
    ch = lax.axis_index("ch")
    zh = seq % NZ
    col = seq // NZ
    xi = col % NX
    yi = col // NX
    own = zh * NC + ch
    core = ch % 2
    zl = ch // 2
    twin = (seq, ch + 1 - 2 * core)
    own8 = zh * 2 + zl
    pending = []
    loads = [
        pltpu.make_async_copy(src, dst, s_in.at[i])
        for i, (src, dst) in enumerate((
            (wa_in, wa_ref), (wb_in, wb_ref), (rows_in, rows_ref), (lanes_in, lanes_ref), (feat_in, feat_ref),
            (gain_a_in, gain_a_ref), (g_in, g_ref), (bias_a_in, bias_a_ref), (gain_b_in, gain_b_ref),
            (bias_b_in, bias_b_ref),
        ))
    ]
    for load in loads:
        load.start()

    def start(src, dst, ssem, rsem, dev):
        copy = pltpu.make_async_remote_copy(
            src_ref=src, dst_ref=dst, send_sem=ssem, recv_sem=rsem, device_id=dev, device_id_type=MESH
        )
        copy.start()
        pending.append(copy)

    def arrived(dst, ssem, rsem):
        pltpu.make_async_remote_copy(
            src_ref=dst, dst_ref=dst, send_sem=ssem, recv_sem=rsem, device_id=(seq, ch), device_id_type=MESH
        ).wait_recv()

    def at_y(d):
        return ((((yi + d + NY) % NY) * NX + xi) * NZ + zh, ch)

    def at_x(d):
        return ((yi * NX + (xi + d + NX) % NX) * NZ + zh, ch)

    def at_z(d):
        return (col * NZ + (zh + d) % NZ, ch)

    def at_c(d):
        return (seq, (ch + d) % NC)

    def at_col(d):
        return (((col + d + 32) % 32) * NZ + zh, ch)

    def member(d):
        tz, tc = (zh + d // NC) % NZ, (ch + d % NC) % NC
        return tz * NC + tc, (col * NZ + tz, tc)

    def source(d):
        return ((zh - d // NC + NZ) % NZ) * NC + (ch - d % NC + NC) % NC

    def beside(way, z):
        return (((col + way + 32) % 32) * NZ + z, ch)

    barrier = pltpu.get_barrier_semaphore()

    def greet(dev):
        pl.semaphore_signal(barrier, inc=1, device_id=dev, device_id_type=MESH)

    for d in (1, 2, 3):
        greet(at_x(d))
    for d in (-1, 1):
        greet(at_y(d))
        greet(at_y(2 * d))
        for z in range(NZ):
            greet(beside(d, z))

    @pl.loop(1, 16)
    def _(d):
        greet(member(d)[1])

    for load in loads:
        load.wait()
    gain_a = gain_a_ref[...].reshape(1, CIN)
    gain_b = gain_b_ref[...].reshape(1, CMID)

    first_a[yi] = jnp.zeros((64, 384), BF)
    bias_pad[...] = jnp.zeros((8, 384), F32)
    bias_pad[0:1, 0:352] = bias_a_ref[...].reshape(1, 352)
    pack_a = jnp.zeros((64, 352), F32)
    pack_b = jnp.zeros((64, 384), F32)
    for k in range(5):
        pick = lax.broadcasted_iota(jnp.int32, (64, 10), 0) == lax.broadcasted_iota(jnp.int32, (64, 10), 1) + 10 * k
        pack_a += dot(jnp.where(pick, 1.0, 0.0).astype(BF), wa_ref[k])
        pick = lax.broadcasted_iota(jnp.int32, (64, 11), 0) == lax.broadcasted_iota(jnp.int32, (64, 11), 1) + 11 * k
        pack_b += dot(jnp.where(pick, 1.0, 0.0).astype(BF), wb_ref[k])
    first_a[yi, :, 0:352] = pack_a.astype(BF)
    first_b[xi] = pack_b.astype(BF)
    whole_a[320:512, :] = jnp.zeros((192, WIDE), BF)
    whole_a[0:320, TAPS:WIDE] = jnp.zeros((320, WIDE - TAPS), BF)
    whole_b[:, TAPS:WIDE] = jnp.zeros((512, WIDE - TAPS), BF)
    for c in range(NC):
        whole_b[c * 128 + 96 : c * 128 + 128, 0:TAPS] = jnp.zeros((32, TAPS), BF)
    taps_a[:, :, 384:512] = jnp.zeros((5, 256, 128), BF)
    pl.semaphore_wait(barrier, 30)

    parts = ((0, 1152), (1152, 768))

    def first_block(d, at=0, n=64):
        return first_a.at[(yi + d + NY) % NY, pl.ds(at, n), :]

    hops = (
        ((0, 1, 0, 64), (0, -1, 0, 64), (0, 2, 0, 64), (0, -2, 0, 64)),
        ((-2, 1, 0, 64), (2, -1, 0, 64), (-2, 2, 0, 32), (2, -2, 32, 32)),
    )

    def send_first(step):
        for n, (b, to, at, rows) in enumerate(hops[step]):
            ref = first_block(b, at, rows)
            start(ref, ref, s_fa.at[step, n], r_fa.at[step, n], at_y(to))

    def first_done(step, which):
        for n in which:
            b, to, at, rows = hops[step][n]
            arrived(first_block(b - to, at, rows), s_fa.at[step, n], r_fa.at[step, n])

    def place_a(b):
        return pl.multiple_of(b * 80, 16)

    def place_b(b):
        return pl.multiple_of((b // 2) * 128 + (b % 2) * 48, 16)

    def ring_wb(r, way, c):
        sign = 1 if way == 0 else -1
        ref = whole_b.at[pl.ds(place_b((yi - sign * r + NY) % NY), 48), pl.ds(*parts[c])]
        start(ref, ref, s_wb.at[way, r, c], r_wb.at[way, r, c], at_y(sign))

    def ring_wb_done(r, way, c):
        sign = 1 if way == 0 else -1
        ref = whole_b.at[pl.ds(place_b((yi - sign * (r + 1) + NY) % NY), 48), pl.ds(*parts[c])]
        arrived(ref, s_wb.at[way, r, c], r_wb.at[way, r, c])

    def ring_wa(r, way, c):
        sign = 1 if way == 0 else -1
        ref = whole_a.at[pl.ds(place_a((xi - sign * r + NX) % NX), 80), pl.ds(*parts[c])]
        start(ref, ref, s_wa.at[way, r, c], r_wa.at[way, r, c], at_x(sign))

    def ring_wa_done(r, way, c):
        sign = 1 if way == 0 else -1
        ref = whole_a.at[pl.ds(place_a((xi - sign * (r + 1) + NX) % NX), 80), pl.ds(*parts[c])]
        arrived(ref, s_wa.at[way, r, c], r_wa.at[way, r, c])

    def pass_on(ring, done, r, last, rank):
        for way in (0, 1):
            c = way if rank == 0 else 1 - way
            done(r, way, c)
            if r + 1 < last or (r + 1 == last and rank == 0):
                ring(r + 1, way, c)

    send_first(0)
    for d in (1, 2, 3):
        start(first_b.at[xi], first_b.at[xi], s_fb.at[d], r_fb.at[d], at_x(d))

    def slot_of(d):
        return (zh - d + NZ) % NZ

    def inverse_a(v):
        return lax.rsqrt(jnp.sum(v * v, axis=-1, keepdims=True) * (1.0 / CIN) + EPS)

    feat = feat_ref[core].astype(F32)
    act = gelu_tanh(feat * inverse_a(feat) * gain_a).astype(BF)
    mine = pl.ds(pl.multiple_of(core * 64, 64), 64)
    others = pl.ds(pl.multiple_of(64 - core * 64, 64), 64)

    def subset(d):
        t = (zh + d) % NZ
        hot = one_hot_lanes(lanes_ref[0:1, pl.ds(pl.multiple_of(t * 384, 128), 384)], CIN)
        part = dot(act, hot).astype(BF)
        if d == 0:
            act_slot[zh, mine, :] = part
            share_act(0)
        else:
            send_act[d] = part
            start(send_act.at[d], act_slot.at[zh, mine, :], s_col.at[1, d], r_col.at[1, d], at_z(d))

    def share_act(d):
        ref = act_slot.at[slot_of(d), mine, :]
        start(ref, ref, s_af.at[d], r_af.at[d], twin)

    subset(2)
    first_done(0, (2, 3))
    send_first(1)

    for d in (1, 2, 3):
        arrived(first_b.at[(xi - d + NX) % NX], s_fb.at[d], r_fb.at[d])
    hot_b = one_hot_rows(rows_ref[0:240, 2:3], 256)
    block = dot(hot_b, first_b[...].reshape(256, 384)).astype(BF)
    for k in range(5):
        whole_b[pl.ds(place_b(yi), 48), k * 384 : (k + 1) * 384] = block[k * 48 : (k + 1) * 48]
    for rank in (0, 1):
        for way in (0, 1):
            ring_wb(0, way, way if rank == 0 else 1 - way)
    subset(1)
    subset(3)
    subset(0)
    g_own = g_ref[...].reshape(32, 384)
    g_slot[zh] = g_own
    g_send[...] = g_own
    for d in (1, 2, 3):
        start(g_send, g_slot.at[zh], s_col.at[0, d], r_col.at[0, d], at_z(d))
    hot_a = one_hot_rows(rows_ref[0:400, 1:2], 512)
    first_done(0, (0, 1))
    first_done(1, range(4))
    block = dot(hot_a, first_a[...].reshape(512, 384)).astype(BF)
    for k in range(5):
        whole_a[pl.ds(place_a(xi), 80), k * 384 : (k + 1) * 384] = block[k * 80 : (k + 1) * 80]
    for rank in (0, 1):
        for way in (0, 1):
            ring_wa(0, way, way if rank == 0 else 1 - way)
    pass_on(ring_wb, ring_wb_done, 0, 3, 0)
    for d in (1, 3, 2):
        arrived(act_slot.at[slot_of(d), mine, :], s_col.at[1, d], r_col.at[1, d])
        share_act(d)
    pass_on(ring_wb, ring_wb_done, 0, 3, 1)

    def edges(slots, rows, prev, nxt, n):
        for w in range(2):
            lo = slots.at[0, pl.ds(w * rows, EDGE), :]
            hi = slots.at[3, pl.ds(w * rows + rows - EDGE, EDGE), :]
            start(hi, prev.at[w], s_edge.at[n, w], r_edge.at[n, w], at_col(1))
            start(lo, nxt.at[w], s_edge.at[n, 2 + w], r_edge.at[n, 2 + w], at_col(-1))

    def edges_done(prev, nxt, n):
        for w in range(2):
            arrived(prev.at[w], s_edge.at[n, w], r_edge.at[n, w])
            arrived(nxt.at[w], s_edge.at[n, 2 + w], r_edge.at[n, 2 + w])

    is_first = jnp.where(col == 0, 0.0, 1.0).astype(F32)
    is_last = jnp.where(col == 31, 0.0, 1.0).astype(F32)

    def lay(slots, rows, prev, nxt, where):
        tiles = where.shape[1]
        for w in range(2):
            for t in range(tiles):
                lanes = slice(t * 128, (t + 1) * 128)
                where[w, t, 0:EDGE, :] = prev[w, :, lanes].astype(F32) * is_first
                for z in range(NZ):
                    at = EDGE + z * rows
                    where[w, t, at : at + rows, :] = slots[z, w * rows : (w + 1) * rows, lanes].astype(F32)
                at = EDGE + NZ * rows
                where[w, t, at : at + EDGE, :] = nxt[w, :, lanes].astype(F32) * is_last

    def pooled_taps(where, rows):
        tiles = where.shape[1]
        parts = [[[where[w, t, pl.ds(EDGE + d, rows, stride=2), :] for t in range(tiles)] for w in range(2)]
                 for d in range(-2, 4)]
        out = []
        for k in range(5):
            wins = []
            for w in range(2):
                wins.append(jnp.concatenate(
                    [((parts[k][w][t] + parts[k + 1][w][t]) * 0.5).astype(BF) for t in range(tiles)], axis=1))
            out.append(jnp.concatenate(wins, axis=0))
        return out

    def shifted(where, rows):
        tiles = where.shape[1]
        return [
            jnp.concatenate([
                jnp.concatenate([where[w, t, EDGE + d : EDGE + d + rows, :].astype(BF) for t in range(tiles)], axis=1)
                for w in range(2)], axis=0)
            for d in (-1, 0, 1)
        ]

    def back_conv(before, here, after, weight, rows, where):
        none = jnp.zeros((2 * rows, WIDE - TAPS), BF)
        even = jnp.concatenate([after, here, here, before, before, none], axis=1)
        odd = jnp.concatenate([after, after, here, here, before, none], axis=1)
        total = dot_t(jnp.concatenate([even, odd], axis=0), weight[...]) * 0.5
        even, odd = total[0 : 2 * rows], total[2 * rows : 4 * rows]
        for w in range(2):
            for t in range(where.shape[1]):
                lanes = slice(t * 128, (t + 1) * 128)
                where[w, t, pl.ds(0, rows, stride=2), :] = even[w * rows : (w + 1) * rows, lanes]
                where[w, t, pl.ds(1, rows, stride=2), :] = odd[w * rows : (w + 1) * rows, lanes]

    pass_on(ring_wb, ring_wb_done, 1, 3, 0)
    pass_on(ring_wa, ring_wa_done, 0, 1, 0)
    for d in (1, 2, 3):
        arrived(g_slot.at[slot_of(d)], s_col.at[0, d], r_col.at[0, d])
    edges(g_slot, 16, g_prev, g_next, 0)
    pass_on(ring_wb, ring_wb_done, 1, 3, 1)
    for d in range(NZ):
        arrived(act_slot.at[slot_of(d), others, :], s_af.at[d], r_af.at[d])
    edges(act_slot, 64, act_prev, act_next, 1)
    pass_on(ring_wb, ring_wb_done, 2, 3, 0)
    edges_done(g_prev, g_next, 0)
    lay(g_slot, 16, g_prev, g_next, g_rows)
    edges_done(act_prev, act_next, 1)
    lay(act_slot, 64, act_prev, act_next, act_rows)
    for k, tap in enumerate(pooled_taps(act_rows, 128)):
        taps_a[k, :, 0:384] = tap
    pass_on(ring_wa, ring_wa_done, 0, 1, 1)
    for way in (0, 1):
        ring_wa_done(1, way, way)

    total = dot(taps_a[0], whole_a[:, 0:384])
    for k in range(1, 5):
        total += dot(taps_a[k], whole_a[:, k * 384 : (k + 1) * 384])
    for w in range(2):
        acc_a[w] = total[w * 128 : (w + 1) * 128]
    for z in range(NZ):
        for w in range(2):
            mid_send[z, w * 32 : (w + 1) * 32, :] = total[w * 128 + z * 32 : w * 128 + (z + 1) * 32].astype(BF)
    for d in (1, 2, 3):
        t = (zh + d) % NZ
        start(mid_send.at[t], mid_recv.at[zh], s_col.at[2, d], r_col.at[2, d], at_z(d))

    pass_on(ring_wb, ring_wb_done, 2, 3, 1)
    for way in (0, 1):
        ring_wb_done(3, way, way)
    before, here, after = shifted(g_rows, 64)
    back_conv(before, here, after, whole_b, 64, back_rows)
    def to_twin(where, per, send, recv, n):
        for z in range(NZ):
            for b in range(2):
                for w in range(2):
                    piece = where[w, b * 2 + 1 - core, z * per : (z + 1) * per, :]
                    send[z * 2 + b, w * per : (w + 1) * per, :] = piece.astype(BF)
        start(send, recv, s_tw.at[n], r_tw.at[n], twin)

    def from_twin(where, per, recv, send, n):
        arrived(recv, s_tw.at[n], r_tw.at[n])
        for z in range(NZ):
            for b in range(2):
                for w in range(2):
                    piece = where[w, b * 2 + core, z * per : (z + 1) * per, :]
                    rows = slice(w * per, (w + 1) * per)
                    send[z * 2 + b, rows, :] = (piece + recv[z * 2 + b, rows, :].astype(F32)).astype(BF)

    def scatter(src, dst, ssem, rsem):
        @pl.loop(1, 8)
        def _(d):
            tz, tb = (zh + d // 2) % NZ, (zl + d % 2) % 2
            pltpu.make_async_remote_copy(
                src_ref=src.at[tz * 2 + tb], dst_ref=dst.at[own8], send_sem=ssem.at[d], recv_sem=rsem.at[d],
                device_id=(col * NZ + tz, tb * 2 + core), device_id_type=MESH,
            ).start()

        dst[own8] = src[own8]

    def scattered(dst, ssem, rsem):
        @pl.loop(1, 8)
        def _(d):
            arrived(dst.at[((zh - d // 2 + NZ) % NZ) * 2 + (zl - d % 2 + 2) % 2], ssem.at[d], rsem.at[d])

    def scatter_sent(src, ssem, rsem):
        @pl.loop(1, 8)
        def _(d):
            pltpu.make_async_remote_copy(
                src_ref=src.at[0], dst_ref=src.at[0], send_sem=ssem.at[d], recv_sem=rsem.at[d],
                device_id=(seq, ch), device_id_type=MESH,
            ).wait_send()

    def to_row(v):
        wide = jnp.broadcast_to(v, (v.shape[0], 128))
        if v.shape[0] < 128:
            wide = jnp.concatenate([wide, jnp.zeros((128 - v.shape[0], 128), F32)], axis=0)
        return jnp.transpose(wide)[0:8]

    def to_column(v, rows):
        return jnp.transpose(jnp.concatenate([v] * 16, axis=0))[0:rows]

    def two_shares(recv):
        return jnp.concatenate(
            [recv[z * 2].astype(F32) + recv[z * 2 + 1].astype(F32) for z in range(NZ)], axis=1)

    to_twin(back_rows, 32, back_over, back_twin, 0)
    from_twin(back_rows, 32, back_twin, back_send, 0)
    scatter(back_send, back_recv, s_b, r_b)

    gain_b = jnp.concatenate([gain_b, jnp.zeros((1, 128), F32)], axis=1)
    hot = one_hot_lanes(lanes_ref[1:2, 0:512] + ch * 352, CMID + 128)
    gain_b_own = spread_gain(gain_b, hot)

    for d in (1, 2, 3):
        arrived(mid_recv.at[slot_of(d)], s_col.at[2, d], r_col.at[2, d])
    total = jnp.concatenate([acc_a[w, pl.ds(pl.multiple_of(zh * 32, 32), 32), :] for w in range(2)], axis=0)
    for d in (1, 2, 3):
        total += mid_recv[slot_of(d)].astype(F32)
    mid = (total + bias_pad[0:1, :]).astype(BF)
    mid_f = mid.astype(F32)
    squares = jnp.sum(mid_f * mid_f, axis=-1, keepdims=True)
    mid_wide = jnp.concatenate([mid, jnp.zeros((64, 128), BF)], axis=1)
    mid_own = dot(mid_wide, one_hot_lanes(lanes_ref[1:2, 0:512], 512))
    lane = lax.broadcasted_iota(jnp.int32, (64, 128), 1)
    high, middle, low = three_parts(squares)
    for z in range(NZ):
        piece = mid_own[:, z * 128 : (z + 1) * 128]
        piece = jnp.where(lane == 96, high, jnp.where(lane == 97, middle, jnp.where(lane == 98, low, piece)))
        x_send[z] = piece.astype(BF)
    for d in (1, 2, 3):
        start(x_send.at[zh], x_recv.at[own], s_x.at[d], r_x.at[d], at_c(d))
    x_recv[own] = x_send[zh]
    far = [(dz, db) for dz in (2, 1, 3) for db in (0, 1)]
    for n, (dz, db) in enumerate(far):
        tz, tb = (zh + dz) % NZ, (zl + db) % 2
        start(x_send.at[tz], x_recv.at[own], s_x.at[4 + n], r_x.at[4 + n], (col * NZ + tz, tb * 2 + core))

    def x_slot(dz, db, side):
        return x_recv.at[slot_of(dz) * NC + ((zl - db + 2) % 2) * 2 + side]

    hot = one_hot_lanes(lanes_ref[2:3, 0:512] + zh * 11, CMID + 128)
    gain_b_all = spread_gain(gain_b, hot)

    hot = one_hot_rows(rows_ref[:, 0:1], 512)
    for k in range(4):
        turned_a[:, k * 512 : (k + 1) * 512] = dot(hot, whole_a[:, k * 512 : (k + 1) * 512]).astype(BF)

    def inverse(z):
        total = jnp.zeros((64, 1), F32)
        for c in range(NC):
            part = x_recv[z * NC + c, :, 96:99].astype(F32)
            total += jnp.sum(part, axis=-1, keepdims=True)
        return lax.rsqrt(total * (1.0 / CMID) + EPS)

    for d in (1, 2, 3):
        arrived(x_recv.at[zh * NC + (ch - d + NC) % NC], s_x.at[d], r_x.at[d])
    inv_b = inverse(zh)
    normed_b = mid_own * inv_b
    factor_b = gelu_slope(normed_b * gain_b_own) * gain_b_own
    scattered(back_recv, s_b, r_b)
    grad_n = two_shares(back_recv) * factor_b
    in_send[...] = to_row(jnp.sum(grad_n * normed_b, axis=-1, keepdims=True))
    for d in (1, 2, 3):
        start(in_send, in_recv.at[ch], s_col.at[3, d], r_col.at[3, d], at_c(d))

    for n, (dz, db) in enumerate(far):
        arrived(x_slot(dz, db, core), s_x.at[4 + n], r_x.at[4 + n])
        start(x_slot(dz, db, core), x_slot(dz, db, core), s_x.at[10 + n], r_x.at[10 + n], twin)
    inner = in_send[...]
    for d in (1, 2, 3):
        at = (ch - d + NC) % NC
        arrived(in_recv.at[at], s_col.at[3, d], r_col.at[3, d])
        inner += in_recv[at]
    inner = jnp.concatenate([to_column(inner * (1.0 / CMID), 64)] * 4, axis=1)
    grad_mid = (inv_b * (grad_n - normed_b * inner)).astype(BF)
    gm_slot[zh] = dot(grad_mid, one_hot_rows(rows_ref[:, 3:4], 384)).astype(BF)
    for d in (1, 2, 3):
        start(gm_slot.at[zh], gm_slot.at[zh], s_col.at[4, d], r_col.at[4, d], at_z(d))

    def last_rows(z, w):
        return pltpu.make_async_remote_copy(
            src_ref=gm_slot.at[3, pl.ds(w * 32 + 16, EDGE), :], dst_ref=gm_prev.at[w], send_sem=s_gm.at[0, z, w],
            recv_sem=s_edge_gm.at[0, w], device_id=beside(1, z), device_id_type=MESH)

    def first_rows(z, w):
        return pltpu.make_async_remote_copy(
            src_ref=gm_slot.at[0, pl.ds(w * 32, EDGE), :], dst_ref=gm_next.at[w], send_sem=s_gm.at[1, z, w],
            recv_sem=s_edge_gm.at[1, w], device_id=beside(-1, z), device_id_type=MESH)

    @pl.when(zh == NZ - 1)
    def _():
        for z in range(NZ):
            for w in range(2):
                last_rows(z, w).start()

    @pl.when(zh == 0)
    def _():
        for z in range(NZ):
            for w in range(2):
                first_rows(z, w).start()

    hot = one_hot_lanes(lanes_ref[3:4, 0:512] + ch * 320, CIN)
    gain_a_own = spread_gain(gain_a, hot)
    feat_bf = feat_ref[...].reshape(128, CIN)
    inv_a = inverse_a(feat_bf.astype(F32))
    feat_own = dot(feat_bf, hot)
    normed_a = feat_own * inv_a
    factor_a = gelu_slope(normed_a * gain_a_own) * gain_a_own

    for n, (dz, db) in enumerate(far):
        arrived(x_slot(dz, db, 1 - core), s_x.at[10 + n], r_x.at[10 + n])
    for z in range(NZ):
        inv = inverse(z)
        values = jnp.concatenate([x_recv[z * NC + c].astype(F32) for c in range(NC)], axis=1)
        b_slot[z] = gelu_tanh(values * inv * gain_b_all).astype(BF)
    edges(b_slot, 32, b_prev, b_next, 2)

    for d in (1, 2, 3):
        arrived(gm_slot.at[slot_of(d)], s_col.at[4, d], r_col.at[4, d])

    for w in range(2):
        arrived(gm_prev.at[w], s_gm.at[0, 0, w], s_edge_gm.at[0, w])
        arrived(gm_next.at[w], s_gm.at[1, 0, w], s_edge_gm.at[1, w])
    lay(gm_slot, 32, gm_prev, gm_next, gm_rows)
    before, here, after = shifted(gm_rows, 128)
    back_conv(before, here, after, turned_a, 128, out_rows)
    to_twin(out_rows, 64, out_over, out_twin, 1)
    edges_done(b_prev, b_next, 2)
    lay(b_slot, 32, b_prev, b_next, b_rows)
    taps = pooled_taps(b_rows, 64)
    from_twin(out_rows, 64, out_twin, out_send, 1)
    scatter(out_send, out_recv, s_o, r_o)

    total = dot(taps[0], whole_b[:, 0:384])
    for k in range(1, 5):
        total += dot(taps[k], whole_b[:, k * 384 : (k + 1) * 384])
    for w in range(2):
        acc_b[w] = total[w * 64 : (w + 1) * 64]
    for z in range(NZ):
        for w in range(2):
            pool_send[z, w * 16 : (w + 1) * 16, :] = total[w * 64 + z * 16 : w * 64 + (z + 1) * 16].astype(BF)


    for d in (1, 2, 3):
        t = (zh + d) % NZ
        start(pool_send.at[t], pool_recv.at[zh], s_col.at[5, d], r_col.at[5, d], at_z(d))

    for d in (1, 2, 3):
        arrived(pool_recv.at[slot_of(d)], s_col.at[5, d], r_col.at[5, d])
    total = jnp.concatenate([acc_b[w, pl.ds(pl.multiple_of(zh * 16, 16), 16), :] for w in range(2)], axis=0)
    for d in (1, 2, 3):
        total += pool_recv[slot_of(d)].astype(F32)
    pooled_ref[...] = (total + bias_b_ref[...].reshape(1, 384)).astype(BF).reshape(2, 16, 384)

    scattered(out_recv, s_o, r_o)
    grad_n = two_shares(out_recv) * factor_a
    ia_send[...] = to_row(jnp.sum(grad_n * normed_a, axis=-1, keepdims=True))
    for d in (1, 2, 3):
        start(ia_send, ia_recv.at[ch], s_col.at[6, d], r_col.at[6, d], at_c(d))
    hot = one_hot_rows(rows_ref[:, 4:5], 384)
    inner = ia_send[...]
    for d in (1, 2, 3):
        at = (ch - d + NC) % NC
        arrived(ia_recv.at[at], s_col.at[6, d], r_col.at[6, d])
        inner += ia_recv[at]
    inner = jnp.concatenate([to_column(inner * (1.0 / CIN), 128)] * 4, axis=1)
    grad = (inv_a * (grad_n - normed_a * inner)).astype(BF)
    grad_ref[...] = dot(grad, hot)[:, 0:320].astype(BF).reshape(2, 64, 320)

    for copy in pending:
        copy.wait_send()
    scatter_sent(back_send, s_b, r_b)
    scatter_sent(out_send, s_o, r_o)

    @pl.when(zh == NZ - 1)
    def _():
        for z in range(NZ):
            for w in range(2):
                last_rows(z, w).wait_send()

    @pl.when(zh == 0)
    def _():
        for z in range(NZ):
            for w in range(2):
                first_rows(z, w).wait_send()


def per_device(dna_features, gain_a, conv_a, bias_a, gain_b, conv_b, bias_b, grad_out):
    lanes, rows = index_tables()
    dma = pltpu.SemaphoreType.DMA
    vmem = pltpu.VMEM
    pooled, grad = pl.pallas_call(
        kernel,
        out_shape=(jax.ShapeDtypeStruct((2, 16, 384), BF), jax.ShapeDtypeStruct((2, 64, 320), BF)),
        in_specs=[pl.BlockSpec(memory_space=pl.ANY)] * 10,
        out_specs=[pl.BlockSpec(memory_space=vmem)] * 2,
        scratch_shapes=[
            vmem((2, 64, CIN), BF), vmem((5, 10, 352), BF), vmem((5, 11, 384), BF), vmem((CIN,), F32), vmem((352,), F32),
            vmem((CMID,), F32), vmem((384,), F32), vmem((2, 16, 384), BF), vmem((8, 1536), jnp.int32), vmem((512, 8), jnp.int32),
            vmem((8, 64, 384), BF), vmem((4, 64, 384), BF), vmem((512, WIDE), BF), vmem((512, WIDE), BF),
            vmem((512, WIDE), BF), vmem((8, 384), F32),
            vmem((4, 128, 384), BF), vmem((2, 16, 384), BF), vmem((2, 16, 384), BF), vmem((2, 3, 288, 128), F32),
            vmem((5, 256, 512), BF), vmem((4, 64, 384), BF),
            vmem((4, 32, 384), BF), vmem((32, 384), BF), vmem((2, 16, 384), BF), vmem((2, 16, 384), BF), vmem((2, 3, 96, 128), F32),
            vmem((2, 4, 128, 128), F32), vmem((8, 64, 128), BF), vmem((8, 64, 128), BF), vmem((8, 64, 128), BF),
            vmem((8, 64, 128), BF), vmem((2, 128, 384), F32), vmem((4, 64, 384), BF), vmem((4, 64, 384), BF),
            vmem((4, 64, 128), BF), vmem((16, 64, 128), BF), vmem((4, 64, 512), BF), vmem((2, 16, 512), BF),
            vmem((2, 16, 512), BF), vmem((2, 4, 160, 128), F32),
            vmem((4, 32, 384), BF), vmem((4, 32, 384), BF), vmem((2, 64, 384), F32),
            vmem((8, 128), F32), vmem((4, 8, 128), F32), vmem((4, 64, 384), BF), vmem((2, 16, 384), BF),
            vmem((2, 16, 384), BF), vmem((2, 3, 160, 128), F32),
            vmem((2, 4, 256, 128), F32), vmem((8, 128, 128), BF), vmem((8, 128, 128), BF), vmem((8, 128, 128), BF),
            vmem((8, 128, 128), BF),
            vmem((8, 128), F32), vmem((4, 8, 128), F32),
            dma((2, 4)), dma((2, 4)), dma((4,)), dma((4,)), dma((2, 4, 2)), dma((2, 4, 2)), dma((2, 2, 2)), dma((2, 2, 2)),
            dma((7, 4)), dma((7, 4)), dma((4, 4)), dma((4, 4)),
            dma((16,)), dma((16,)), dma((16,)), dma((16,)), dma((16,)), dma((16,)), dma((10,)), dma((2, 4, 2)), dma((2, 2)), dma((4,)), dma((4,)),
            dma((2,)), dma((2,)),
        ],
        compiler_params=pltpu.CompilerParams(
            collective_id=0, has_side_effects=True, vmem_limit_bytes=60 * 1024 * 1024
        ),
        cost_estimate=pl.CostEstimate(flops=3_000_000_000, bytes_accessed=8_000_000, transcendentals=800_000),
    )(
        dna_features, conv_a, conv_b, gain_a, bias_a, gain_b, bias_b, grad_out, jnp.asarray(lanes), jnp.asarray(rows),
    )
    return pooled, grad


def solution(mesh):
    return jax.shard_map(
        per_device,
        mesh=mesh,
        in_specs=(
            P(None, "seq", None), P(), P(None, "seq", "ch"), P("ch"), P(), P(None, "seq", "ch"), P("ch"),
            P(None, "seq", "ch"),
        ),
        out_specs=(P(None, "seq", "ch"), P(None, "seq", "ch")),
        check_vma=False,
    )
```

```python
import math

import jax
import jax.numpy as jnp
import numpy as np
from jax import lax
from jax.experimental import pallas as pl
from jax.experimental.pallas import tpu as pltpu
from jax.sharding import PartitionSpec as P

EPS = 1e-06
ROOT = math.sqrt(2.0 / math.pi)
MESH = pl.DeviceIdType.MESH
BF = jnp.bfloat16
F32 = jnp.float32
NY, NX, NZ, NC = 8, 4, 4, 4
CIN, CMID = 1280, 1408
EDGE = 16
WIDE = 2048
TAPS = 5 * 384


def gelu_tanh(z):
    return 0.5 * z * (1.0 + jnp.tanh(ROOT * (z + 0.044715 * z * z * z)))


def gelu_slope(z):
    t = jnp.tanh(ROOT * (z + 0.044715 * z * z * z))
    return 0.5 * (1.0 + t) + 0.5 * z * (1.0 - t * t) * ROOT * (1.0 + 3.0 * 0.044715 * z * z)


def index_tables():
    lanes = np.full((8, 1536), -100000, np.int32)
    rows = np.full((512, 8), -100000, np.int32)
    for zb in range(NZ):
        for xb in range(NX):
            for yb in range(NY):
                for i in range(10):
                    lanes[0, zb * 384 + xb * 80 + yb * 10 + i] = ((yb * 4 + xb) * 4 + zb) * 10 + i
            for yy in range(2):
                for i in range(11):
                    q = yy * 48 + xb * 11 + i
                    here = ((yy * 4 + xb) * 4 + zb) * 11 + i
                    lanes[1, zb * 128 + q] = here
                    rows[zb * 128 + q, 3] = here
                for i in range(10):
                    q = xb * 20 + yy * 10 + i
                    here = ((yy * 4 + xb) * 4 + zb) * 10 + i
                    lanes[3, zb * 128 + q] = here
                    rows[zb * 128 + q, 4] = here
    for cb in range(NC):
        for xb in range(NX):
            for yy in range(2):
                for i in range(11):
                    lanes[2, cb * 128 + yy * 48 + xb * 11 + i] = (((cb * 2 + yy) * 4 + xb) * 4) * 11 + i
                for i in range(10):
                    rows[cb * 128 + xb * 20 + yy * 10 + i, 0] = xb * 80 + (cb * 2 + yy) * 10 + i
    for k in range(5):
        for yb in range(NY):
            for i in range(10):
                rows[k * 80 + yb * 10 + i, 1] = yb * 64 + k * 10 + i
        for xb in range(NX):
            for i in range(11):
                rows[k * 48 + xb * 11 + i, 2] = xb * 64 + k * 11 + i
    return lanes, rows


def dot(a, b):
    return lax.dot_general(a, b, (((1,), (0,)), ((), ())), preferred_element_type=F32)


def dot_t(a, b):
    return lax.dot_general(a, b, (((1,), (1,)), ((), ())), preferred_element_type=F32)


def one_hot_lanes(table, depth):
    row = lax.broadcasted_iota(jnp.int32, (depth, table.shape[1]), 0)
    return jnp.where(row == table, 1.0, 0.0).astype(BF)


def one_hot_rows(table, depth):
    col = lax.broadcasted_iota(jnp.int32, (table.shape[0], depth), 1)
    return jnp.where(col == table, 1.0, 0.0).astype(BF)


def three_parts(v):
    high = v.astype(BF).astype(F32)
    rest = v - high
    middle = rest.astype(BF).astype(F32)
    return high, middle, rest - middle


def spread_gain(gain, hot):
    high, middle, low = three_parts(gain)
    row = lax.broadcasted_iota(jnp.int32, (16, gain.shape[1]), 0)
    stack = jnp.where(row == 0, high, jnp.where(row == 1, middle, jnp.where(row == 2, low, 0.0)))
    return jnp.sum(dot(stack.astype(BF), hot), axis=0, keepdims=True)


def kernel(
    feat_in, wa_in, wb_in, gain_a_in, bias_a_in, gain_b_in, bias_b_in, g_in, lanes_in, rows_in,
    pooled_ref, grad_ref,
    feat_ref, wa_ref, wb_ref, gain_a_ref, bias_a_ref, gain_b_ref, bias_b_ref, g_ref, lanes_ref, rows_ref,
    first_a, first_b, whole_a, turned_a, whole_b, bias_pad,
    act_slot, act_prev, act_next, act_rows, taps_a, send_act,
    g_slot, g_send, g_prev, g_next, g_rows,
    back_rows, back_over, back_twin, back_send, back_recv,
    acc_a, mid_send, mid_recv,
    x_send, x_recv, b_slot, b_prev, b_next, b_rows,
    pool_send, pool_recv, acc_b,
    in_send, in_recv, gm_slot, gm_prev, gm_next, gm_rows,
    out_rows, out_over, out_twin, out_send, out_recv, ia_send, ia_recv,
    s_fa, r_fa, s_fb, r_fb, s_wb, r_wb, s_wa, r_wa, s_col, r_col, s_edge, r_edge,
    s_b, r_b, s_x, r_x, s_o, r_o, s_in, s_gm, s_edge_gm, s_af, r_af, s_tw, r_tw,
):
    seq = lax.axis_index("seq")
    ch = lax.axis_index("ch")
    zh = seq % NZ
    col = seq // NZ
    xi = col % NX
    yi = col // NX
    own = zh * NC + ch
    core = ch % 2
    zl = ch // 2
    twin = (seq, ch + 1 - 2 * core)
    own8 = zh * 2 + zl
    pending = []
    loads = [
        pltpu.make_async_copy(src, dst, s_in.at[i])
        for i, (src, dst) in enumerate((
            (wa_in, wa_ref), (wb_in, wb_ref), (rows_in, rows_ref), (lanes_in, lanes_ref), (feat_in, feat_ref),
            (gain_a_in, gain_a_ref), (g_in, g_ref), (bias_a_in, bias_a_ref), (gain_b_in, gain_b_ref),
            (bias_b_in, bias_b_ref),
        ))
    ]
    for load in loads:
        load.start()

    def start(src, dst, ssem, rsem, dev):
        copy = pltpu.make_async_remote_copy(
            src_ref=src, dst_ref=dst, send_sem=ssem, recv_sem=rsem, device_id=dev, device_id_type=MESH
        )
        copy.start()
        pending.append(copy)

    def arrived(dst, ssem, rsem):
        pltpu.make_async_remote_copy(
            src_ref=dst, dst_ref=dst, send_sem=ssem, recv_sem=rsem, device_id=(seq, ch), device_id_type=MESH
        ).wait_recv()

    def at_y(d):
        return ((((yi + d + NY) % NY) * NX + xi) * NZ + zh, ch)

    def at_x(d):
        return ((yi * NX + (xi + d + NX) % NX) * NZ + zh, ch)

    def at_z(d):
        return (col * NZ + (zh + d) % NZ, ch)

    def at_c(d):
        return (seq, (ch + d) % NC)

    def at_col(d):
        return (((col + d + 32) % 32) * NZ + zh, ch)

    def member(d):
        tz, tc = (zh + d // NC) % NZ, (ch + d % NC) % NC
        return tz * NC + tc, (col * NZ + tz, tc)

    def source(d):
        return ((zh - d // NC + NZ) % NZ) * NC + (ch - d % NC + NC) % NC

    def beside(way, z):
        return (((col + way + 32) % 32) * NZ + z, ch)

    barrier = pltpu.get_barrier_semaphore()

    def greet(dev):
        pl.semaphore_signal(barrier, inc=1, device_id=dev, device_id_type=MESH)

    for d in (1, 2, 3):
        greet(at_x(d))
    for d in (-1, 1):
        greet(at_y(d))
        greet(at_y(2 * d))
        for z in range(NZ):
            greet(beside(d, z))

    @pl.loop(1, 16)
    def _(d):
        greet(member(d)[1])

    for load in loads:
        load.wait()
    gain_a = gain_a_ref[...].reshape(1, CIN)
    gain_b = gain_b_ref[...].reshape(1, CMID)

    first_a[yi] = jnp.zeros((64, 384), BF)
    bias_pad[...] = jnp.zeros((8, 384), F32)
    bias_pad[0:1, 0:352] = bias_a_ref[...].reshape(1, 352)
    pack_a = jnp.zeros((64, 352), F32)
    pack_b = jnp.zeros((64, 384), F32)
    for k in range(5):
        pick = lax.broadcasted_iota(jnp.int32, (64, 10), 0) == lax.broadcasted_iota(jnp.int32, (64, 10), 1) + 10 * k
        pack_a += dot(jnp.where(pick, 1.0, 0.0).astype(BF), wa_ref[k])
        pick = lax.broadcasted_iota(jnp.int32, (64, 11), 0) == lax.broadcasted_iota(jnp.int32, (64, 11), 1) + 11 * k
        pack_b += dot(jnp.where(pick, 1.0, 0.0).astype(BF), wb_ref[k])
    first_a[yi, :, 0:352] = pack_a.astype(BF)
    first_b[xi] = pack_b.astype(BF)
    whole_a[320:512, :] = jnp.zeros((192, WIDE), BF)
    whole_a[0:320, TAPS:WIDE] = jnp.zeros((320, WIDE - TAPS), BF)
    whole_b[:, TAPS:WIDE] = jnp.zeros((512, WIDE - TAPS), BF)
    for c in range(NC):
        whole_b[c * 128 + 96 : c * 128 + 128, 0:TAPS] = jnp.zeros((32, TAPS), BF)
    taps_a[:, :, 384:512] = jnp.zeros((5, 256, 128), BF)
    pl.semaphore_wait(barrier, 30)

    parts = ((0, 1152), (1152, 768))

    def first_block(d, at=0, n=64):
        return first_a.at[(yi + d + NY) % NY, pl.ds(at, n), :]

    hops = (
        ((0, 1, 0, 64), (0, -1, 0, 64), (0, 2, 0, 64), (0, -2, 0, 64)),
        ((-2, 1, 0, 64), (2, -1, 0, 64), (-2, 2, 0, 32), (2, -2, 32, 32)),
    )

    def send_first(step):
        for n, (b, to, at, rows) in enumerate(hops[step]):
            ref = first_block(b, at, rows)
            start(ref, ref, s_fa.at[step, n], r_fa.at[step, n], at_y(to))

    def first_done(step, which):
        for n in which:
            b, to, at, rows = hops[step][n]
            arrived(first_block(b - to, at, rows), s_fa.at[step, n], r_fa.at[step, n])

    def place_a(b):
        return pl.multiple_of(b * 80, 16)

    def place_b(b):
        return pl.multiple_of((b // 2) * 128 + (b % 2) * 48, 16)

    def ring_wb(r, way, c):
        sign = 1 if way == 0 else -1
        ref = whole_b.at[pl.ds(place_b((yi - sign * r + NY) % NY), 48), pl.ds(*parts[c])]
        start(ref, ref, s_wb.at[way, r, c], r_wb.at[way, r, c], at_y(sign))

    def ring_wb_done(r, way, c):
        sign = 1 if way == 0 else -1
        ref = whole_b.at[pl.ds(place_b((yi - sign * (r + 1) + NY) % NY), 48), pl.ds(*parts[c])]
        arrived(ref, s_wb.at[way, r, c], r_wb.at[way, r, c])

    def ring_wa(r, way, c):
        sign = 1 if way == 0 else -1
        ref = whole_a.at[pl.ds(place_a((xi - sign * r + NX) % NX), 80), pl.ds(*parts[c])]
        start(ref, ref, s_wa.at[way, r, c], r_wa.at[way, r, c], at_x(sign))

    def ring_wa_done(r, way, c):
        sign = 1 if way == 0 else -1
        ref = whole_a.at[pl.ds(place_a((xi - sign * (r + 1) + NX) % NX), 80), pl.ds(*parts[c])]
        arrived(ref, s_wa.at[way, r, c], r_wa.at[way, r, c])

    def pass_on(ring, done, r, last, rank):
        for way in (0, 1):
            c = way if rank == 0 else 1 - way
            done(r, way, c)
            if r + 1 < last or (r + 1 == last and rank == 0):
                ring(r + 1, way, c)

    send_first(0)
    for d in (1, 2, 3):
        start(first_b.at[xi], first_b.at[xi], s_fb.at[d], r_fb.at[d], at_x(d))

    def slot_of(d):
        return (zh - d + NZ) % NZ

    def inverse_a(v):
        return lax.rsqrt(jnp.sum(v * v, axis=-1, keepdims=True) * (1.0 / CIN) + EPS)

    feat = feat_ref[core].astype(F32)
    act = gelu_tanh(feat * inverse_a(feat) * gain_a).astype(BF)
    mine = pl.ds(pl.multiple_of(core * 64, 64), 64)
    others = pl.ds(pl.multiple_of(64 - core * 64, 64), 64)

    def subset(d):
        t = (zh + d) % NZ
        hot = one_hot_lanes(lanes_ref[0:1, pl.ds(pl.multiple_of(t * 384, 128), 384)], CIN)
        part = dot(act, hot).astype(BF)
        if d == 0:
            act_slot[zh, mine, :] = part
            share_act(0)
        else:
            send_act[d] = part
            start(send_act.at[d], act_slot.at[zh, mine, :], s_col.at[1, d], r_col.at[1, d], at_z(d))

    def share_act(d):
        ref = act_slot.at[slot_of(d), mine, :]
        start(ref, ref, s_af.at[d], r_af.at[d], twin)

    subset(2)
    first_done(0, (2, 3))
    send_first(1)

    for d in (1, 2, 3):
        arrived(first_b.at[(xi - d + NX) % NX], s_fb.at[d], r_fb.at[d])
    hot_b = one_hot_rows(rows_ref[0:240, 2:3], 256)
    block = dot(hot_b, first_b[...].reshape(256, 384)).astype(BF)
    for k in range(5):
        whole_b[pl.ds(place_b(yi), 48), k * 384 : (k + 1) * 384] = block[k * 48 : (k + 1) * 48]
    for rank in (0, 1):
        for way in (0, 1):
            ring_wb(0, way, way if rank == 0 else 1 - way)
    subset(1)
    subset(3)
    subset(0)
    g_own = g_ref[...].reshape(32, 384)
    g_slot[zh] = g_own
    g_send[...] = g_own
    for d in (1, 2, 3):
        start(g_send, g_slot.at[zh], s_col.at[0, d], r_col.at[0, d], at_z(d))
    hot_a = one_hot_rows(rows_ref[0:400, 1:2], 512)
    first_done(0, (0, 1))
    first_done(1, range(4))
    block = dot(hot_a, first_a[...].reshape(512, 384)).astype(BF)
    for k in range(5):
        whole_a[pl.ds(place_a(xi), 80), k * 384 : (k + 1) * 384] = block[k * 80 : (k + 1) * 80]
    for rank in (0, 1):
        for way in (0, 1):
            ring_wa(0, way, way if rank == 0 else 1 - way)
    pass_on(ring_wb, ring_wb_done, 0, 3, 0)
    for d in (1, 3, 2):
        arrived(act_slot.at[slot_of(d), mine, :], s_col.at[1, d], r_col.at[1, d])
        share_act(d)
    pass_on(ring_wb, ring_wb_done, 0, 3, 1)

    def edges(slots, rows, prev, nxt, n):
        for w in range(2):
            lo = slots.at[0, pl.ds(w * rows, EDGE), :]
            hi = slots.at[3, pl.ds(w * rows + rows - EDGE, EDGE), :]
            start(hi, prev.at[w], s_edge.at[n, w], r_edge.at[n, w], at_col(1))
            start(lo, nxt.at[w], s_edge.at[n, 2 + w], r_edge.at[n, 2 + w], at_col(-1))

    def edges_done(prev, nxt, n):
        for w in range(2):
            arrived(prev.at[w], s_edge.at[n, w], r_edge.at[n, w])
            arrived(nxt.at[w], s_edge.at[n, 2 + w], r_edge.at[n, 2 + w])

    is_first = jnp.where(col == 0, 0.0, 1.0).astype(F32)
    is_last = jnp.where(col == 31, 0.0, 1.0).astype(F32)

    def lay(slots, rows, prev, nxt, where):
        tiles = where.shape[1]
        for w in range(2):
            for t in range(tiles):
                lanes = slice(t * 128, (t + 1) * 128)
                where[w, t, 0:EDGE, :] = prev[w, :, lanes].astype(F32) * is_first
                for z in range(NZ):
                    at = EDGE + z * rows
                    where[w, t, at : at + rows, :] = slots[z, w * rows : (w + 1) * rows, lanes].astype(F32)
                at = EDGE + NZ * rows
                where[w, t, at : at + EDGE, :] = nxt[w, :, lanes].astype(F32) * is_last

    def pooled_taps(where, rows):
        tiles = where.shape[1]
        parts = [[[where[w, t, pl.ds(EDGE + d, rows, stride=2), :] for t in range(tiles)] for w in range(2)]
                 for d in range(-2, 4)]
        out = []
        for k in range(5):
            wins = []
            for w in range(2):
                wins.append(jnp.concatenate(
                    [((parts[k][w][t] + parts[k + 1][w][t]) * 0.5).astype(BF) for t in range(tiles)], axis=1))
            out.append(jnp.concatenate(wins, axis=0))
        return out

    def shifted(where, rows):
        tiles = where.shape[1]
        return [
            jnp.concatenate([
                jnp.concatenate([where[w, t, EDGE + d : EDGE + d + rows, :].astype(BF) for t in range(tiles)], axis=1)
                for w in range(2)], axis=0)
            for d in (-1, 0, 1)
        ]

    def back_conv(before, here, after, weight, rows, where):
        none = jnp.zeros((2 * rows, WIDE - TAPS), BF)
        even = jnp.concatenate([after, here, here, before, before, none], axis=1)
        odd = jnp.concatenate([after, after, here, here, before, none], axis=1)
        total = dot_t(jnp.concatenate([even, odd], axis=0), weight[...]) * 0.5
        even, odd = total[0 : 2 * rows], total[2 * rows : 4 * rows]
        for w in range(2):
            for t in range(where.shape[1]):
                lanes = slice(t * 128, (t + 1) * 128)
                where[w, t, pl.ds(0, rows, stride=2), :] = even[w * rows : (w + 1) * rows, lanes]
                where[w, t, pl.ds(1, rows, stride=2), :] = odd[w * rows : (w + 1) * rows, lanes]

    pass_on(ring_wa, ring_wa_done, 0, 1, 0)
    pass_on(ring_wb, ring_wb_done, 1, 3, 0)
    for d in (1, 2, 3):
        arrived(g_slot.at[slot_of(d)], s_col.at[0, d], r_col.at[0, d])
    edges(g_slot, 16, g_prev, g_next, 0)
    pass_on(ring_wb, ring_wb_done, 1, 3, 1)
    for d in range(NZ):
        arrived(act_slot.at[slot_of(d), others, :], s_af.at[d], r_af.at[d])
    edges(act_slot, 64, act_prev, act_next, 1)
    pass_on(ring_wb, ring_wb_done, 2, 3, 0)
    edges_done(g_prev, g_next, 0)
    lay(g_slot, 16, g_prev, g_next, g_rows)
    edges_done(act_prev, act_next, 1)
    lay(act_slot, 64, act_prev, act_next, act_rows)
    for k, tap in enumerate(pooled_taps(act_rows, 128)):
        taps_a[k, :, 0:384] = tap
    pass_on(ring_wa, ring_wa_done, 0, 1, 1)
    for way in (0, 1):
        ring_wa_done(1, way, way)

    total = dot(taps_a[0], whole_a[:, 0:384])
    for k in range(1, 5):
        total += dot(taps_a[k], whole_a[:, k * 384 : (k + 1) * 384])
    for w in range(2):
        acc_a[w] = total[w * 128 : (w + 1) * 128]
    for z in range(NZ):
        for w in range(2):
            mid_send[z, w * 32 : (w + 1) * 32, :] = total[w * 128 + z * 32 : w * 128 + (z + 1) * 32].astype(BF)
    for d in (1, 2, 3):
        t = (zh + d) % NZ
        start(mid_send.at[t], mid_recv.at[zh], s_col.at[2, d], r_col.at[2, d], at_z(d))

    pass_on(ring_wb, ring_wb_done, 2, 3, 1)
    for way in (0, 1):
        ring_wb_done(3, way, way)
    before, here, after = shifted(g_rows, 64)
    back_conv(before, here, after, whole_b, 64, back_rows)
    def to_twin(where, per, send, recv, n):
        for z in range(NZ):
            for b in range(2):
                for w in range(2):
                    piece = where[w, b * 2 + 1 - core, z * per : (z + 1) * per, :]
                    send[z * 2 + b, w * per : (w + 1) * per, :] = piece.astype(BF)
        start(send, recv, s_tw.at[n], r_tw.at[n], twin)

    def from_twin(where, per, recv, send, n):
        arrived(recv, s_tw.at[n], r_tw.at[n])
        for z in range(NZ):
            for b in range(2):
                for w in range(2):
                    piece = where[w, b * 2 + core, z * per : (z + 1) * per, :]
                    rows = slice(w * per, (w + 1) * per)
                    send[z * 2 + b, rows, :] = (piece + recv[z * 2 + b, rows, :].astype(F32)).astype(BF)

    def scatter(src, dst, ssem, rsem):
        @pl.loop(1, 8)
        def _(d):
            tz, tb = (zh + d // 2) % NZ, (zl + d % 2) % 2
            pltpu.make_async_remote_copy(
                src_ref=src.at[tz * 2 + tb], dst_ref=dst.at[own8], send_sem=ssem.at[d], recv_sem=rsem.at[d],
                device_id=(col * NZ + tz, tb * 2 + core), device_id_type=MESH,
            ).start()

        dst[own8] = src[own8]

    def scattered(dst, ssem, rsem):
        @pl.loop(1, 8)
        def _(d):
            arrived(dst.at[((zh - d // 2 + NZ) % NZ) * 2 + (zl - d % 2 + 2) % 2], ssem.at[d], rsem.at[d])

    def scatter_sent(src, ssem, rsem):
        @pl.loop(1, 8)
        def _(d):
            pltpu.make_async_remote_copy(
                src_ref=src.at[0], dst_ref=src.at[0], send_sem=ssem.at[d], recv_sem=rsem.at[d],
                device_id=(seq, ch), device_id_type=MESH,
            ).wait_send()

    def to_row(v):
        wide = jnp.broadcast_to(v, (v.shape[0], 128))
        if v.shape[0] < 128:
            wide = jnp.concatenate([wide, jnp.zeros((128 - v.shape[0], 128), F32)], axis=0)
        return jnp.transpose(wide)[0:8]

    def to_column(v, rows):
        return jnp.transpose(jnp.concatenate([v] * 16, axis=0))[0:rows]

    def two_shares(recv):
        return jnp.concatenate(
            [recv[z * 2].astype(F32) + recv[z * 2 + 1].astype(F32) for z in range(NZ)], axis=1)

    to_twin(back_rows, 32, back_over, back_twin, 0)
    from_twin(back_rows, 32, back_twin, back_send, 0)
    scatter(back_send, back_recv, s_b, r_b)

    gain_b = jnp.concatenate([gain_b, jnp.zeros((1, 128), F32)], axis=1)
    hot = one_hot_lanes(lanes_ref[1:2, 0:512] + ch * 352, CMID + 128)
    gain_b_own = spread_gain(gain_b, hot)

    for d in (1, 2, 3):
        arrived(mid_recv.at[slot_of(d)], s_col.at[2, d], r_col.at[2, d])
    total = jnp.concatenate([acc_a[w, pl.ds(pl.multiple_of(zh * 32, 32), 32), :] for w in range(2)], axis=0)
    for d in (1, 2, 3):
        total += mid_recv[slot_of(d)].astype(F32)
    mid = (total + bias_pad[0:1, :]).astype(BF)
    mid_f = mid.astype(F32)
    squares = jnp.sum(mid_f * mid_f, axis=-1, keepdims=True)
    mid_wide = jnp.concatenate([mid, jnp.zeros((64, 128), BF)], axis=1)
    mid_own = dot(mid_wide, one_hot_lanes(lanes_ref[1:2, 0:512], 512))
    lane = lax.broadcasted_iota(jnp.int32, (64, 128), 1)
    high, middle, low = three_parts(squares)
    for z in range(NZ):
        piece = mid_own[:, z * 128 : (z + 1) * 128]
        piece = jnp.where(lane == 96, high, jnp.where(lane == 97, middle, jnp.where(lane == 98, low, piece)))
        x_send[z] = piece.astype(BF)
    for d in (1, 2, 3):
        start(x_send.at[zh], x_recv.at[own], s_x.at[d], r_x.at[d], at_c(d))
    x_recv[own] = x_send[zh]
    far = [(dz, db) for dz in (2, 1, 3) for db in (0, 1)]
    for n, (dz, db) in enumerate(far):
        tz, tb = (zh + dz) % NZ, (zl + db) % 2
        start(x_send.at[tz], x_recv.at[own], s_x.at[4 + n], r_x.at[4 + n], (col * NZ + tz, tb * 2 + core))

    def x_slot(dz, db, side):
        return x_recv.at[slot_of(dz) * NC + ((zl - db + 2) % 2) * 2 + side]

    hot = one_hot_lanes(lanes_ref[2:3, 0:512] + zh * 11, CMID + 128)
    gain_b_all = spread_gain(gain_b, hot)

    hot = one_hot_rows(rows_ref[:, 0:1], 512)
    for k in range(4):
        turned_a[:, k * 512 : (k + 1) * 512] = dot(hot, whole_a[:, k * 512 : (k + 1) * 512]).astype(BF)

    def inverse(z):
        total = jnp.zeros((64, 1), F32)
        for c in range(NC):
            part = x_recv[z * NC + c, :, 96:99].astype(F32)
            total += jnp.sum(part, axis=-1, keepdims=True)
        return lax.rsqrt(total * (1.0 / CMID) + EPS)

    for d in (1, 2, 3):
        arrived(x_recv.at[zh * NC + (ch - d + NC) % NC], s_x.at[d], r_x.at[d])
    inv_b = inverse(zh)
    normed_b = mid_own * inv_b
    factor_b = gelu_slope(normed_b * gain_b_own) * gain_b_own
    scattered(back_recv, s_b, r_b)
    grad_n = two_shares(back_recv) * factor_b
    in_send[...] = to_row(jnp.sum(grad_n * normed_b, axis=-1, keepdims=True))
    for d in (1, 2, 3):
        start(in_send, in_recv.at[ch], s_col.at[3, d], r_col.at[3, d], at_c(d))

    for n, (dz, db) in enumerate(far):
        arrived(x_slot(dz, db, core), s_x.at[4 + n], r_x.at[4 + n])
        start(x_slot(dz, db, core), x_slot(dz, db, core), s_x.at[10 + n], r_x.at[10 + n], twin)
    inner = in_send[...]
    for d in (1, 2, 3):
        at = (ch - d + NC) % NC
        arrived(in_recv.at[at], s_col.at[3, d], r_col.at[3, d])
        inner += in_recv[at]
    inner = jnp.concatenate([to_column(inner * (1.0 / CMID), 64)] * 4, axis=1)
    grad_mid = (inv_b * (grad_n - normed_b * inner)).astype(BF)
    gm_slot[zh] = dot(grad_mid, one_hot_rows(rows_ref[:, 3:4], 384)).astype(BF)
    for d in (1, 2, 3):
        start(gm_slot.at[zh], gm_slot.at[zh], s_col.at[4, d], r_col.at[4, d], at_z(d))

    def last_rows(z, w):
        return pltpu.make_async_remote_copy(
            src_ref=gm_slot.at[3, pl.ds(w * 32 + 16, EDGE), :], dst_ref=gm_prev.at[w], send_sem=s_gm.at[0, z, w],
            recv_sem=s_edge_gm.at[0, w], device_id=beside(1, z), device_id_type=MESH)

    def first_rows(z, w):
        return pltpu.make_async_remote_copy(
            src_ref=gm_slot.at[0, pl.ds(w * 32, EDGE), :], dst_ref=gm_next.at[w], send_sem=s_gm.at[1, z, w],
            recv_sem=s_edge_gm.at[1, w], device_id=beside(-1, z), device_id_type=MESH)

    @pl.when(zh == NZ - 1)
    def _():
        for z in range(NZ):
            for w in range(2):
                last_rows(z, w).start()

    @pl.when(zh == 0)
    def _():
        for z in range(NZ):
            for w in range(2):
                first_rows(z, w).start()

    hot = one_hot_lanes(lanes_ref[3:4, 0:512] + ch * 320, CIN)
    gain_a_own = spread_gain(gain_a, hot)
    feat_bf = feat_ref[...].reshape(128, CIN)
    inv_a = inverse_a(feat_bf.astype(F32))
    feat_own = dot(feat_bf, hot)
    normed_a = feat_own * inv_a
    factor_a = gelu_slope(normed_a * gain_a_own) * gain_a_own

    for n, (dz, db) in enumerate(far):
        arrived(x_slot(dz, db, 1 - core), s_x.at[10 + n], r_x.at[10 + n])
    for z in range(NZ):
        inv = inverse(z)
        values = jnp.concatenate([x_recv[z * NC + c].astype(F32) for c in range(NC)], axis=1)
        b_slot[z] = gelu_tanh(values * inv * gain_b_all).astype(BF)
    edges(b_slot, 32, b_prev, b_next, 2)

    for d in (1, 2, 3):
        arrived(gm_slot.at[slot_of(d)], s_col.at[4, d], r_col.at[4, d])

    for w in range(2):
        arrived(gm_prev.at[w], s_gm.at[0, 0, w], s_edge_gm.at[0, w])
        arrived(gm_next.at[w], s_gm.at[1, 0, w], s_edge_gm.at[1, w])
    lay(gm_slot, 32, gm_prev, gm_next, gm_rows)
    before, here, after = shifted(gm_rows, 128)
    back_conv(before, here, after, turned_a, 128, out_rows)
    to_twin(out_rows, 64, out_over, out_twin, 1)
    edges_done(b_prev, b_next, 2)
    lay(b_slot, 32, b_prev, b_next, b_rows)
    taps = pooled_taps(b_rows, 64)
    total = dot(taps[0], whole_b[:, 0:384])
    for k in range(1, 5):
        total += dot(taps[k], whole_b[:, k * 384 : (k + 1) * 384])
    for w in range(2):
        acc_b[w] = total[w * 64 : (w + 1) * 64]
    for z in range(NZ):
        for w in range(2):
            pool_send[z, w * 16 : (w + 1) * 16, :] = total[w * 64 + z * 16 : w * 64 + (z + 1) * 16].astype(BF)

    from_twin(out_rows, 64, out_twin, out_send, 1)
    scatter(out_send, out_recv, s_o, r_o)

    for d in (1, 2, 3):
        t = (zh + d) % NZ
        start(pool_send.at[t], pool_recv.at[zh], s_col.at[5, d], r_col.at[5, d], at_z(d))

    for d in (1, 2, 3):
        arrived(pool_recv.at[slot_of(d)], s_col.at[5, d], r_col.at[5, d])
    total = jnp.concatenate([acc_b[w, pl.ds(pl.multiple_of(zh * 16, 16), 16), :] for w in range(2)], axis=0)
    for d in (1, 2, 3):
        total += pool_recv[slot_of(d)].astype(F32)
    pooled_ref[...] = (total + bias_b_ref[...].reshape(1, 384)).astype(BF).reshape(2, 16, 384)

    scattered(out_recv, s_o, r_o)
    grad_n = two_shares(out_recv) * factor_a
    ia_send[...] = to_row(jnp.sum(grad_n * normed_a, axis=-1, keepdims=True))
    for d in (1, 2, 3):
        start(ia_send, ia_recv.at[ch], s_col.at[6, d], r_col.at[6, d], at_c(d))
    hot = one_hot_rows(rows_ref[:, 4:5], 384)
    inner = ia_send[...]
    for d in (1, 2, 3):
        at = (ch - d + NC) % NC
        arrived(ia_recv.at[at], s_col.at[6, d], r_col.at[6, d])
        inner += ia_recv[at]
    inner = jnp.concatenate([to_column(inner * (1.0 / CIN), 128)] * 4, axis=1)
    grad = (inv_a * (grad_n - normed_a * inner)).astype(BF)
    grad_ref[...] = dot(grad, hot)[:, 0:320].astype(BF).reshape(2, 64, 320)

    for copy in pending:
        copy.wait_send()
    scatter_sent(back_send, s_b, r_b)
    scatter_sent(out_send, s_o, r_o)

    @pl.when(zh == NZ - 1)
    def _():
        for z in range(NZ):
            for w in range(2):
                last_rows(z, w).wait_send()

    @pl.when(zh == 0)
    def _():
        for z in range(NZ):
            for w in range(2):
                first_rows(z, w).wait_send()


def per_device(dna_features, gain_a, conv_a, bias_a, gain_b, conv_b, bias_b, grad_out):
    lanes, rows = index_tables()
    dma = pltpu.SemaphoreType.DMA
    vmem = pltpu.VMEM
    pooled, grad = pl.pallas_call(
        kernel,
        out_shape=(jax.ShapeDtypeStruct((2, 16, 384), BF), jax.ShapeDtypeStruct((2, 64, 320), BF)),
        in_specs=[pl.BlockSpec(memory_space=pl.ANY)] * 10,
        out_specs=[pl.BlockSpec(memory_space=vmem)] * 2,
        scratch_shapes=[
            vmem((2, 64, CIN), BF), vmem((5, 10, 352), BF), vmem((5, 11, 384), BF), vmem((CIN,), F32), vmem((352,), F32),
            vmem((CMID,), F32), vmem((384,), F32), vmem((2, 16, 384), BF), vmem((8, 1536), jnp.int32), vmem((512, 8), jnp.int32),
            vmem((8, 64, 384), BF), vmem((4, 64, 384), BF), vmem((512, WIDE), BF), vmem((512, WIDE), BF),
            vmem((512, WIDE), BF), vmem((8, 384), F32),
            vmem((4, 128, 384), BF), vmem((2, 16, 384), BF), vmem((2, 16, 384), BF), vmem((2, 3, 288, 128), F32),
            vmem((5, 256, 512), BF), vmem((4, 64, 384), BF),
            vmem((4, 32, 384), BF), vmem((32, 384), BF), vmem((2, 16, 384), BF), vmem((2, 16, 384), BF), vmem((2, 3, 96, 128), F32),
            vmem((2, 4, 128, 128), F32), vmem((8, 64, 128), BF), vmem((8, 64, 128), BF), vmem((8, 64, 128), BF),
            vmem((8, 64, 128), BF), vmem((2, 128, 384), F32), vmem((4, 64, 384), BF), vmem((4, 64, 384), BF),
            vmem((4, 64, 128), BF), vmem((16, 64, 128), BF), vmem((4, 64, 512), BF), vmem((2, 16, 512), BF),
            vmem((2, 16, 512), BF), vmem((2, 4, 160, 128), F32),
            vmem((4, 32, 384), BF), vmem((4, 32, 384), BF), vmem((2, 64, 384), F32),
            vmem((8, 128), F32), vmem((4, 8, 128), F32), vmem((4, 64, 384), BF), vmem((2, 16, 384), BF),
            vmem((2, 16, 384), BF), vmem((2, 3, 160, 128), F32),
            vmem((2, 4, 256, 128), F32), vmem((8, 128, 128), BF), vmem((8, 128, 128), BF), vmem((8, 128, 128), BF),
            vmem((8, 128, 128), BF),
            vmem((8, 128), F32), vmem((4, 8, 128), F32),
            dma((2, 4)), dma((2, 4)), dma((4,)), dma((4,)), dma((2, 4, 2)), dma((2, 4, 2)), dma((2, 2, 2)), dma((2, 2, 2)),
            dma((7, 4)), dma((7, 4)), dma((4, 4)), dma((4, 4)),
            dma((16,)), dma((16,)), dma((16,)), dma((16,)), dma((16,)), dma((16,)), dma((10,)), dma((2, 4, 2)), dma((2, 2)), dma((4,)), dma((4,)),
            dma((2,)), dma((2,)),
        ],
        compiler_params=pltpu.CompilerParams(
            collective_id=0, has_side_effects=True, vmem_limit_bytes=60 * 1024 * 1024
        ),
        cost_estimate=pl.CostEstimate(flops=3_000_000_000, bytes_accessed=8_000_000, transcendentals=800_000),
    )(
        dna_features, conv_a, conv_b, gain_a, bias_a, gain_b, bias_b, grad_out, jnp.asarray(lanes), jnp.asarray(rows),
    )
    return pooled, grad


def solution(mesh):
    return jax.shard_map(
        per_device,
        mesh=mesh,
        in_specs=(
            P(None, "seq", None), P(), P(None, "seq", "ch"), P("ch"), P(), P(None, "seq", "ch"), P("ch"),
            P(None, "seq", "ch"),
        ),
        out_specs=(P(None, "seq", "ch"), P(None, "seq", "ch")),
        check_vma=False,
    )
```
